256 devices in a mesh: dp: 16 (over z, x_lo), fsdp: 16 (over y, x_hi, core).
Axes of the slice: x: 4 (x_hi: 2, x_lo: 2; x = x_hi * 2 + x_lo), y: 4, z: 8, core: 2. Of those that a mesh axis runs over, the one named last changes fastest.
Arguments:
- residual: bfloat16 [73728, 2048], P(('dp', 'fsdp')), may hold values from -6 to 6
- student_mix: bfloat16 [73728, 2048], P(('dp', 'fsdp')), may hold values from -6 to 6
- teacher_mix: bfloat16 [73728, 2048], P(('dp', 'fsdp')), may hold values from -6 to 6
- positions: int32 [512, 144], P(('dp', 'fsdp')), may hold values from 0 to 143
- layer_scale: float32 [2048], replicated, may hold values from 0.3 to 3
- student_weight: float32 [2048, 2048], P('fsdp'), may hold values from -6 to 6
- teacher_weight: float32 [2048, 2048], P('fsdp'), may hold values from -6 to 6
- moment: float32 [2048, 2048], P('fsdp'), may hold values from -0.00036621094 to 0.00036621094
- second: float32 [2048, 2048], P('fsdp'), may hold values from 1.9868216e-09 to 1.9868216e-08
Outputs:
- student_new: float32 [2048, 2048], P('fsdp')
- teacher_new: float32 [2048, 2048], P('fsdp')
- moment_new: float32 [2048, 2048], P('fsdp')
- second_new: float32 [2048, 2048], P('fsdp')
- student_tokens: bfloat16 [73728, 2048], P(('dp', 'fsdp'))
The draws below stay inside these ranges and needn't reach their ends.
All inputs are finite; a program needn't handle non-finite values.
Results may differ from the reference program's by a relative error of at most 0.01.
Values may be sent and summed in bfloat16 or wider, within the bound.
No kernel may reach another device: no remote copies, remote signals or barrier semaphores. Data moves between devices by JAX's collectives and lax.ppermute only.
A program may use at most 128 MiB of HBM per device.

```python
import math
import jax
import jax.numpy as jnp
from jax import lax

KIN = 2048
DOUT = 2048
CROPS = 2
PATCHES = 144
TOK_DEV = 288
TOKENS = 73728
ALL_CROPS = 512
N_DP = 16
N_FSDP = 16


def place_ends(array, stream_key, low, largest):
    dims = array.shape
    spot = [jax.random.randint(jax.random.fold_in(stream_key, axis), (), 0, dims[axis]) for axis in range(len(dims))]
    array = array.at[tuple(spot)].set(low)
    longest = dims.index(max(dims))
    spot[longest] = (spot[longest] + 1) % dims[longest]
    return array.at[tuple(spot)].set(largest)


def block_levels(stream_key, dims, cuts, smallest, top_value):
    def one(axis_at, shards_of):
        draws = jax.random.uniform(jax.random.fold_in(jax.random.fold_in(stream_key, 6), axis_at), (shards_of,), jnp.float32, smallest / len(cuts), top_value / len(cuts))
        return jnp.repeat(jnp.exp(draws), dims[axis_at] // shards_of).reshape((-1,) + (1,) * (len(dims) - axis_at - 1))

    loudness = one(*cuts[0])
    for cut in cuts[1:]:
        loudness = loudness * one(*cut)
    return loudness


def bell_draw(key, dims, width, bound, split=(), dtype=jnp.bfloat16):
    result = width * jax.random.normal(key, dims, jnp.float32)
    if split:
        result = result * block_levels(key, dims, split, -0.22, 0.18)
    return jnp.clip(result, -bound, bound).astype(dtype)


def setup_inputs(seed: int = 0) -> dict:
    arg_keys = jax.random.split(jax.random.key(seed), 10)
    return {
        "residual": bell_draw(arg_keys[0], (TOKENS, DOUT), 1.0, 6.0, ((0, 256),)),
        "student_mix": bell_draw(arg_keys[1], (TOKENS, KIN), 1.0, 6.0, ((0, 256),)),
        "teacher_mix": bell_draw(arg_keys[2], (TOKENS, KIN), 1.0, 6.0, ((0, 256),)),
        "positions": place_ends(jax.random.randint(arg_keys[3], (ALL_CROPS, PATCHES), 0, PATCHES), jax.random.fold_in(arg_keys[3], 1), 0, PATCHES - 1).astype(jnp.int32),
        "layer_scale": jnp.clip(jnp.exp(jax.random.uniform(arg_keys[4], (DOUT,), jnp.float32, math.log(0.3), math.log(3.0))), 0.3, 3.0),
        "student_weight": bell_draw(arg_keys[5], (KIN, DOUT), 1.0, 6.0, ((0, 16),), jnp.float32),
        "teacher_weight": bell_draw(arg_keys[6], (KIN, DOUT), 1.0, 6.0, ((0, 16),), jnp.float32),
        "moment": bell_draw(arg_keys[7], (KIN, DOUT), (0.3 * (TOKENS * KIN) ** -0.5), 0.00036621094, ((0, 16),), jnp.float32),
        "second": jnp.clip(jnp.exp(math.log(1.9868215517249155e-08) - 2.3025851 * jax.random.uniform(arg_keys[8], (KIN, DOUT), jnp.float32) ** block_levels(arg_keys[8], (KIN, DOUT), ((0, 16),), -0.2, 0.2)), 1.9868215961338365e-09, 1.9868215517249155e-08),
    }


def normalize(values):
    inverse_rms = lax.rsqrt(lax.optimization_barrier(jnp.mean(values * values, axis=-1, keepdims=True)) + 1e-06)
    return (values * inverse_rms, inverse_rms)

def reference(residual, student_mix, teacher_mix, positions, layer_scale, student_weight, teacher_weight, moment, second):
    inverse_root = KIN ** (-0.5)
    count = N_DP * N_FSDP
    student_copy = student_weight.astype(jnp.bfloat16)
    teacher_copy = teacher_weight.astype(jnp.bfloat16)
    stacked = (residual.reshape(count, TOK_DEV, DOUT), student_mix.reshape(count, TOK_DEV, KIN), teacher_mix.reshape(count, TOK_DEV, KIN), positions.reshape(count, CROPS, PATCHES))

    def device_rows(running, pieces):
        rows_res, mix_student, mix_teacher, place_ids = pieces
        base = rows_res.astype(jnp.float32)
        student_out = base + layer_scale * (jnp.dot(mix_student, student_copy, preferred_element_type=jnp.float32) * inverse_root)
        teacher_out = base + layer_scale * (jnp.dot(mix_teacher, teacher_copy, preferred_element_type=jnp.float32) * inverse_root)
        student_norm, inverse_rms = normalize(student_out)
        teacher_norm, unused = normalize(teacher_out)
        matched = jnp.take_along_axis(teacher_norm.reshape(CROPS, PATCHES, DOUT), place_ids[:, :, None], axis=1)
        matched = matched.reshape(TOK_DEV, DOUT)
        mismatch = (student_norm - matched) / TOKENS
        out_grad = inverse_rms * (mismatch - student_norm * lax.optimization_barrier(jnp.mean(mismatch * student_norm, axis=-1, keepdims=True)))
        mix_grad = (layer_scale * out_grad * inverse_root).astype(jnp.bfloat16)
        partial_grad = lax.dot_general(mix_student, mix_grad, (((0,), (0,)), ((), ())), preferred_element_type=jnp.float32)
        partial_grad = lax.optimization_barrier(partial_grad.astype(jnp.bfloat16)).astype(jnp.float32)
        return (running + partial_grad, student_norm.astype(jnp.bfloat16))
    grad, token_rows = lax.scan(device_rows, jnp.zeros((KIN, DOUT), jnp.float32), stacked)
    moment_new = 0.9 * moment + 0.1 * grad
    second_new = 0.95 * second + 0.05 * grad * grad
    student_new = student_weight - 0.1 * (moment_new / (jnp.sqrt(second_new) + 1e-08) + 0.04 * student_weight)
    teacher_new = 0.96 * teacher_weight + 0.04 * student_new
    return (student_new, teacher_new, moment_new, second_new, token_rows.reshape(TOKENS, DOUT))
```

```python
import functools

import jax
import jax.numpy as jnp
from jax import lax
from jax.experimental import pallas as pl
from jax.experimental.pallas import tpu as pltpu
from jax.sharding import Mesh, PartitionSpec as P

KIN = 2048
DOUT = 2048
PATCHES = 144
EPS = 1e-06
AXES = ("z", "xlo", "y", "xhi", "core")
VMEM_LIMIT = 44 * 1024 * 1024

X_INDEX = (0, 2, 1, 3)
CORE_SWAP = ((0, 1), (1, 0))
X_NEAR = tuple((X_INDEX[a], X_INDEX[b]) for a, b in ((1, 2), (2, 1), (0, 3), (3, 0)))


def from_next(size):
    return tuple(((i + 1) % size, i) for i in range(size))


def from_previous(size):
    return tuple((i, (i + 1) % size) for i in range(size))


def swap_cores(value):
    return lax.ppermute(value, "core", CORE_SWAP)


def from_y_next(value):
    return lax.ppermute(value, "y", from_next(4))


def from_y_previous(value):
    return lax.ppermute(value, "y", from_previous(4))


def from_x_near(value):
    return lax.ppermute(value, ("xlo", "xhi"), X_NEAR)


def from_z_next(value):
    return lax.ppermute(value, "z", from_next(8))


def from_z_previous(value):
    return lax.ppermute(value, "z", from_previous(8))


def from_x_twin(value):
    return lax.ppermute(value, "xlo", CORE_SWAP)


def gather_rows(own, other):
    first = {(0, 0): own}
    first[1, 0] = from_y_next(own)
    first[3, 0] = from_y_previous(own)
    first[0, 1] = from_x_near(own)
    first[2, 0] = from_y_next(first[1, 0])
    first[3, 1] = from_y_previous(first[0, 1])
    first[1, 1] = from_x_near(first[1, 0])
    last_student = from_y_next(first[1, 1][0])
    last_teacher = from_y_previous(first[3, 1][1])

    second = {(0, 0): other}
    second[1, 0] = from_z_next(first[1, 0])
    second[3, 0] = from_z_previous(first[3, 0])
    second[0, 1] = from_x_twin(first[0, 1])
    second[2, 0] = from_z_next(first[2, 0])
    second[3, 1] = from_x_twin(first[3, 1])
    second[1, 1] = from_z_previous(first[1, 1])
    other_student = from_z_next(last_student)
    other_teacher = from_z_previous(last_teacher)

    pieces = []
    for group, student, teacher in ((first, last_student, last_teacher), (second, other_student, other_teacher)):
        for dy in range(4):
            for dx in range(2):
                if (dy, dx) == (2, 1):
                    pieces.append((student, teacher))
                else:
                    pieces.append(group[dy, dx])
    return pieces


def forward_kernel(layout, order, student_mix, teacher_mix, residual, scale, positions, *refs):
    count = sum(2 if split else 1 for split in layout)
    weights, (student_out, matched_out, sums_out, held) = refs[:count], refs[count:]
    at = 0
    for block, split in enumerate(layout):
        rows = pl.ds(pl.multiple_of(order[block] * 128, 128), 128)
        if split:
            held[0, rows, :] = weights[at][...]
            held[1, rows, :] = weights[at + 1][...]
            at += 2
        else:
            held[0, rows, :] = weights[at][0]
            held[1, rows, :] = weights[at][1]
            at += 1
    inverse_root = KIN ** (-0.5)
    base = residual[...].astype(jnp.float32)
    factor = scale[...]
    student = base + factor * (
        jnp.dot(student_mix[...], held[0], preferred_element_type=jnp.float32) * inverse_root
    )
    teacher = base + factor * (
        jnp.dot(teacher_mix[...], held[1], preferred_element_type=jnp.float32) * inverse_root
    )
    high = teacher.astype(jnp.bfloat16)
    low = (teacher - high.astype(jnp.float32)).astype(jnp.bfloat16)
    lane = lax.broadcasted_iota(jnp.int32, (PATCHES, PATCHES), 1)
    parts = []
    for crop in range(student.shape[0] // PATCHES):
        rows = slice(crop * PATCHES, (crop + 1) * PATCHES)
        pick = (positions[rows, :] == lane).astype(jnp.float32).astype(jnp.bfloat16)
        parts.append(
            jnp.dot(pick, high[rows], preferred_element_type=jnp.float32)
            + jnp.dot(pick, low[rows], preferred_element_type=jnp.float32)
        )
    matched = jnp.concatenate(parts, axis=0)
    student_out[...] = student
    matched_out[...] = matched
    spot = lax.broadcasted_iota(jnp.int32, sums_out.shape, 1)
    sums = jnp.where(
        spot == 0,
        jnp.sum(student * student, axis=-1, keepdims=True),
        jnp.where(
            spot == 1,
            jnp.sum(matched * matched, axis=-1, keepdims=True),
            jnp.where(spot == 2, jnp.sum(student * matched, axis=-1, keepdims=True), 0.0),
        ),
    )

    @pl.when(pl.program_id(0) == 0)
    def _():
        sums_out[...] = sums

    @pl.when(pl.program_id(0) != 0)
    def _():
        sums_out[...] += sums


def forward(order, pieces, student_mix, teacher_mix, residual, scale, positions):
    rows, columns, width = student_mix.shape[0], scale.shape[1], 256
    layout, weights, weight_specs = [], [], []
    for piece in pieces:
        if isinstance(piece, tuple):
            layout.append(True)
            weights.extend(piece)
            weight_specs.extend([pl.BlockSpec((128, width), lambda j, order: (0, j))] * 2)
        else:
            layout.append(False)
            weights.append(piece)
            weight_specs.append(pl.BlockSpec((2, 128, width), lambda j, order: (0, 0, j)))
    whole = pl.BlockSpec((rows, KIN), lambda j, order: (0, 0))
    column = pl.BlockSpec((rows, width), lambda j, order: (0, j))
    return pl.pallas_call(
        functools.partial(forward_kernel, tuple(layout)),
        grid_spec=pltpu.PrefetchScalarGridSpec(
            num_scalar_prefetch=1,
            grid=(columns // width,),
            in_specs=[
                whole,
                whole,
                column,
                pl.BlockSpec((1, width), lambda j, order: (0, j)),
                pl.BlockSpec((rows, 1), lambda j, order: (0, 0)),
            ]
            + weight_specs,
            out_specs=[column, column, pl.BlockSpec((rows, 128), lambda j, order: (0, 0))],
            scratch_shapes=[pltpu.VMEM((2, KIN, width), jnp.bfloat16)],
        ),
        out_shape=[
            jax.ShapeDtypeStruct((rows, columns), jnp.float32),
            jax.ShapeDtypeStruct((rows, columns), jnp.float32),
            jax.ShapeDtypeStruct((rows, 128), jnp.float32),
        ],
        compiler_params=pltpu.CompilerParams(vmem_limit_bytes=VMEM_LIMIT),
        cost_estimate=pl.CostEstimate(
            flops=4 * rows * KIN * columns, bytes_accessed=20 * 1024 * 1024, transcendentals=0
        ),
    )(order, student_mix, teacher_mix, residual, scale, positions, *weights)


def backward_kernel(total_tokens, student, matched, sums, more_sums, scale, mix, grad_out, tokens_out, held):
    @pl.when(pl.program_id(0) == 0)
    def _():
        own = more_sums.shape[0] // 2
        swapped = jnp.concatenate([more_sums[own:, :], more_sums[:own, :]], axis=0)
        total = (sums[...] + swapped) * (1.0 / DOUT)
        inverse_rms = lax.rsqrt(total[:, 0:1] + EPS)
        inverse_matched = lax.rsqrt(total[:, 1:2] + EPS)
        overlap = inverse_rms * inverse_matched * total[:, 2:3]
        shared = inverse_rms * (1.0 / total_tokens)
        student_part = shared * inverse_rms * (EPS * inverse_rms * inverse_rms + overlap)
        matched_part = shared * inverse_matched
        values = student[...]
        tokens_out[...] = (values * inverse_rms).astype(jnp.bfloat16)
        factor = scale[...] * (KIN ** (-0.5))
        held[...] = (factor * (values * student_part - matched[...] * matched_part)).astype(jnp.bfloat16)

    grad_out[...] = jnp.dot(mix[...], held[...], preferred_element_type=jnp.float32).astype(jnp.bfloat16)


def backward(total_tokens, student, matched, sums, more_sums, scale, mix):
    rows, columns = student.shape
    depth = 256
    whole = pl.BlockSpec((rows, columns), lambda i: (0, 0))
    narrow = pl.BlockSpec((rows, 128), lambda i: (0, 0))
    return pl.pallas_call(
        functools.partial(backward_kernel, total_tokens),
        grid=(KIN // depth,),
        in_specs=[
            whole,
            whole,
            narrow,
            narrow,
            pl.BlockSpec((1, columns), lambda i: (0, 0)),
            pl.BlockSpec((depth, rows), lambda i: (i, 0)),
        ],
        out_specs=[pl.BlockSpec((depth, columns), lambda i: (i, 0)), whole],
        out_shape=[
            jax.ShapeDtypeStruct((KIN, columns), jnp.bfloat16),
            jax.ShapeDtypeStruct((rows, columns), jnp.bfloat16),
        ],
        scratch_shapes=[pltpu.VMEM((rows, columns), jnp.bfloat16)],
        compiler_params=pltpu.CompilerParams(vmem_limit_bytes=VMEM_LIMIT),
        cost_estimate=pl.CostEstimate(
            flops=2 * rows * KIN * columns, bytes_accessed=12 * 1024 * 1024, transcendentals=0
        ),
    )(student, matched, sums, more_sums, scale, mix)


def adamw_update(grad, weight, teacher, first, squares):
    first_next = 0.9 * first + 0.1 * grad
    squares_next = 0.95 * squares + 0.05 * grad * grad
    weight_next = weight - 0.1 * (first_next / (jnp.sqrt(squares_next) + 1e-08) + 0.04 * weight)
    teacher_next = 0.96 * teacher + 0.04 * weight_next
    return (weight_next, teacher_next, first_next, squares_next)


def join_columns(core, own, other):
    return jnp.where(
        core == 0, jnp.concatenate([own, other], axis=-1), jnp.concatenate([other, own], axis=-1)
    )


def shards(
    residual,
    student_mix,
    teacher_mix,
    positions,
    layer_scale,
    student_weight,
    teacher_weight,
    moment,
    second,
):
    half = DOUT // 2
    token_count = student_mix.shape[0]
    total_tokens = token_count * 256
    z, xlo, y, xhi, core = (lax.axis_index(name) for name in AXES)
    parity = (z + (xhi ^ xlo)) & 1

    def columns_of(value, which):
        return lax.dynamic_slice_in_dim(value, which * half, half, axis=-1)

    copies = jnp.stack([student_weight, teacher_weight]).astype(jnp.bfloat16)
    mine = columns_of(copies, core)
    theirs = swap_cores(columns_of(copies, 1 - core))
    fetched = jnp.where(core == parity, mine, theirs)
    passed = jnp.where(core == parity, theirs, mine)
    pieces = gather_rows(fetched, passed)
    order = jnp.stack(
        [
            (((y + dy) & 3) * 2 + (xhi ^ dx)) * 2 + (parity ^ side)
            for side in range(2)
            for dy in range(4)
            for dx in range(2)
        ]
    ).astype(jnp.int32)

    student_rows = jnp.concatenate([student_mix, swap_cores(student_mix)], axis=0)
    teacher_rows = jnp.concatenate([teacher_mix, swap_cores(teacher_mix)], axis=0)
    residual_rows = jnp.concatenate(
        [columns_of(residual, core), swap_cores(columns_of(residual, 1 - core))], axis=0
    )
    places = jnp.concatenate([positions, swap_cores(positions)], axis=0).reshape(2 * token_count, 1)
    scale = columns_of(layer_scale, core).reshape(1, half)

    student_out, matched, sums = forward(
        order, pieces, student_rows, teacher_rows, residual_rows, scale, places
    )
    grads, tokens = backward(
        total_tokens, student_out, matched, sums, swap_cores(sums), scale, student_rows.T
    )

    student_tokens = join_columns(core, tokens[:token_count], swap_cores(tokens[token_count:]))

    by_chip = lax.all_to_all(grads.reshape(8, 256, half), ("y", "xhi"), 0, 0)
    chip_rows = jnp.sum(by_chip.astype(jnp.float32), axis=0).astype(jnp.bfloat16)
    by_copy = lax.all_to_all(chip_rows.reshape(16, 16, half), ("z", "xlo"), 0, 0)
    copy_rows = jnp.sum(by_copy.astype(jnp.float32), axis=0).astype(jnp.bfloat16)
    full = lax.all_to_all(
        jnp.broadcast_to(copy_rows[None], (16, 16, half)), ("z", "xlo"), 0, 0
    ).reshape(256, half)
    own_rows = lax.dynamic_slice_in_dim(full, core * 128, 128, axis=0)
    other_rows = lax.dynamic_slice_in_dim(full, (1 - core) * 128, 128, axis=0)
    grad = join_columns(core, own_rows, swap_cores(other_rows)).astype(jnp.float32)
    weight_next, teacher_next, first_next, squares_next = adamw_update(
        grad, student_weight, teacher_weight, moment, second
    )
    return (weight_next, teacher_next, first_next, squares_next, student_tokens)


def solution(mesh):
    split = Mesh(mesh.devices.reshape(8, 2, 4, 2, 2), AXES)
    tokens = P(AXES, None)
    owned = P(("y", "xhi", "core"), None)
    return jax.shard_map(
        shards,
        mesh=split,
        in_specs=(tokens, tokens, tokens, tokens, P(), owned, owned, owned, owned),
        out_specs=(owned, owned, owned, owned, tokens),
        check_vma=False,
    )
```

```python
import functools

import jax
import jax.numpy as jnp
from jax import lax
from jax.experimental import pallas as pl
from jax.experimental.pallas import tpu as pltpu
from jax.sharding import Mesh, PartitionSpec as P

KIN = 2048
DOUT = 2048
PATCHES = 144
EPS = 1e-06
AXES = ("z", "xlo", "y", "xhi", "core")
VMEM_LIMIT = 44 * 1024 * 1024

X_INDEX = (0, 2, 1, 3)
CORE_SWAP = ((0, 1), (1, 0))
X_NEAR = tuple((X_INDEX[a], X_INDEX[b]) for a, b in ((1, 2), (2, 1), (0, 3), (3, 0)))


def from_next(size):
    return tuple(((i + 1) % size, i) for i in range(size))


def from_previous(size):
    return tuple((i, (i + 1) % size) for i in range(size))


def with_core_flip(pairs):
    return tuple((2 * a + 1 - core, 2 * b + core) for a, b in pairs for core in range(2))


FSDP_GROUPS = tuple(
    tuple((xhi ^ side) * 8 + y * 2 + xhi for y in range(4) for xhi in range(2)) for side in range(2)
)
DP_GROUPS = tuple(
    tuple((z * 2 + xlo) * 2 + (side ^ ((z + xlo) & 1)) for z in range(8) for xlo in range(2)) for side in range(2)
)


def swap_cores(value):
    return lax.ppermute(value, "core", CORE_SWAP)


def from_y_next(value):
    return lax.ppermute(value, "y", from_next(4))


def from_y_previous(value):
    return lax.ppermute(value, "y", from_previous(4))


def from_x_near(value):
    return lax.ppermute(value, ("xlo", "xhi"), X_NEAR)


def from_z_next(value):
    return lax.ppermute(value, ("z", "core"), with_core_flip(from_next(8)))


def from_z_previous(value):
    return lax.ppermute(value, ("z", "core"), with_core_flip(from_previous(8)))


def from_x_twin(value):
    return lax.ppermute(value, ("xlo", "core"), with_core_flip(CORE_SWAP))


def fsdp_exchange(value):
    return lax.all_to_all(value, ("xlo", "y", "xhi"), 0, 0, axis_index_groups=FSDP_GROUPS)


def dp_exchange(value):
    return lax.all_to_all(value, ("z", "xlo", "core"), 0, 0, axis_index_groups=DP_GROUPS)


EARLY = (
    (0, 0, 0), (1, 0, 0), (0, 1, 0), (0, 3, 0), (0, 0, 1), (0, 2, 0), (0, 3, 1), (0, 1, 1), (1, 1, 0), (1, 3, 0),
    (1, 0, 1),
)
LATE = ((0, 2, 1), (1, 2, 0), (1, 3, 1), (1, 1, 1), (1, 2, 1))


def gather_rows(own, other):
    up, down, across = lax.optimization_barrier((from_y_next(own), from_y_previous(own), from_x_near(own)))
    up_two = from_y_next(up)
    across_up = from_x_near(up)
    across_down = from_y_previous(across)
    passed_up, passed_down, passed_across = from_z_next(up), from_z_previous(down), from_x_twin(across)
    up_two, across_up, across_down = lax.optimization_barrier((up_two, across_up, across_down))
    student = from_y_next(across_up[0])
    teacher = from_y_previous(across_down[1])
    passed_two = from_z_next(up_two)
    passed_across_up = from_z_previous(across_up)
    passed_across_down = from_x_twin(across_down)
    student, teacher = lax.optimization_barrier((student, teacher))
    passed_student = from_z_next(student)
    passed_teacher = from_z_previous(teacher)
    early = (
        own, other, up, down, across, up_two, across_down, across_up, passed_up, passed_down, passed_across,
    )
    late = (
        student, teacher, passed_two, passed_across_down, passed_across_up, passed_student, passed_teacher,
    )
    return early, late


def early_kernel(order, student_own, student_other, teacher_own, teacher_other, *refs):
    count = len(EARLY)
    weights = refs[:count]
    student_out, teacher_out, student_late, teacher_late, turned, mix, held = refs[count:]
    step, own = pl.program_id(0), student_own.shape[0]

    @pl.when(step == 0)
    def _():
        for block in range(count + len(LATE)):
            columns = pl.ds(pl.multiple_of(order[block] * 128, 128), 128)
            at = block if block < count else block - count
            spot = slice(at * 128, (at + 1) * 128)
            to_student = mix.at[0] if block < count else student_late
            to_teacher = mix.at[1] if block < count else teacher_late
            to_student[:own, spot] = student_own[:, columns]
            to_student[own:, spot] = student_other[:, columns]
            to_teacher[:own, spot] = teacher_own[:, columns]
            to_teacher[own:, spot] = teacher_other[:, columns]

    for block in range(count):
        rows = slice(block * 128, (block + 1) * 128)
        held[0, rows, :] = weights[block][0]
        held[1, rows, :] = weights[block][1]
    student_out[...] = jnp.dot(mix[0], held[0], preferred_element_type=jnp.float32)
    teacher_out[...] = jnp.dot(mix[1], held[1], preferred_element_type=jnp.float32)
    width = turned.shape[0]
    columns = pl.ds(pl.multiple_of(step * width, width), width)
    turned[...] = jnp.concatenate([student_own[:, columns], student_other[:, columns]], axis=0).T


def early_forward(order, weights, student_own, student_other, teacher_own, teacher_other):
    own, columns, width = student_own.shape[0], weights[0].shape[-1], 256
    rows, steps, count = 2 * own, columns // width, len(EARLY)
    whole = pl.BlockSpec((own, KIN), lambda j, order: (0, 0))
    column = pl.BlockSpec((rows, width), lambda j, order: (0, j))
    late = pl.BlockSpec((rows, len(LATE) * 128), lambda j, order: (0, 0))
    return pl.pallas_call(
        early_kernel,
        grid_spec=pltpu.PrefetchScalarGridSpec(
            num_scalar_prefetch=1,
            grid=(steps,),
            in_specs=[whole] * 4 + [pl.BlockSpec((2, 128, width), lambda j, order: (0, 0, j))] * count,
            out_specs=[column, column, late, late, pl.BlockSpec((KIN // steps, rows), lambda j, order: (j, 0))],
            scratch_shapes=[
                pltpu.VMEM((2, rows, count * 128), jnp.bfloat16),
                pltpu.VMEM((2, count * 128, width), jnp.bfloat16),
            ],
        ),
        out_shape=[
            jax.ShapeDtypeStruct((rows, columns), jnp.float32),
            jax.ShapeDtypeStruct((rows, columns), jnp.float32),
            jax.ShapeDtypeStruct((rows, len(LATE) * 128), jnp.bfloat16),
            jax.ShapeDtypeStruct((rows, len(LATE) * 128), jnp.bfloat16),
            jax.ShapeDtypeStruct((KIN, rows), jnp.bfloat16),
        ],
        compiler_params=pltpu.CompilerParams(vmem_limit_bytes=VMEM_LIMIT),
        cost_estimate=pl.CostEstimate(
            flops=4 * rows * count * 128 * columns, bytes_accessed=18 * 1024 * 1024, transcendentals=0
        ),
    )(order, student_own, student_other, teacher_own, teacher_other, *weights)


def late_kernel(
    order, student_mix, teacher_mix, student_part, teacher_part, residual_own, residual_other, scale, places_own,
    places_other, *refs
):
    weights = refs[:7]
    student_out, matched_out, sums_out, held = refs[7:]
    depth = held.shape[1]
    held[0, :128, :] = weights[0][...]
    held[1, :128, :] = weights[1][...]
    for block in range(1, 4):
        rows = slice(block * 128, (block + 1) * 128)
        held[0, rows, :] = weights[block + 1][0]
        held[1, rows, :] = weights[block + 1][1]
    held[0, depth - 128 :, :] = weights[5][...]
    held[1, depth - 128 :, :] = weights[6][...]
    factor = scale[...] * (KIN ** (-0.5))
    student_sum = student_part[...] + jnp.dot(student_mix[...], held[0], preferred_element_type=jnp.float32)
    teacher_sum = teacher_part[...] + jnp.dot(teacher_mix[...], held[1], preferred_element_type=jnp.float32)
    own = residual_own.shape[0]
    lane = lax.broadcasted_iota(jnp.int32, (PATCHES, PATCHES), 1)
    students, parts = [], []
    for side, (residual, places) in enumerate(((residual_own, places_own), (residual_other, places_other))):
        tokens = slice(side * own, (side + 1) * own)
        base = residual[...].astype(jnp.float32)
        students.append(base + factor * student_sum[tokens])
        teacher = base + factor * teacher_sum[tokens]
        high = teacher.astype(jnp.bfloat16)
        low = (teacher - high.astype(jnp.float32)).astype(jnp.bfloat16)
        for crop in range(own // PATCHES):
            rows = slice(crop * PATCHES, (crop + 1) * PATCHES)
            pick = (places[rows, :] == lane).astype(jnp.float32).astype(jnp.bfloat16)
            parts.append(
                jnp.dot(pick, high[rows], preferred_element_type=jnp.float32)
                + jnp.dot(pick, low[rows], preferred_element_type=jnp.float32)
            )
    student = jnp.concatenate(students, axis=0)
    matched = jnp.concatenate(parts, axis=0)
    student_out[...] = student
    matched_out[...] = matched
    spot = lax.broadcasted_iota(jnp.int32, sums_out.shape, 1)
    sums = jnp.where(
        spot == 0,
        jnp.sum(student * student, axis=-1, keepdims=True),
        jnp.where(
            spot == 1,
            jnp.sum(matched * matched, axis=-1, keepdims=True),
            jnp.where(spot == 2, jnp.sum(student * matched, axis=-1, keepdims=True), 0.0),
        ),
    )

    @pl.when(pl.program_id(0) == 0)
    def _():
        sums_out[...] = sums

    @pl.when(pl.program_id(0) != 0)
    def _():
        sums_out[...] += sums


def late_forward(
    order, weights, student_mix, teacher_mix, student_part, teacher_part, residual_own, residual_other, scale,
    places_own, places_other
):
    (rows, columns), own, width, depth = student_part.shape, residual_own.shape[0], 256, student_mix.shape[1]
    steps = columns // width
    half_at = len(EARLY) + len(LATE)
    mix = pl.BlockSpec((rows, depth), lambda j, order: (0, 0))
    column = pl.BlockSpec((rows, width), lambda j, order: (0, j))
    places = pl.BlockSpec((own, 1), lambda j, order: (0, 0))
    pair = pl.BlockSpec((2, 128, width), lambda j, order: (0, 0, j))
    single = pl.BlockSpec((128, width), lambda j, order: (0, j))
    return pl.pallas_call(
        late_kernel,
        grid_spec=pltpu.PrefetchScalarGridSpec(
            num_scalar_prefetch=1,
            grid=(steps,),
            in_specs=[
                mix,
                mix,
                column,
                column,
                pl.BlockSpec((own, width), lambda j, order: (0, order[half_at] * steps + j)),
                pl.BlockSpec((own, width), lambda j, order: (0, j)),
                pl.BlockSpec((1, width), lambda j, order: (0, order[half_at] * steps + j)),
                places,
                places,
                single,
                single,
                pair,
                pair,
                pair,
                single,
                single,
            ],
            out_specs=[column, column, pl.BlockSpec((rows, 128), lambda j, order: (0, 0))],
            scratch_shapes=[pltpu.VMEM((2, depth, width), jnp.bfloat16)],
        ),
        out_shape=[
            jax.ShapeDtypeStruct((rows, columns), jnp.float32),
            jax.ShapeDtypeStruct((rows, columns), jnp.float32),
            jax.ShapeDtypeStruct((rows, 128), jnp.float32),
        ],
        compiler_params=pltpu.CompilerParams(vmem_limit_bytes=VMEM_LIMIT),
        cost_estimate=pl.CostEstimate(
            flops=4 * rows * depth * columns, bytes_accessed=16 * 1024 * 1024, transcendentals=0
        ),
    )(
        order, student_mix, teacher_mix, student_part, teacher_part, residual_own, residual_other, scale, places_own,
        places_other, *weights
    )


def backward_kernel(total_tokens, order, student, matched, sums, more_sums, scale, mix, grad_out, tokens_out, held):
    @pl.when(pl.program_id(0) == 0)
    def _():
        own = more_sums.shape[0] // 2
        swapped = jnp.concatenate([more_sums[own:, :], more_sums[:own, :]], axis=0)
        total = (sums[...] + swapped) * (1.0 / DOUT)
        inverse_rms = lax.rsqrt(total[:, 0:1] + EPS)
        inverse_matched = lax.rsqrt(total[:, 1:2] + EPS)
        overlap = inverse_rms * inverse_matched * total[:, 2:3]
        shared = inverse_rms * (1.0 / total_tokens)
        student_part = shared * inverse_rms * (EPS * inverse_rms * inverse_rms + overlap)
        matched_part = shared * inverse_matched
        values = student[...]
        tokens_out[...] = (values * inverse_rms).astype(jnp.bfloat16)
        factor = scale[...] * (KIN ** (-0.5))
        held[...] = (factor * (values * student_part - matched[...] * matched_part)).astype(jnp.bfloat16)

    width = grad_out.shape[-1]
    for part in range(grad_out.shape[1]):
        grad_out[0, part] = jnp.dot(
            mix[...], held[:, part * width : (part + 1) * width], preferred_element_type=jnp.float32
        ).astype(jnp.bfloat16)


def backward(total_tokens, order, student, matched, sums, more_sums, scale, mix):
    rows, columns = student.shape
    depth = 256
    half_at = len(EARLY) + len(LATE)
    whole = pl.BlockSpec((rows, columns), lambda i, order: (0, 0))
    narrow = pl.BlockSpec((rows, 128), lambda i, order: (0, 0))
    return pl.pallas_call(
        functools.partial(backward_kernel, total_tokens),
        grid_spec=pltpu.PrefetchScalarGridSpec(
            num_scalar_prefetch=1,
            grid=(KIN // depth,),
            in_specs=[
                whole,
                whole,
                narrow,
                narrow,
                pl.BlockSpec((1, columns), lambda i, order: (0, order[half_at])),
                pl.BlockSpec((depth, rows), lambda i, order: (i, 0)),
            ],
            out_specs=[pl.BlockSpec((1, 2, depth, columns // 2), lambda i, order: (i, 0, 0, 0)), whole],
            scratch_shapes=[pltpu.VMEM((rows, columns), jnp.bfloat16)],
        ),
        out_shape=[
            jax.ShapeDtypeStruct((KIN // depth, 2, depth, columns // 2), jnp.bfloat16),
            jax.ShapeDtypeStruct((rows, columns), jnp.bfloat16),
        ],
        compiler_params=pltpu.CompilerParams(vmem_limit_bytes=VMEM_LIMIT),
        cost_estimate=pl.CostEstimate(
            flops=2 * rows * KIN * columns, bytes_accessed=12 * 1024 * 1024, transcendentals=0
        ),
    )(order, student, matched, sums, more_sums, scale, mix)


def adamw_update(grad, weight, teacher, first, squares):
    first_next = 0.9 * first + 0.1 * grad
    squares_next = 0.95 * squares + 0.05 * grad * grad
    weight_next = weight - 0.1 * (first_next / (jnp.sqrt(squares_next) + 1e-08) + 0.04 * weight)
    teacher_next = 0.96 * teacher + 0.04 * weight_next
    return (weight_next, teacher_next, first_next, squares_next)


def join_columns(which, own, other):
    return jnp.where(
        which == 0, jnp.concatenate([own, other], axis=-1), jnp.concatenate([other, own], axis=-1)
    )


def shards(
    residual,
    student_mix,
    teacher_mix,
    positions,
    layer_scale,
    student_weight,
    teacher_weight,
    moment,
    second,
):
    half = DOUT // 2
    token_count = student_mix.shape[0]
    total_tokens = token_count * 256
    z, xlo, y, xhi, core = (lax.axis_index(name) for name in AXES)
    which = (core + z + xhi + xlo) & 1

    def columns_of(value, index):
        return lax.dynamic_slice_in_dim(value, index * half, half, axis=-1)

    def both_weights(index):
        return jnp.stack([columns_of(student_weight, index), columns_of(teacher_weight, index)]).astype(jnp.bfloat16)

    own = both_weights(which)
    order = jnp.stack(
        [
            (((y + dy) & 3) * 2 + (xhi ^ dx)) * 2 + (core ^ side)
            for side, dy, dx in EARLY + LATE
        ]
        + [which]
    ).astype(jnp.int32)
    own, student_sent, teacher_sent, residual_sent, positions_sent, student_held, teacher_held = (
        lax.optimization_barrier(
            (own, student_mix, teacher_mix, residual, positions, student_weight, teacher_weight)
        )
    )
    student_weight, teacher_weight = student_held, teacher_held
    other = swap_cores(both_weights(1 - which))
    student_other = swap_cores(student_sent)
    teacher_other = swap_cores(teacher_sent)
    residual_other = swap_cores(columns_of(residual_sent, 1 - which))
    places_other = swap_cores(positions_sent).reshape(token_count, 1)
    places = positions.reshape(token_count, 1)
    scale = layer_scale.reshape(1, DOUT)

    early, late = gather_rows(own, other)
    student_part, teacher_part, student_late, teacher_late, turned = early_forward(
        order, early, student_mix, student_other, teacher_mix, teacher_other
    )
    student_out, matched, sums = late_forward(
        order, late, student_late, teacher_late, student_part, teacher_part, residual, residual_other, scale, places,
        places_other
    )
    grads, tokens = backward(
        total_tokens, order, student_out, matched, sums, swap_cores(sums), scale, turned
    )

    student_tokens = join_columns(which, tokens[:token_count], swap_cores(tokens[token_count:]))

    by_chip = fsdp_exchange(grads)
    chip_rows = jnp.sum(by_chip.astype(jnp.float32), axis=0).astype(jnp.bfloat16)
    by_copy = dp_exchange(chip_rows.reshape(2, 16, 16, half // 2).transpose(1, 0, 2, 3))
    copy_rows = jnp.sum(by_copy.astype(jnp.float32), axis=0).astype(jnp.bfloat16)
    full = dp_exchange(jnp.broadcast_to(copy_rows[None], (16, 2, 16, half // 2)))

    def rows_of(index):
        return (
            lax.dynamic_slice_in_dim(full, index * 8, 8, axis=0).transpose(0, 2, 1, 3).reshape(128, half)
        )

    grad = join_columns(which, rows_of(core), swap_cores(rows_of(1 - core))).astype(jnp.float32)
    weight_next, teacher_next, first_next, squares_next = adamw_update(
        grad, student_weight, teacher_weight, moment, second
    )
    return (weight_next, teacher_next, first_next, squares_next, student_tokens)


def solution(mesh):
    split = Mesh(mesh.devices.reshape(8, 2, 4, 2, 2), AXES)
    tokens = P(AXES, None)
    owned = P(("y", "xhi", "core"), None)
    return jax.shard_map(
        shards,
        mesh=split,
        in_specs=(tokens, tokens, tokens, tokens, P(), owned, owned, owned, owned),
        out_specs=(owned, owned, owned, owned, tokens),
        check_vma=False,
    )
```

```python
import functools

import jax
import jax.numpy as jnp
from jax import lax
from jax.experimental import pallas as pl
from jax.experimental.pallas import tpu as pltpu
from jax.sharding import Mesh, PartitionSpec as P

KIN = 2048
DOUT = 2048
PATCHES = 144
EPS = 1e-06
AXES = ("z", "xlo", "y", "xhi", "core")
VMEM_LIMIT = 60 * 1024 * 1024

X_INDEX = (0, 2, 1, 3)
CORE_SWAP = ((0, 1), (1, 0))
X_NEAR = tuple((X_INDEX[a], X_INDEX[b]) for a, b in ((1, 2), (2, 1), (0, 3), (3, 0)))


def from_next(size):
    return tuple(((i + 1) % size, i) for i in range(size))


def from_previous(size):
    return tuple((i, (i + 1) % size) for i in range(size))


def with_core_flip(pairs):
    return tuple((2 * a + 1 - core, 2 * b + core) for a, b in pairs for core in range(2))


DP_GROUPS = tuple(tuple(z * 2 + ((z + side) & 1) for z in range(8)) for side in range(2))


def swap_cores(value):
    return lax.ppermute(value, "core", CORE_SWAP)


def from_y_next(value):
    return lax.ppermute(value, "y", from_next(4))


def from_y_previous(value):
    return lax.ppermute(value, "y", from_previous(4))


def from_x_near(value):
    return lax.ppermute(value, ("xlo", "xhi"), X_NEAR)


def from_z_next(value):
    return lax.ppermute(value, ("z", "core"), with_core_flip(from_next(8)))


def from_z_previous(value):
    return lax.ppermute(value, ("z", "core"), with_core_flip(from_previous(8)))


def from_x_twin(value):
    return lax.ppermute(value, ("xlo", "core"), with_core_flip(CORE_SWAP))


def to_y_next(value):
    return from_y_previous(value)


def to_y_previous(value):
    return from_y_next(value)


EARLY = (
    (0, 0, 0), (1, 0, 0), (0, 1, 0), (0, 3, 0), (0, 0, 1), (0, 2, 0), (0, 3, 1), (0, 1, 1), (1, 1, 0), (1, 3, 0),
    (1, 0, 1),
)
LATE = ((0, 2, 1), (1, 2, 0), (1, 3, 1), (1, 1, 1), (1, 2, 1))
SENT = ((1, 2, 1), (1, 2, 0), (1, 1, 1), (1, 3, 0), (1, 3, 1), (1, 1, 0), (1, 0, 1), (1, 0, 0))
KEPT = tuple((0, dy, dx) for side, dy, dx in SENT)
HALF_AT = len(EARLY) + len(LATE)
TURNED_AT = HALF_AT + 1


def gather_rows(own, other, swapped):
    up, down, across = from_y_next(own), from_y_previous(own), from_x_near(own)
    up, down, across, other, *swapped = lax.optimization_barrier((up, down, across, other, *swapped))
    up_two = from_y_next(up)
    across_up = from_x_near(up)
    across_down = from_y_previous(across)
    passed_up, passed_down, passed_across = from_z_next(up), from_z_previous(down), from_x_twin(across)
    up_two, across_up, across_down, passed_up, passed_down, passed_across = lax.optimization_barrier(
        (up_two, across_up, across_down, passed_up, passed_down, passed_across)
    )
    student = from_y_next(across_up[0])
    teacher = from_y_previous(across_down[1])
    passed_two = from_z_next(up_two)
    passed_across_up = from_z_previous(across_up)
    passed_across_down = from_x_twin(across_down)
    student, teacher = lax.optimization_barrier((student, teacher))
    passed_student = from_z_next(student)
    passed_teacher = from_z_previous(teacher)
    early = (
        own, other, up, down, across, up_two, across_down, across_up, passed_up, passed_down, passed_across,
    )
    late = (
        student, teacher, passed_two, passed_across_down, passed_across_up, passed_student, passed_teacher,
    )
    return early, late, swapped


def early_kernel(order, student_own, student_other, teacher_own, teacher_other, *refs):
    count = len(EARLY)
    weights = refs[:count]
    student_out, teacher_out, student_late, teacher_late, turned, mix, held = refs[count:]
    step, own = pl.program_id(0), student_own.shape[0]

    @pl.when(step == 0)
    def _():
        for block in range(count + len(LATE)):
            columns = pl.ds(pl.multiple_of(order[block] * 128, 128), 128)
            at = block if block < count else block - count
            spot = slice(at * 128, (at + 1) * 128)
            to_student = mix.at[0] if block < count else student_late
            to_teacher = mix.at[1] if block < count else teacher_late
            to_student[:own, spot] = student_own[:, columns]
            to_student[own:, spot] = student_other[:, columns]
            to_teacher[:own, spot] = teacher_own[:, columns]
            to_teacher[own:, spot] = teacher_other[:, columns]

    for block in range(count):
        rows = slice(block * 128, (block + 1) * 128)
        held[0, rows, :] = weights[block][0]
        held[1, rows, :] = weights[block][1]
    student_out[...] = jnp.dot(mix[0], held[0], preferred_element_type=jnp.float32)
    teacher_out[...] = jnp.dot(mix[1], held[1], preferred_element_type=jnp.float32)
    for block in range(turned.shape[0]):
        spot = order[TURNED_AT + step * turned.shape[0] + block]
        columns = pl.ds(pl.multiple_of(spot * 128, 128), 128)
        turned[block] = jnp.concatenate([student_own[:, columns], student_other[:, columns]], axis=0).T


def early_forward(order, weights, student_own, student_other, teacher_own, teacher_other):
    own, columns, width = student_own.shape[0], weights[0].shape[-1], 256
    rows, steps, count = 2 * own, columns // width, len(EARLY)
    whole = pl.BlockSpec((own, KIN), lambda j, order: (0, 0))
    column = pl.BlockSpec((rows, width), lambda j, order: (0, j))
    late = pl.BlockSpec((rows, len(LATE) * 128), lambda j, order: (0, 0))
    return pl.pallas_call(
        early_kernel,
        grid_spec=pltpu.PrefetchScalarGridSpec(
            num_scalar_prefetch=1,
            grid=(steps,),
            in_specs=[whole] * 4 + [pl.BlockSpec((2, 128, width), lambda j, order: (0, 0, j))] * count,
            out_specs=[column, column, late, late, pl.BlockSpec((16 // steps, 128, rows), lambda j, order: (j, 0, 0))],
            scratch_shapes=[
                pltpu.VMEM((2, rows, count * 128), jnp.bfloat16),
                pltpu.VMEM((2, count * 128, width), jnp.bfloat16),
            ],
        ),
        out_shape=[
            jax.ShapeDtypeStruct((rows, columns), jnp.float32),
            jax.ShapeDtypeStruct((rows, columns), jnp.float32),
            jax.ShapeDtypeStruct((rows, len(LATE) * 128), jnp.bfloat16),
            jax.ShapeDtypeStruct((rows, len(LATE) * 128), jnp.bfloat16),
            jax.ShapeDtypeStruct((16, 128, rows), jnp.bfloat16),
        ],
        compiler_params=pltpu.CompilerParams(vmem_limit_bytes=VMEM_LIMIT),
        cost_estimate=pl.CostEstimate(
            flops=4 * rows * count * 128 * columns, bytes_accessed=18 * 1024 * 1024, transcendentals=0
        ),
    )(order, student_own, student_other, teacher_own, teacher_other, *weights)


def late_kernel(
    order, student_mix, teacher_mix, student_part, teacher_part, residual_own, residual_other, scale, places_own,
    places_other, *refs
):
    weights = refs[:7]
    student_out, matched_out, sums_out, held = refs[7:]
    depth = held.shape[1]
    held[0, :128, :] = weights[0][...]
    held[1, :128, :] = weights[1][...]
    for block in range(1, 4):
        rows = slice(block * 128, (block + 1) * 128)
        held[0, rows, :] = weights[block + 1][0]
        held[1, rows, :] = weights[block + 1][1]
    held[0, depth - 128 :, :] = weights[5][...]
    held[1, depth - 128 :, :] = weights[6][...]
    factor = scale[...] * (KIN ** (-0.5))
    student_sum = student_part[...] + jnp.dot(student_mix[...], held[0], preferred_element_type=jnp.float32)
    teacher_sum = teacher_part[...] + jnp.dot(teacher_mix[...], held[1], preferred_element_type=jnp.float32)
    own = residual_own.shape[0]
    lane = lax.broadcasted_iota(jnp.int32, (PATCHES, PATCHES), 1)
    students, parts = [], []
    for side, (residual, places) in enumerate(((residual_own, places_own), (residual_other, places_other))):
        tokens = slice(side * own, (side + 1) * own)
        base = residual[...].astype(jnp.float32)
        students.append(base + factor * student_sum[tokens])
        teacher = base + factor * teacher_sum[tokens]
        high = teacher.astype(jnp.bfloat16)
        low = (teacher - high.astype(jnp.float32)).astype(jnp.bfloat16)
        for crop in range(own // PATCHES):
            rows = slice(crop * PATCHES, (crop + 1) * PATCHES)
            pick = (places[rows, :] == lane).astype(jnp.float32).astype(jnp.bfloat16)
            parts.append(
                jnp.dot(pick, high[rows], preferred_element_type=jnp.float32)
                + jnp.dot(pick, low[rows], preferred_element_type=jnp.float32)
            )
    student = jnp.concatenate(students, axis=0)
    matched = jnp.concatenate(parts, axis=0)
    student_out[...] = student
    matched_out[...] = matched
    spot = lax.broadcasted_iota(jnp.int32, sums_out.shape, 1)
    sums = jnp.where(
        spot == 0,
        jnp.sum(student * student, axis=-1, keepdims=True),
        jnp.where(
            spot == 1,
            jnp.sum(matched * matched, axis=-1, keepdims=True),
            jnp.where(spot == 2, jnp.sum(student * matched, axis=-1, keepdims=True), 0.0),
        ),
    )

    @pl.when(pl.program_id(0) == 0)
    def _():
        sums_out[...] = sums

    @pl.when(pl.program_id(0) != 0)
    def _():
        sums_out[...] += sums


def late_forward(
    order, weights, student_mix, teacher_mix, student_part, teacher_part, residual_own, residual_other, scale,
    places_own, places_other
):
    (rows, columns), own, width, depth = student_part.shape, residual_own.shape[0], 256, student_mix.shape[1]
    steps = columns // width
    mix = pl.BlockSpec((rows, depth), lambda j, order: (0, 0))
    column = pl.BlockSpec((rows, width), lambda j, order: (0, j))
    places = pl.BlockSpec((own, 1), lambda j, order: (0, 0))
    pair = pl.BlockSpec((2, 128, width), lambda j, order: (0, 0, j))
    single = pl.BlockSpec((128, width), lambda j, order: (0, j))
    return pl.pallas_call(
        late_kernel,
        grid_spec=pltpu.PrefetchScalarGridSpec(
            num_scalar_prefetch=1,
            grid=(steps,),
            in_specs=[
                mix,
                mix,
                column,
                column,
                pl.BlockSpec((own, width), lambda j, order: (0, order[HALF_AT] * steps + j)),
                pl.BlockSpec((own, width), lambda j, order: (0, j)),
                pl.BlockSpec((1, width), lambda j, order: (0, order[HALF_AT] * steps + j)),
                places,
                places,
                single,
                single,
                pair,
                pair,
                pair,
                single,
                single,
            ],
            out_specs=[column, column, pl.BlockSpec((rows, 128), lambda j, order: (0, 0))],
            scratch_shapes=[pltpu.VMEM((2, depth, width), jnp.bfloat16)],
        ),
        out_shape=[
            jax.ShapeDtypeStruct((rows, columns), jnp.float32),
            jax.ShapeDtypeStruct((rows, columns), jnp.float32),
            jax.ShapeDtypeStruct((rows, 128), jnp.float32),
        ],
        compiler_params=pltpu.CompilerParams(vmem_limit_bytes=VMEM_LIMIT),
        cost_estimate=pl.CostEstimate(
            flops=4 * rows * depth * columns, bytes_accessed=16 * 1024 * 1024, transcendentals=0
        ),
    )(
        order, student_mix, teacher_mix, student_part, teacher_part, residual_own, residual_other, scale, places_own,
        places_other, *weights
    )


def send_kernel(
    total_tokens, order, student, matched, sums, more_sums, scale, mix, next_out, previous_out, twin_out, held_out,
    tokens_out
):
    own = more_sums.shape[0] // 2
    swapped = jnp.concatenate([more_sums[own:, :], more_sums[:own, :]], axis=0)
    total = (sums[...] + swapped) * (1.0 / DOUT)
    inverse_rms = lax.rsqrt(total[:, 0:1] + EPS)
    inverse_matched = lax.rsqrt(total[:, 1:2] + EPS)
    overlap = inverse_rms * inverse_matched * total[:, 2:3]
    shared = inverse_rms * (1.0 / total_tokens)
    student_part = shared * inverse_rms * (EPS * inverse_rms * inverse_rms + overlap)
    matched_part = shared * inverse_matched
    values = student[...]
    tokens_out[...] = (values * inverse_rms).astype(jnp.bfloat16)
    factor = scale[...] * (KIN ** (-0.5))
    held_out[...] = (factor * (values * student_part - matched[...] * matched_part)).astype(jnp.bfloat16)
    at = 0
    for out in (next_out, previous_out, twin_out):
        count = out.shape[0]
        grad = jnp.dot(
            mix[at : at + count].reshape(count * 128, mix.shape[-1]),
            held_out[...],
            preferred_element_type=jnp.float32,
        )
        out[...] = grad.astype(jnp.bfloat16).reshape(out.shape)
        at += count


def send_grads(total_tokens, order, student, matched, sums, more_sums, scale, turned):
    (rows, columns), width = student.shape, 256
    steps = columns // width
    column = pl.BlockSpec((rows, width), lambda j, order: (0, j))
    narrow = pl.BlockSpec((rows, 128), lambda j, order: (0, 0))

    def blocks(count):
        return pl.BlockSpec((count, 128, width), lambda j, order: (0, 0, j))

    return pl.pallas_call(
        functools.partial(send_kernel, total_tokens),
        grid_spec=pltpu.PrefetchScalarGridSpec(
            num_scalar_prefetch=1,
            grid=(steps,),
            in_specs=[
                column,
                column,
                narrow,
                narrow,
                pl.BlockSpec((1, width), lambda j, order: (0, order[HALF_AT] * steps + j)),
                pl.BlockSpec((8, 128, rows), lambda j, order: (0, 0, 0)),
            ],
            out_specs=[blocks(3), blocks(3), blocks(2), column, column],
        ),
        out_shape=[
            jax.ShapeDtypeStruct((3, 128, columns), jnp.bfloat16),
            jax.ShapeDtypeStruct((3, 128, columns), jnp.bfloat16),
            jax.ShapeDtypeStruct((2, 128, columns), jnp.bfloat16),
            jax.ShapeDtypeStruct((rows, columns), jnp.bfloat16),
            jax.ShapeDtypeStruct((rows, columns), jnp.bfloat16),
        ],
        compiler_params=pltpu.CompilerParams(vmem_limit_bytes=VMEM_LIMIT),
        cost_estimate=pl.CostEstimate(
            flops=rows * KIN * columns, bytes_accessed=12 * 1024 * 1024, transcendentals=0
        ),
    )(order, student, matched, sums, more_sums, scale, turned)


def keep_kernel(held, mix, out):
    grad = jnp.dot(
        mix[...].reshape(8 * 128, mix.shape[-1]), held[...], preferred_element_type=jnp.float32
    )
    out[...] = grad.reshape(out.shape)


def keep_grads(held, turned):
    (rows, columns), width = held.shape, 256
    return pl.pallas_call(
        keep_kernel,
        grid=(columns // width,),
        in_specs=[
            pl.BlockSpec((rows, width), lambda j: (0, j)),
            pl.BlockSpec((8, 128, rows), lambda j: (1, 0, 0)),
        ],
        out_specs=pl.BlockSpec((8, 128, width), lambda j: (0, 0, j)),
        out_shape=jax.ShapeDtypeStruct((8, 128, columns), jnp.float32),
        compiler_params=pltpu.CompilerParams(vmem_limit_bytes=VMEM_LIMIT),
        cost_estimate=pl.CostEstimate(
            flops=rows * KIN * columns, bytes_accessed=7 * 1024 * 1024, transcendentals=0
        ),
    )(held, turned)


def add_kernel(plan, count, *refs):
    inputs, outs = refs[:count], refs[count:]
    at = 0
    for out, (rows, terms) in zip(outs, plan):
        total = None
        for skip in terms:
            ref = inputs[at]
            value = (ref[0] if len(ref.shape) == 3 else ref[...]).astype(jnp.float32)
            if value.shape[0] < rows.stop - rows.start:
                gap = jnp.zeros_like(value)
                value = jnp.concatenate([gap, value] if skip else [value, gap], axis=0)
            else:
                value = value[rows]
            total = value if total is None else total + value
            at += 1
        out[...] = total.astype(jnp.bfloat16)


def add_blocks(*outs):
    width, operands, specs, plan = 512, [], [], []
    for rows, terms in outs:
        skips = []
        for array, index in terms:
            operands.append(array)
            skips.append(index == "second")
            if array.ndim == 3:
                specs.append(pl.BlockSpec((1, 128, width), functools.partial(lambda at, j: (at, 0, j), index)))
            else:
                specs.append(pl.BlockSpec((array.shape[0], width), lambda j: (0, j)))
        plan.append((rows, tuple(skips)))
    columns = operands[0].shape[-1]
    sizes = [rows.stop - rows.start for rows, _ in plan]
    return pl.pallas_call(
        functools.partial(add_kernel, tuple(plan), len(operands)),
        grid=(columns // width,),
        in_specs=specs,
        out_specs=[pl.BlockSpec((size, width), lambda j: (0, j)) for size in sizes],
        out_shape=[jax.ShapeDtypeStruct((size, columns), jnp.bfloat16) for size in sizes],
        compiler_params=pltpu.CompilerParams(vmem_limit_bytes=VMEM_LIMIT),
    )(*operands)


def reduce_rows(kept, next_sent, previous_sent, twin_sent):
    passed = (from_z_previous(next_sent), from_z_next(previous_sent), from_x_twin(twin_sent))
    passed = lax.optimization_barrier(passed)
    places = {}
    for number, (_, dy, dx) in enumerate(SENT):
        group = 0 if number < 3 else 1 if number < 6 else 2
        places[dy, dx] = ((kept, number), (passed[group], number - 3 * group))
    whole = slice(0, 128)
    first, last, up_two, down = add_blocks(
        (slice(0, 64), places[2, 1]), (slice(64, 128), places[2, 1]), (whole, places[2, 0]), (whole, places[3, 0])
    )
    first, last = to_y_next(first), to_y_previous(last)
    up_two, down = to_y_next(up_two), to_y_previous(down)
    first, last = lax.optimization_barrier((first, last))
    across_up, across_down = add_blocks(
        (whole, places[1, 1] + ((first, None),)), (whole, places[3, 1] + ((last, "second"),))
    )
    across_up, across_down, up_two = lax.optimization_barrier(
        (from_x_near(across_up), to_y_previous(across_down), up_two)
    )
    up, across = add_blocks(
        (whole, places[1, 0] + ((up_two, None), (across_up, None))), (whole, places[0, 1] + ((across_down, None),))
    )
    up, across, down = lax.optimization_barrier((to_y_next(up), from_x_near(across), down))
    (total,) = add_blocks((whole, places[0, 0] + ((up, None), (down, None), (across, None))))
    return total


def update_kernel(flip, grads, weight, teacher, first, squares, weight_out, teacher_out, first_out, squares_out):
    rows = []
    for index in range(grads.shape[0]):
        swap = ((flip[0] + index) & 1) == 1
        left = jnp.where(swap, grads[index, 1], grads[index, 0])
        right = jnp.where(swap, grads[index, 0], grads[index, 1])
        rows.append(jnp.concatenate([left, right], axis=1))
    grad = jnp.concatenate(rows, axis=0).astype(jnp.float32)
    first_next = 0.9 * first[...] + 0.1 * grad
    squares_next = 0.95 * squares[...] + 0.05 * grad * grad
    held = weight[...]
    weight_next = held - 0.1 * (first_next / (jnp.sqrt(squares_next) + 1e-08) + 0.04 * held)
    weight_out[...] = weight_next
    teacher_out[...] = 0.96 * teacher[...] + 0.04 * weight_next
    first_out[...] = first_next
    squares_out[...] = squares_next


def adamw_update(flip, grads, weight, teacher, first, squares):
    rows = pl.BlockSpec((32, DOUT), lambda i, flip: (i, 0))
    return pl.pallas_call(
        update_kernel,
        grid_spec=pltpu.PrefetchScalarGridSpec(
            num_scalar_prefetch=1,
            grid=(4,),
            in_specs=[pl.BlockSpec((2, 2, 16, DOUT // 2), lambda i, flip: (i, 0, 0, 0))] + [rows] * 4,
            out_specs=[rows] * 4,
        ),
        out_shape=[jax.ShapeDtypeStruct(weight.shape, jnp.float32)] * 4,
        compiler_params=pltpu.CompilerParams(vmem_limit_bytes=VMEM_LIMIT),
    )(flip, grads, weight, teacher, first, squares)


def join_columns(which, own, other):
    return jnp.where(
        which == 0, jnp.concatenate([own, other], axis=-1), jnp.concatenate([other, own], axis=-1)
    )


def shards(
    residual,
    student_mix,
    teacher_mix,
    positions,
    layer_scale,
    student_weight,
    teacher_weight,
    moment,
    second,
):
    half = DOUT // 2
    token_count = student_mix.shape[0]
    total_tokens = token_count * 256
    z, xlo, y, xhi, core = (lax.axis_index(name) for name in AXES)
    which = (core + z + xhi + xlo) & 1

    def columns_of(value, index):
        return lax.dynamic_slice_in_dim(value, index * half, half, axis=-1)

    def both_weights(index):
        return jnp.stack([columns_of(student_weight, index), columns_of(teacher_weight, index)]).astype(jnp.bfloat16)

    own = both_weights(which)
    order = jnp.stack(
        [
            (((y + dy) & 3) * 2 + (xhi ^ dx)) * 2 + (core ^ side)
            for side, dy, dx in EARLY + LATE
        ]
        + [which]
        + [(((y + dy) & 3) * 2 + (xhi ^ dx)) * 2 + (core ^ side) for side, dy, dx in SENT + KEPT]
    ).astype(jnp.int32)
    own, student_sent, teacher_sent, residual_sent, positions_sent, student_held, teacher_held = (
        lax.optimization_barrier(
            (own, student_mix, teacher_mix, residual, positions, student_weight, teacher_weight)
        )
    )
    student_weight, teacher_weight = student_held, teacher_held
    other = swap_cores(both_weights(1 - which))
    student_other = swap_cores(student_sent)
    teacher_other = swap_cores(teacher_sent)
    residual_other = swap_cores(columns_of(residual_sent, 1 - which))
    places_other = swap_cores(positions_sent)
    places = positions.reshape(token_count, 1)
    scale = layer_scale.reshape(1, DOUT)

    early, late, (student_other, teacher_other, residual_other, places_other) = gather_rows(
        own, other, (student_other, teacher_other, residual_other, places_other)
    )
    places_other = places_other.reshape(token_count, 1)
    student_part, teacher_part, student_late, teacher_late, turned = early_forward(
        order, early, student_mix, student_other, teacher_mix, teacher_other
    )
    student_out, matched, sums = late_forward(
        order, late, student_late, teacher_late, student_part, teacher_part, residual, residual_other, scale, places,
        places_other
    )
    next_sent, previous_sent, twin_sent, held, tokens = send_grads(
        total_tokens, order, student_out, matched, sums, swap_cores(sums), scale, turned
    )
    kept = keep_grads(held, turned)
    student_tokens = join_columns(which, tokens[:token_count], swap_cores(tokens[token_count:]))
    total = reduce_rows(kept, next_sent, previous_sent, twin_sent)
    total, student_tokens = lax.optimization_barrier((total, student_tokens))
    by_copy = lax.all_to_all(
        total.reshape(8, 16, half), ("z", "xlo"), 0, 0, axis_index_groups=DP_GROUPS
    )
    copy_rows = jnp.sum(by_copy.astype(jnp.float32), axis=0).astype(jnp.bfloat16)
    full = lax.all_to_all(jnp.broadcast_to(copy_rows[None], (16, 16, half)), ("z", "xlo"), 0, 0)
    flip = ((core + xhi) & 1).astype(jnp.int32).reshape(1)
    weight_next, teacher_next, first_next, squares_next = adamw_update(
        flip, full.reshape(8, 2, 16, half), student_weight, teacher_weight, moment, second
    )
    return (weight_next, teacher_next, first_next, squares_next, student_tokens)


def solution(mesh):
    split = Mesh(mesh.devices.reshape(8, 2, 4, 2, 2), AXES)
    tokens = P(AXES, None)
    owned = P(("y", "xhi", "core"), None)
    return jax.shard_map(
        shards,
        mesh=split,
        in_specs=(tokens, tokens, tokens, tokens, P(), owned, owned, owned, owned),
        out_specs=(owned, owned, owned, owned, tokens),
        check_vma=False,
    )
```

```python
import functools

import jax
import jax.numpy as jnp
from jax import lax
from jax.experimental import pallas as pl
from jax.experimental.pallas import tpu as pltpu
from jax.sharding import Mesh, PartitionSpec as P

KIN = 2048
DOUT = 2048
PATCHES = 144
EPS = 1e-06
AXES = ("z", "xlo", "y", "xhi", "core")
VMEM_LIMIT = 60 * 1024 * 1024

X_INDEX = (0, 2, 1, 3)
CORE_SWAP = ((0, 1), (1, 0))
X_NEAR = tuple((X_INDEX[a], X_INDEX[b]) for a, b in ((1, 2), (2, 1), (0, 3), (3, 0)))


def from_next(size):
    return tuple(((i + 1) % size, i) for i in range(size))


def from_previous(size):
    return tuple((i, (i + 1) % size) for i in range(size))


def with_core_flip(pairs):
    return tuple((2 * a + 1 - core, 2 * b + core) for a, b in pairs for core in range(2))


DP_GROUPS = tuple(tuple(z * 2 + ((z + side) & 1) for z in range(8)) for side in range(2))


def swap_cores(value):
    return lax.ppermute(value, "core", CORE_SWAP)


def from_y_next(value):
    return lax.ppermute(value, "y", from_next(4))


def from_y_previous(value):
    return lax.ppermute(value, "y", from_previous(4))


def from_x_near(value):
    return lax.ppermute(value, ("xlo", "xhi"), X_NEAR)


def from_z_next(value):
    return lax.ppermute(value, ("z", "core"), with_core_flip(from_next(8)))


def from_z_previous(value):
    return lax.ppermute(value, ("z", "core"), with_core_flip(from_previous(8)))


def from_x_twin(value):
    return lax.ppermute(value, ("xlo", "core"), with_core_flip(CORE_SWAP))


def to_y_next(value):
    return from_y_previous(value)


def to_y_previous(value):
    return from_y_next(value)


ORDER = (
    (0, 0, 0), (1, 0, 0), (0, 1, 0), (0, 3, 0), (0, 0, 1), (0, 2, 0), (0, 3, 1), (0, 1, 1), (1, 1, 0), (1, 3, 0),
    (1, 0, 1), (1, 2, 0), (1, 1, 1), (1, 3, 1), (0, 2, 1), (1, 2, 1),
)
SPLIT = 14
SENT = ((2, 1), (2, 0), (1, 1), (3, 0), (3, 1), (1, 0), (0, 1), (0, 0))
HALF_AT = len(ORDER)
CORE_AT = HALF_AT + 1
PLACE_AT = CORE_AT + 1


def gather_rows(own, ready_other, swapped, prepare):
    up, down, across = from_y_next(own), from_y_previous(own), from_x_near(own)
    up, down, across, swapped = lax.optimization_barrier((up, down, across, swapped))
    up_two = from_y_next(up)
    across_down = from_y_previous(across)
    across_up = from_x_near(up)
    passed_up, passed_down = from_z_next(up), from_z_previous(down)
    up_two, across_up, across_down, passed_up, passed_down, prepared = lax.optimization_barrier(
        (up_two, across_up, across_down, passed_up, passed_down, prepare(*swapped))
    )
    student = from_y_next(across_up[0])
    teacher = from_y_previous(across_down[1])
    passed_two = from_z_next(up_two)
    passed_across_up = from_z_previous(across_up)
    passed_across = from_x_twin(across)
    (student, teacher), other = ready_other((student, teacher))
    passed_student = from_z_next(student)
    passed_teacher = from_z_previous(teacher)
    passed_student, passed_teacher, other = lax.optimization_barrier((passed_student, passed_teacher, other))
    other = swap_cores(other)
    passed_across_down = from_x_twin(lax.optimization_barrier((across_down, passed_across))[0])
    pieces = (
        own, other, up, down, across, up_two, across_down, across_up, passed_up, passed_down, passed_across,
        passed_two, passed_across_up, passed_across_down, student, teacher, passed_student, passed_teacher,
    )
    return pieces, prepared


def prepare_kernel(
    order, student_own, student_other, teacher_own, teacher_other, residual_own, residual_other, places_own, places_other,
    student_out, teacher_out, residual_out, picked_out, sent_out, kept_out
):
    own = student_own.shape[0]
    lane = lax.broadcasted_iota(jnp.int32, (PATCHES, PATCHES), 1)
    sides = ((teacher_own, residual_own, places_own), (teacher_other, residual_other, places_other))
    for side, (teacher, residual, places) in enumerate(sides):
        for crop in range(own // PATCHES):
            rows = slice(crop * PATCHES, (crop + 1) * PATCHES)
            out_rows = slice(side * own + crop * PATCHES, side * own + (crop + 1) * PATCHES)
            pick = (places[rows, :] == lane).astype(jnp.float32).astype(jnp.bfloat16)
            teacher_out[out_rows, :] = jnp.dot(
                pick, teacher[rows, :], preferred_element_type=jnp.float32
            ).astype(jnp.bfloat16)
            picked_out[out_rows, :] = jnp.dot(
                pick, residual[rows, :], preferred_element_type=jnp.float32
            ).astype(jnp.bfloat16)
        residual_out[side * own : (side + 1) * own, :] = residual[...]
    student_out[:own, :] = student_own[...]
    student_out[own:, :] = student_other[...]
    turned = student_out[...].T
    first = order[CORE_AT] == 0
    kept_out[0] = jnp.where(first, turned[:128], turned[128:])
    sent_out[0] = jnp.where(first, turned[128:], turned[:128])


def prepare_rows(order, student_own, student_other, teacher_own, teacher_other, residual, residual_other, places, places_other):
    own, steps = student_own.shape[0], 8
    rows, columns = 2 * own, DOUT // 2
    width, narrow = KIN // steps, columns // steps
    mix = pl.BlockSpec((own, width), lambda i, order: (0, i))
    place = pl.BlockSpec((own, 1), lambda i, order: (0, 0))
    packed = pl.BlockSpec((rows, width), lambda i, order: (0, i))
    slim = pl.BlockSpec((rows, narrow), lambda i, order: (0, i))
    turned = pl.BlockSpec((1, 128, rows), lambda i, order: (order[PLACE_AT + i], 0, 0))
    return pl.pallas_call(
        prepare_kernel,
        grid_spec=pltpu.PrefetchScalarGridSpec(
            num_scalar_prefetch=1,
            grid=(steps,),
            in_specs=[mix] * 4
            + [
                pl.BlockSpec((own, narrow), lambda i, order: (0, order[HALF_AT] * steps + i)),
                pl.BlockSpec((own, narrow), lambda i, order: (0, order[HALF_AT] * steps + i)),
                place,
                place,
            ],
            out_specs=[packed, packed, slim, slim, turned, turned],
        ),
        out_shape=[
            jax.ShapeDtypeStruct((rows, KIN), jnp.bfloat16),
            jax.ShapeDtypeStruct((rows, KIN), jnp.bfloat16),
            jax.ShapeDtypeStruct((rows, columns), jnp.bfloat16),
            jax.ShapeDtypeStruct((rows, columns), jnp.bfloat16),
            jax.ShapeDtypeStruct((8, 128, rows), jnp.bfloat16),
            jax.ShapeDtypeStruct((8, 128, rows), jnp.bfloat16),
        ],
        compiler_params=pltpu.CompilerParams(vmem_limit_bytes=VMEM_LIMIT),
        cost_estimate=pl.CostEstimate(
            flops=4 * rows * PATCHES * KIN, bytes_accessed=16 * 1024 * 1024, transcendentals=0
        ),
    )(order, student_own, student_other, teacher_own, teacher_other, residual, residual_other, places, places_other)


def forward_kernel(order, student_mix, teacher_mix, residual, picked, scale, *refs):
    count = SPLIT + 2 * (len(ORDER) - SPLIT)
    weights, (student_out, matched_out, sums_out, held) = refs[:count], refs[count:]
    for block in range(len(ORDER)):
        rows = pl.ds(pl.multiple_of(order[block] * 128, 128), 128)
        if block < SPLIT:
            held[0, rows, :] = weights[block][0]
            held[1, rows, :] = weights[block][1]
        else:
            held[0, rows, :] = weights[2 * block - SPLIT][...]
            held[1, rows, :] = weights[2 * block - SPLIT + 1][...]
    factor = scale[...] * (KIN ** (-0.5))
    student = residual[...].astype(jnp.float32) + factor * jnp.dot(
        student_mix[...], held[0], preferred_element_type=jnp.float32
    )
    matched = picked[...].astype(jnp.float32) + factor * jnp.dot(
        teacher_mix[...], held[1], preferred_element_type=jnp.float32
    )
    student_out[...] = student
    matched_out[...] = matched
    spot = lax.broadcasted_iota(jnp.int32, sums_out.shape, 1)
    sums = jnp.where(
        spot == 0,
        jnp.sum(student * student, axis=-1, keepdims=True),
        jnp.where(
            spot == 1,
            jnp.sum(matched * matched, axis=-1, keepdims=True),
            jnp.where(spot == 2, jnp.sum(student * matched, axis=-1, keepdims=True), 0.0),
        ),
    )

    @pl.when(pl.program_id(0) == 0)
    def _():
        sums_out[...] = sums

    @pl.when(pl.program_id(0) != 0)
    def _():
        sums_out[...] += sums


def forward(order, pieces, student_mix, teacher_mix, residual, picked, scale):
    rows, columns, width = student_mix.shape[0], residual.shape[1], 256
    steps = columns // width
    whole = pl.BlockSpec((rows, KIN), lambda j, order: (0, 0))
    column = pl.BlockSpec((rows, width), lambda j, order: (0, j))
    pair = pl.BlockSpec((2, 128, width), lambda j, order: (0, 0, j))
    single = pl.BlockSpec((128, width), lambda j, order: (0, j))
    return pl.pallas_call(
        forward_kernel,
        grid_spec=pltpu.PrefetchScalarGridSpec(
            num_scalar_prefetch=1,
            grid=(steps,),
            in_specs=[
                whole,
                whole,
                column,
                column,
                pl.BlockSpec((1, width), lambda j, order: (0, order[HALF_AT] * steps + j)),
            ]
            + [pair] * SPLIT
            + [single] * (2 * (len(ORDER) - SPLIT)),
            out_specs=[column, column, pl.BlockSpec((rows, 128), lambda j, order: (0, 0))],
            scratch_shapes=[pltpu.VMEM((2, KIN, width), jnp.bfloat16)],
        ),
        out_shape=[
            jax.ShapeDtypeStruct((rows, columns), jnp.float32),
            jax.ShapeDtypeStruct((rows, columns), jnp.float32),
            jax.ShapeDtypeStruct((rows, 128), jnp.float32),
        ],
        compiler_params=pltpu.CompilerParams(vmem_limit_bytes=VMEM_LIMIT),
        cost_estimate=pl.CostEstimate(
            flops=4 * rows * KIN * columns, bytes_accessed=20 * 1024 * 1024, transcendentals=0
        ),
    )(order, student_mix, teacher_mix, residual, picked, scale, *pieces)


def send_kernel(
    total_tokens, order, student, matched, sums, more_sums, scale, mix, next_out, previous_out, twin_out, held_out,
    tokens_out
):
    own = more_sums.shape[0] // 2
    swapped = jnp.concatenate([more_sums[own:, :], more_sums[:own, :]], axis=0)
    total = (sums[...] + swapped) * (1.0 / DOUT)
    inverse_rms = lax.rsqrt(total[:, 0:1] + EPS)
    inverse_matched = lax.rsqrt(total[:, 1:2] + EPS)
    overlap = inverse_rms * inverse_matched * total[:, 2:3]
    shared = inverse_rms * (1.0 / total_tokens)
    student_part = shared * inverse_rms * (EPS * inverse_rms * inverse_rms + overlap)
    matched_part = shared * inverse_matched
    values = student[...]
    tokens_out[...] = (values * inverse_rms).astype(jnp.bfloat16)
    factor = scale[...] * (KIN ** (-0.5))
    held_out[...] = (factor * (values * student_part - matched[...] * matched_part)).astype(jnp.bfloat16)
    at = 0
    for out in (next_out, previous_out, twin_out):
        count = out.shape[0]
        grad = jnp.dot(
            mix[at : at + count].reshape(count * 128, mix.shape[-1]),
            held_out[...],
            preferred_element_type=jnp.float32,
        )
        out[...] = grad.astype(jnp.bfloat16).reshape(out.shape)
        at += count


def send_grads(total_tokens, order, student, matched, sums, more_sums, scale, turned):
    (rows, columns), width = student.shape, 256
    steps = columns // width
    column = pl.BlockSpec((rows, width), lambda j, order: (0, j))
    narrow = pl.BlockSpec((rows, 128), lambda j, order: (0, 0))

    def blocks(count):
        return pl.BlockSpec((count, 128, width), lambda j, order: (0, 0, j))

    return pl.pallas_call(
        functools.partial(send_kernel, total_tokens),
        grid_spec=pltpu.PrefetchScalarGridSpec(
            num_scalar_prefetch=1,
            grid=(steps,),
            in_specs=[
                column,
                column,
                narrow,
                narrow,
                pl.BlockSpec((1, width), lambda j, order: (0, order[HALF_AT] * steps + j)),
                pl.BlockSpec((8, 128, rows), lambda j, order: (0, 0, 0)),
            ],
            out_specs=[blocks(3), blocks(3), blocks(2), column, column],
        ),
        out_shape=[
            jax.ShapeDtypeStruct((3, 128, columns), jnp.bfloat16),
            jax.ShapeDtypeStruct((3, 128, columns), jnp.bfloat16),
            jax.ShapeDtypeStruct((2, 128, columns), jnp.bfloat16),
            jax.ShapeDtypeStruct((rows, columns), jnp.bfloat16),
            jax.ShapeDtypeStruct((rows, columns), jnp.bfloat16),
        ],
        compiler_params=pltpu.CompilerParams(vmem_limit_bytes=VMEM_LIMIT),
        cost_estimate=pl.CostEstimate(
            flops=rows * KIN * columns, bytes_accessed=12 * 1024 * 1024, transcendentals=0
        ),
    )(order, student, matched, sums, more_sums, scale, turned)


def keep_kernel(held, mix, out):
    grad = jnp.dot(
        mix[...].reshape(8 * 128, mix.shape[-1]), held[...], preferred_element_type=jnp.float32
    )
    out[...] = grad.reshape(out.shape)


def keep_grads(held, kept):
    (rows, columns), width = held.shape, 256
    return pl.pallas_call(
        keep_kernel,
        grid=(columns // width,),
        in_specs=[
            pl.BlockSpec((rows, width), lambda j: (0, j)),
            pl.BlockSpec((8, 128, rows), lambda j: (0, 0, 0)),
        ],
        out_specs=pl.BlockSpec((8, 128, width), lambda j: (0, 0, j)),
        out_shape=jax.ShapeDtypeStruct((8, 128, columns), jnp.float32),
        compiler_params=pltpu.CompilerParams(vmem_limit_bytes=VMEM_LIMIT),
        cost_estimate=pl.CostEstimate(
            flops=rows * KIN * columns, bytes_accessed=7 * 1024 * 1024, transcendentals=0
        ),
    )(held, kept)


def add_kernel(plan, count, *refs):
    inputs, outs = refs[:count], refs[count:]
    at = 0
    for out, (rows, terms) in zip(outs, plan):
        total = None
        for skip in terms:
            ref = inputs[at]
            value = (ref[0] if len(ref.shape) == 3 else ref[...]).astype(jnp.float32)
            if value.shape[0] < rows.stop - rows.start:
                gap = jnp.zeros_like(value)
                value = jnp.concatenate([gap, value] if skip else [value, gap], axis=0)
            else:
                value = value[rows]
            total = value if total is None else total + value
            at += 1
        out[...] = total.astype(jnp.bfloat16)


def add_blocks(*outs):
    width, operands, specs, plan = 512, [], [], []
    for rows, terms in outs:
        skips = []
        for array, index in terms:
            operands.append(array)
            skips.append(index == "second")
            if array.ndim == 3:
                specs.append(pl.BlockSpec((1, 128, width), functools.partial(lambda at, j: (at, 0, j), index)))
            else:
                specs.append(pl.BlockSpec((array.shape[0], width), lambda j: (0, j)))
        plan.append((rows, tuple(skips)))
    columns = operands[0].shape[-1]
    sizes = [rows.stop - rows.start for rows, _ in plan]
    return pl.pallas_call(
        functools.partial(add_kernel, tuple(plan), len(operands)),
        grid=(columns // width,),
        in_specs=specs,
        out_specs=[pl.BlockSpec((size, width), lambda j: (0, j)) for size in sizes],
        out_shape=[jax.ShapeDtypeStruct((size, columns), jnp.bfloat16) for size in sizes],
        compiler_params=pltpu.CompilerParams(vmem_limit_bytes=VMEM_LIMIT),
    )(*operands)


def reduce_rows(kept, next_sent, previous_sent, twin_sent):
    passed = (from_z_previous(next_sent), from_z_next(previous_sent), from_x_twin(twin_sent))
    passed = lax.optimization_barrier(passed)
    places = {}
    for number, (dy, dx) in enumerate(SENT):
        group = 0 if number < 3 else 1 if number < 6 else 2
        places[dy, dx] = ((kept, number), (passed[group], number - 3 * group))
    whole = slice(0, 128)
    first, last, up_two, down = add_blocks(
        (slice(0, 64), places[2, 1]), (slice(64, 128), places[2, 1]), (whole, places[2, 0]), (whole, places[3, 0])
    )
    first, last = to_y_next(first), to_y_previous(last)
    up_two, down = to_y_next(up_two), to_y_previous(down)
    first, last = lax.optimization_barrier((first, last))
    across_up, across_down = add_blocks(
        (whole, places[1, 1] + ((first, None),)), (whole, places[3, 1] + ((last, "second"),))
    )
    across_up, across_down, up_two = lax.optimization_barrier(
        (from_x_near(across_up), to_y_previous(across_down), up_two)
    )
    up, across = add_blocks(
        (whole, places[1, 0] + ((up_two, None), (across_up, None))), (whole, places[0, 1] + ((across_down, None),))
    )
    up, across, down = lax.optimization_barrier((to_y_next(up), from_x_near(across), down))
    total = up.astype(jnp.float32) + down.astype(jnp.float32) + across.astype(jnp.float32)
    for array, index in places[0, 0]:
        total = total + array[index].astype(jnp.float32)
    return total.astype(jnp.bfloat16)


def update_kernel(flip, grads, weight, teacher, first, squares, weight_out, teacher_out, first_out, squares_out):
    rows = []
    for index in range(grads.shape[0]):
        swap = ((flip[0] + index) & 1) == 1
        left = jnp.where(swap, grads[index, 1], grads[index, 0])
        right = jnp.where(swap, grads[index, 0], grads[index, 1])
        rows.append(jnp.concatenate([left, right], axis=1))
    grad = jnp.concatenate(rows, axis=0).astype(jnp.float32)
    first_next = 0.9 * first[...] + 0.1 * grad
    squares_next = 0.95 * squares[...] + 0.05 * grad * grad
    held = weight[...]
    weight_next = held - 0.1 * (first_next / (jnp.sqrt(squares_next) + 1e-08) + 0.04 * held)
    weight_out[...] = weight_next
    teacher_out[...] = 0.96 * teacher[...] + 0.04 * weight_next
    first_out[...] = first_next
    squares_out[...] = squares_next


def adamw_update(flip, grads, weight, teacher, first, squares):
    rows = pl.BlockSpec((32, DOUT), lambda i, flip: (i, 0))
    return pl.pallas_call(
        update_kernel,
        grid_spec=pltpu.PrefetchScalarGridSpec(
            num_scalar_prefetch=1,
            grid=(4,),
            in_specs=[pl.BlockSpec((2, 2, 16, DOUT // 2), lambda i, flip: (i, 0, 0, 0))] + [rows] * 4,
            out_specs=[rows] * 4,
        ),
        out_shape=[jax.ShapeDtypeStruct(weight.shape, jnp.float32)] * 4,
        compiler_params=pltpu.CompilerParams(vmem_limit_bytes=VMEM_LIMIT),
    )(flip, grads, weight, teacher, first, squares)


def join_columns(which, own, other):
    return jnp.where(
        which == 0, jnp.concatenate([own, other], axis=-1), jnp.concatenate([other, own], axis=-1)
    )


def shards(
    residual,
    student_mix,
    teacher_mix,
    positions,
    layer_scale,
    student_weight,
    teacher_weight,
    moment,
    second,
):
    half = DOUT // 2
    token_count = student_mix.shape[0]
    total_tokens = token_count * 256
    z, xlo, y, xhi, core = (lax.axis_index(name) for name in AXES)
    which = (core + z + xhi + xlo) & 1

    def columns_of(value, index):
        return lax.dynamic_slice_in_dim(value, index * half, half, axis=-1)

    def both_weights(index):
        return jnp.stack([columns_of(student_weight, index), columns_of(teacher_weight, index)]).astype(jnp.bfloat16)

    own = both_weights(which)
    chips = jnp.stack([((y + dy) & 3) * 2 + (xhi ^ dx) for dy, dx in SENT])
    number = jnp.arange(8, dtype=jnp.int32)
    place = jnp.sum(jnp.where(chips[:, None] == number[None, :], number[:, None], 0), axis=0)
    order = jnp.concatenate(
        [
            jnp.stack(
                [(((y + dy) & 3) * 2 + (xhi ^ dx)) * 2 + (core ^ side) for side, dy, dx in ORDER] + [which, core]
            ).astype(jnp.int32),
            place.astype(jnp.int32),
        ]
    )
    own, student_sent, teacher_sent, residual_sent, positions_sent, student_held, teacher_held = (
        lax.optimization_barrier(
            (own, student_mix, teacher_mix, residual, positions, student_weight, teacher_weight)
        )
    )
    student_weight, teacher_weight = student_held, teacher_held
    student_other, residual_sent = lax.optimization_barrier((swap_cores(student_sent), residual_sent))
    residual_other = swap_cores(residual_sent)
    teacher_other, positions_sent = lax.optimization_barrier((swap_cores(teacher_sent), positions_sent))
    places_other = swap_cores(positions_sent)

    def ready_other(ready):
        ready, student_late, teacher_late = lax.optimization_barrier((ready, student_held, teacher_held))
        return ready, jnp.stack(
            [columns_of(student_late, 1 - which), columns_of(teacher_late, 1 - which)]
        ).astype(jnp.bfloat16)

    scale = layer_scale.reshape(1, DOUT)

    def prepare(student_other, teacher_other, residual_other, places_other):
        return prepare_rows(
            order, student_mix, student_other, teacher_mix, teacher_other, residual, residual_other,
            positions.reshape(token_count, 1), places_other.reshape(token_count, 1)
        )

    pieces, (student_rows, teacher_rows, residual_rows, picked_rows, sent_mix, kept_mix) = gather_rows(
        own, ready_other, (student_other, teacher_other, residual_other, places_other), prepare
    )
    student_out, matched, sums = forward(
        order, pieces, student_rows, teacher_rows, residual_rows, picked_rows, scale
    )
    next_sent, previous_sent, twin_sent, held, tokens = send_grads(
        total_tokens, order, student_out, matched, sums, swap_cores(sums), scale, sent_mix
    )
    kept = keep_grads(held, kept_mix)
    student_tokens = join_columns(which, tokens[:token_count], swap_cores(tokens[token_count:]))
    total = reduce_rows(kept, next_sent, previous_sent, twin_sent)
    total, student_tokens = lax.optimization_barrier((total, student_tokens))
    by_copy = lax.all_to_all(
        total.reshape(8, 16, half), ("z", "xlo"), 0, 0, axis_index_groups=DP_GROUPS
    )
    copy_rows = jnp.sum(by_copy.astype(jnp.float32), axis=0).astype(jnp.bfloat16)
    full = lax.all_to_all(jnp.broadcast_to(copy_rows[None], (16, 16, half)), ("z", "xlo"), 0, 0)
    flip = ((core + xhi) & 1).astype(jnp.int32).reshape(1)
    weight_next, teacher_next, first_next, squares_next = adamw_update(
        flip, full.reshape(8, 2, 16, half), student_weight, teacher_weight, moment, second
    )
    return (weight_next, teacher_next, first_next, squares_next, student_tokens)


def solution(mesh):
    split = Mesh(mesh.devices.reshape(8, 2, 4, 2, 2), AXES)
    tokens = P(AXES, None)
    owned = P(("y", "xhi", "core"), None)
    return jax.shard_map(
        shards,
        mesh=split,
        in_specs=(tokens, tokens, tokens, tokens, P(), owned, owned, owned, owned),
        out_specs=(owned, owned, owned, owned, tokens),
        check_vma=False,
    )
```

```python
import functools

import jax
import jax.numpy as jnp
from jax import lax
from jax.experimental import pallas as pl
from jax.experimental.pallas import tpu as pltpu
from jax.sharding import Mesh, PartitionSpec as P

KIN = 2048
DOUT = 2048
PATCHES = 144
EPS = 1e-06
AXES = ("z", "xlo", "y", "xhi", "core")
VMEM_LIMIT = 60 * 1024 * 1024

X_INDEX = (0, 2, 1, 3)
CORE_SWAP = ((0, 1), (1, 0))
X_NEAR = tuple((X_INDEX[a], X_INDEX[b]) for a, b in ((1, 2), (2, 1), (0, 3), (3, 0)))


def from_next(size):
    return tuple(((i + 1) % size, i) for i in range(size))


def from_previous(size):
    return tuple((i, (i + 1) % size) for i in range(size))


def with_core_flip(pairs):
    return tuple((2 * a + 1 - core, 2 * b + core) for a, b in pairs for core in range(2))


FSDP_GROUPS = tuple(
    tuple((xhi ^ side) * 8 + y * 2 + xhi for y in range(4) for xhi in range(2)) for side in range(2)
)
DP_GROUPS = tuple(tuple(z * 2 + ((z + side) & 1) for z in range(8)) for side in range(2))


def swap_cores(value):
    return lax.ppermute(value, "core", CORE_SWAP)


def from_y_next(value):
    return lax.ppermute(value, "y", from_next(4))


def from_y_previous(value):
    return lax.ppermute(value, "y", from_previous(4))


def from_x_near(value):
    return lax.ppermute(value, ("xlo", "xhi"), X_NEAR)


def from_z_next(value):
    return lax.ppermute(value, ("z", "core"), with_core_flip(from_next(8)))


def from_z_previous(value):
    return lax.ppermute(value, ("z", "core"), with_core_flip(from_previous(8)))


def from_x_twin(value):
    return lax.ppermute(value, ("xlo", "core"), with_core_flip(CORE_SWAP))


ORDER = (
    (0, 0, 0), (0, 1, 0), (0, 3, 0), (0, 0, 1), (0, 2, 0), (0, 3, 1), (0, 1, 1), (1, 1, 0), (1, 3, 0), (0, 2, 1),
    (1, 2, 0), (1, 1, 1), (1, 3, 1), (1, 0, 1), (1, 0, 0), (1, 2, 1),
)
EARLY = 14
LATE = len(ORDER) - EARLY
HALF_AT = len(ORDER)
CORE_AT = HALF_AT + 1
SENT = (3, 3, 2)


def prepare_kernel(
    order, student_own, student_other, teacher_own, teacher_other, residual, places_own, places_other, student_early,
    teacher_early, student_late, teacher_late, picked_out, sent_out, kept_out, turned, packed, gathered
):
    own, step = student_own.shape[0], pl.program_id(0)
    lane = lax.broadcasted_iota(jnp.int32, (PATCHES, PATCHES), 1)
    for side, (teacher, places) in enumerate(((teacher_own, places_own), (teacher_other, places_other))):
        for crop in range(own // PATCHES):
            rows = slice(crop * PATCHES, (crop + 1) * PATCHES)
            out_rows = slice(side * own + crop * PATCHES, side * own + (crop + 1) * PATCHES)
            pick = (places[rows, :] == lane).astype(jnp.float32).astype(jnp.bfloat16)
            gathered[out_rows, :] = jnp.dot(
                pick, teacher[rows, :], preferred_element_type=jnp.float32
            ).astype(jnp.bfloat16)
            if side == 0:
                picked_out[rows, :] = jnp.dot(
                    pick, residual[rows, :], preferred_element_type=jnp.float32
                ).astype(jnp.bfloat16)
    packed[:own, :] = student_own[...]
    packed[own:, :] = student_other[...]
    turned[...] = packed[...].T
    core = order[CORE_AT]
    kept_out[0] = turned[pl.ds(pl.multiple_of(core * 128, 128), 128), :]
    sent_out[0] = turned[pl.ds(pl.multiple_of((1 - core) * 128, 128), 128), :]
    for part in range(2):
        columns = slice(part * 128, (part + 1) * 128)
        for block in range(len(ORDER)):
            @pl.when(order[block] == 2 * step + part)
            def _():
                at = block if block < EARLY else block - EARLY
                spot = slice(at * 128, (at + 1) * 128)
                if block < EARLY:
                    student_early[:, spot] = packed[:, columns]
                    teacher_early[:, spot] = gathered[:, columns]
                else:
                    student_late[:, spot] = packed[:, columns]
                    teacher_late[:, spot] = gathered[:, columns]


def prepare_rows(order, student_own, student_other, teacher_own, teacher_other, residual, places, places_other):
    own, steps = student_own.shape[0], 8
    rows, width = 2 * own, KIN // steps
    mix = pl.BlockSpec((own, width), lambda i, order: (0, i))
    place = pl.BlockSpec((own, 1), lambda i, order: (0, 0))
    early = pl.BlockSpec((rows, EARLY * 128), lambda i, order: (0, 0))
    late = pl.BlockSpec((rows, LATE * 128), lambda i, order: (0, 0))
    turned = pl.BlockSpec((1, 128, rows), lambda i, order: (i, 0, 0))
    return pl.pallas_call(
        prepare_kernel,
        grid_spec=pltpu.PrefetchScalarGridSpec(
            num_scalar_prefetch=1,
            grid=(steps,),
            in_specs=[mix] * 5 + [place] * 2,
            out_specs=[early, early, late, late, mix, turned, turned],
            scratch_shapes=[
                pltpu.VMEM((width, rows), jnp.bfloat16),
                pltpu.VMEM((rows, width), jnp.bfloat16),
                pltpu.VMEM((rows, width), jnp.bfloat16),
            ],
        ),
        out_shape=[
            jax.ShapeDtypeStruct((rows, EARLY * 128), jnp.bfloat16),
            jax.ShapeDtypeStruct((rows, EARLY * 128), jnp.bfloat16),
            jax.ShapeDtypeStruct((rows, LATE * 128), jnp.bfloat16),
            jax.ShapeDtypeStruct((rows, LATE * 128), jnp.bfloat16),
            jax.ShapeDtypeStruct((own, DOUT), jnp.bfloat16),
            jax.ShapeDtypeStruct((8, 128, rows), jnp.bfloat16),
            jax.ShapeDtypeStruct((8, 128, rows), jnp.bfloat16),
        ],
        compiler_params=pltpu.CompilerParams(vmem_limit_bytes=VMEM_LIMIT),
        cost_estimate=pl.CostEstimate(
            flops=4 * rows * PATCHES * KIN, bytes_accessed=16 * 1024 * 1024, transcendentals=0
        ),
    )(order, student_own, student_other, teacher_own, teacher_other, residual, places, places_other)


def early_kernel(student_mix, teacher_mix, *refs):
    weights, (student_out, teacher_out, held) = refs[:EARLY], refs[EARLY:]
    for block in range(EARLY):
        rows = slice(block * 128, (block + 1) * 128)
        held[0, rows, :] = weights[block][0]
        held[1, rows, :] = weights[block][1]
    student_out[...] = jnp.dot(student_mix[...], held[0], preferred_element_type=jnp.float32)
    teacher_out[...] = jnp.dot(teacher_mix[...], held[1], preferred_element_type=jnp.float32)


def early_forward(pieces, student_mix, teacher_mix):
    rows, depth = student_mix.shape
    columns, width = pieces[0].shape[-1], 256
    whole = pl.BlockSpec((rows, depth), lambda j: (0, 0))
    column = pl.BlockSpec((rows, width), lambda j: (0, j))
    return pl.pallas_call(
        early_kernel,
        grid=(columns // width,),
        in_specs=[whole, whole] + [pl.BlockSpec((2, 128, width), lambda j: (0, 0, j))] * EARLY,
        out_specs=[column, column],
        out_shape=[jax.ShapeDtypeStruct((rows, columns), jnp.float32)] * 2,
        scratch_shapes=[pltpu.VMEM((2, depth, width), jnp.bfloat16)],
        compiler_params=pltpu.CompilerParams(vmem_limit_bytes=VMEM_LIMIT),
        cost_estimate=pl.CostEstimate(
            flops=4 * rows * depth * columns, bytes_accessed=17 * 1024 * 1024, transcendentals=0
        ),
    )(student_mix, teacher_mix, *pieces)


def late_kernel(
    order, student_mix, teacher_mix, student_part, teacher_part, residual_own, residual_other, picked_own, picked_other,
    scale, *refs
):
    weights, (student_out, matched_out, sums_out, held) = refs[:LATE], refs[LATE:]
    for block in range(LATE):
        rows = slice(block * 128, (block + 1) * 128)
        held[0, rows, :] = weights[block][0]
        held[1, rows, :] = weights[block][1]
    factor = scale[...] * (KIN ** (-0.5))
    student_sum = student_part[...] + jnp.dot(student_mix[...], held[0], preferred_element_type=jnp.float32)
    teacher_sum = teacher_part[...] + jnp.dot(teacher_mix[...], held[1], preferred_element_type=jnp.float32)
    own = residual_own.shape[0]
    first = pl.program_id(0) == 0
    for side, (residual, picked) in enumerate(((residual_own, picked_own), (residual_other, picked_other))):
        tokens = slice(side * own, (side + 1) * own)
        student = residual[...].astype(jnp.float32) + factor * student_sum[tokens]
        matched = picked[...].astype(jnp.float32) + factor * teacher_sum[tokens]
        student_out[tokens, :] = student
        matched_out[tokens, :] = matched
        spot = lax.broadcasted_iota(jnp.int32, (own, 128), 1)
        sums = jnp.where(
            spot == 0,
            jnp.sum(student * student, axis=-1, keepdims=True),
            jnp.where(
                spot == 1,
                jnp.sum(matched * matched, axis=-1, keepdims=True),
                jnp.where(spot == 2, jnp.sum(student * matched, axis=-1, keepdims=True), 0.0),
            ),
        )
        sums_out[tokens, :] = sums + jnp.where(first, 0.0, sums_out[tokens, :])


def late_forward(
    order, pieces, student_mix, teacher_mix, student_part, teacher_part, residual, residual_other, picked, picked_other,
    scale
):
    (rows, columns), own, width = student_part.shape, residual.shape[0], 256
    steps = columns // width
    whole = pl.BlockSpec((rows, LATE * 128), lambda j, order: (0, 0))
    column = pl.BlockSpec((rows, width), lambda j, order: (0, j))
    tokens = pl.BlockSpec((own, width), lambda j, order: (0, order[HALF_AT] * steps + j))
    return pl.pallas_call(
        late_kernel,
        grid_spec=pltpu.PrefetchScalarGridSpec(
            num_scalar_prefetch=1,
            grid=(steps,),
            in_specs=[whole, whole, column, column]
            + [tokens] * 4
            + [pl.BlockSpec((1, width), lambda j, order: (0, order[HALF_AT] * steps + j))]
            + [pl.BlockSpec((2, 128, width), lambda j, order: (0, 0, j))] * LATE,
            out_specs=[column, column, pl.BlockSpec((rows, 128), lambda j, order: (0, 0))],
            scratch_shapes=[pltpu.VMEM((2, LATE * 128, width), jnp.bfloat16)],
        ),
        out_shape=[
            jax.ShapeDtypeStruct((rows, columns), jnp.float32),
            jax.ShapeDtypeStruct((rows, columns), jnp.float32),
            jax.ShapeDtypeStruct((rows, 128), jnp.float32),
        ],
        compiler_params=pltpu.CompilerParams(vmem_limit_bytes=VMEM_LIMIT),
        cost_estimate=pl.CostEstimate(
            flops=4 * rows * LATE * 128 * columns, bytes_accessed=13 * 1024 * 1024, transcendentals=0
        ),
    )(
        order, student_mix, teacher_mix, student_part, teacher_part, residual, residual_other, picked, picked_other,
        scale, *pieces
    )


def send_kernel(
    total_tokens, order, student, matched, sums, more_sums, scale, mix, next_out, previous_out, twin_out, held_out,
    tokens_own, tokens_other
):
    own = more_sums.shape[0] // 2
    swapped = jnp.concatenate([more_sums[own:, :], more_sums[:own, :]], axis=0)
    total = (sums[...] + swapped) * (1.0 / DOUT)
    inverse_rms = lax.rsqrt(total[:, 0:1] + EPS)
    inverse_matched = lax.rsqrt(total[:, 1:2] + EPS)
    overlap = inverse_rms * inverse_matched * total[:, 2:3]
    shared = inverse_rms * (1.0 / total_tokens)
    student_part = shared * inverse_rms * (EPS * inverse_rms * inverse_rms + overlap)
    matched_part = shared * inverse_matched
    values = student[...]
    tokens = (values * inverse_rms).astype(jnp.bfloat16)
    tokens_own[...] = tokens[:own]
    tokens_other[...] = tokens[own:]
    factor = scale[...] * (KIN ** (-0.5))
    held_out[...] = (factor * (values * student_part - matched[...] * matched_part)).astype(jnp.bfloat16)
    at = 0
    for out in (next_out, previous_out, twin_out):
        count = out.shape[0]
        grad = jnp.dot(
            mix[at : at + count].reshape(count * 128, mix.shape[-1]),
            held_out[...],
            preferred_element_type=jnp.float32,
        )
        out[...] = grad.astype(jnp.bfloat16).reshape(out.shape)
        at += count


def send_grads(total_tokens, order, student, matched, sums, more_sums, scale, turned):
    (rows, columns), width = student.shape, 256
    steps = columns // width
    column = pl.BlockSpec((rows, width), lambda j, order: (0, j))
    narrow = pl.BlockSpec((rows, 128), lambda j, order: (0, 0))
    half = pl.BlockSpec((rows // 2, width), lambda j, order: (0, j))

    def blocks(count):
        return pl.BlockSpec((count, 128, width), lambda j, order: (0, 0, j))

    return pl.pallas_call(
        functools.partial(send_kernel, total_tokens),
        grid_spec=pltpu.PrefetchScalarGridSpec(
            num_scalar_prefetch=1,
            grid=(steps,),
            in_specs=[
                column,
                column,
                narrow,
                narrow,
                pl.BlockSpec((1, width), lambda j, order: (0, order[HALF_AT] * steps + j)),
                pl.BlockSpec((8, 128, rows), lambda j, order: (0, 0, 0)),
            ],
            out_specs=[blocks(count) for count in SENT] + [column, half, half],
        ),
        out_shape=[
            jax.ShapeDtypeStruct((count, 128, columns), jnp.bfloat16) for count in SENT
        ]
        + [
            jax.ShapeDtypeStruct((rows, columns), jnp.bfloat16),
            jax.ShapeDtypeStruct((rows // 2, columns), jnp.bfloat16),
            jax.ShapeDtypeStruct((rows // 2, columns), jnp.bfloat16),
        ],
        compiler_params=pltpu.CompilerParams(vmem_limit_bytes=VMEM_LIMIT),
        cost_estimate=pl.CostEstimate(
            flops=rows * KIN * columns, bytes_accessed=12 * 1024 * 1024, transcendentals=0
        ),
    )(order, student, matched, sums, more_sums, scale, turned)


def keep_kernel(held, mix, out):
    grad = jnp.dot(
        mix[...].reshape(8 * 128, mix.shape[-1]), held[...], preferred_element_type=jnp.float32
    )
    out[...] = grad.reshape(out.shape)


def keep_grads(held, kept):
    (rows, columns), width = held.shape, 256
    return pl.pallas_call(
        keep_kernel,
        grid=(columns // width,),
        in_specs=[
            pl.BlockSpec((rows, width), lambda j: (0, j)),
            pl.BlockSpec((8, 128, rows), lambda j: (0, 0, 0)),
        ],
        out_specs=pl.BlockSpec((8, 128, width), lambda j: (0, 0, j)),
        out_shape=jax.ShapeDtypeStruct((8, 128, columns), jnp.float32),
        compiler_params=pltpu.CompilerParams(vmem_limit_bytes=VMEM_LIMIT),
        cost_estimate=pl.CostEstimate(
            flops=rows * KIN * columns, bytes_accessed=7 * 1024 * 1024, transcendentals=0
        ),
    )(held, kept)


def add_kernel(kept, *refs):
    passed, out = refs[:-1], refs[-1]
    at = 0
    for part in passed:
        spot = slice(at, at + part.shape[0])
        out[spot] = (kept[spot] + part[...].astype(jnp.float32)).astype(jnp.bfloat16)
        at += part.shape[0]


def add_passed(kept, passed):
    width = 256

    def blocks(count):
        return pl.BlockSpec((count, 128, width), lambda j: (0, 0, j))

    return pl.pallas_call(
        add_kernel,
        grid=(kept.shape[-1] // width,),
        in_specs=[blocks(8)] + [blocks(count) for count in SENT],
        out_specs=blocks(8),
        out_shape=jax.ShapeDtypeStruct(kept.shape, jnp.bfloat16),
        compiler_params=pltpu.CompilerParams(vmem_limit_bytes=VMEM_LIMIT),
    )(kept, *passed)


def update_kernel(flip, grads, weight, teacher, first, squares, weight_out, teacher_out, first_out, squares_out):
    rows = []
    for index in range(grads.shape[0]):
        swap = ((flip[0] + index) & 1) == 1
        left = jnp.where(swap, grads[index, 1], grads[index, 0])
        right = jnp.where(swap, grads[index, 0], grads[index, 1])
        rows.append(jnp.concatenate([left, right], axis=1))
    grad = jnp.concatenate(rows, axis=0).astype(jnp.float32)
    first_next = 0.9 * first[...] + 0.1 * grad
    squares_next = 0.95 * squares[...] + 0.05 * grad * grad
    held = weight[...]
    weight_next = held - 0.1 * (first_next / (jnp.sqrt(squares_next) + 1e-08) + 0.04 * held)
    weight_out[...] = weight_next
    teacher_out[...] = 0.96 * teacher[...] + 0.04 * weight_next
    first_out[...] = first_next
    squares_out[...] = squares_next


def adamw_update(flip, grads, weight, teacher, first, squares):
    rows = pl.BlockSpec((32, DOUT), lambda i, flip: (i, 0))
    return pl.pallas_call(
        update_kernel,
        grid_spec=pltpu.PrefetchScalarGridSpec(
            num_scalar_prefetch=1,
            grid=(4,),
            in_specs=[pl.BlockSpec((2, 2, 16, DOUT // 2), lambda i, flip: (i, 0, 0, 0))] + [rows] * 4,
            out_specs=[rows] * 4,
        ),
        out_shape=[jax.ShapeDtypeStruct(weight.shape, jnp.float32)] * 4,
        compiler_params=pltpu.CompilerParams(vmem_limit_bytes=VMEM_LIMIT),
    )(flip, grads, weight, teacher, first, squares)


def join_columns(which, own, other):
    return jnp.where(
        which == 0, jnp.concatenate([own, other], axis=-1), jnp.concatenate([other, own], axis=-1)
    )


def shards(
    residual,
    student_mix,
    teacher_mix,
    positions,
    layer_scale,
    student_weight,
    teacher_weight,
    moment,
    second,
):
    half = DOUT // 2
    token_count = student_mix.shape[0]
    total_tokens = token_count * 256
    z, xlo, y, xhi, core = (lax.axis_index(name) for name in AXES)
    which = (core + z + xhi + xlo) & 1

    def columns_of(value, index):
        return lax.dynamic_slice_in_dim(value, index * half, half, axis=-1)

    def both_weights(index):
        return jnp.stack([columns_of(student_weight, index), columns_of(teacher_weight, index)]).astype(jnp.bfloat16)

    own = both_weights(which)
    order = jnp.stack(
        [(((y + dy) & 3) * 2 + (xhi ^ dx)) * 2 + (core ^ side) for side, dy, dx in ORDER] + [which, core]
    ).astype(jnp.int32)
    scale = layer_scale.reshape(1, DOUT)

    own, student_sent, teacher_sent, positions_sent, student_held, teacher_held, residual = lax.optimization_barrier(
        (own, student_mix, teacher_mix, positions, student_weight, teacher_weight, residual)
    )
    student_weight, teacher_weight = student_held, teacher_held
    student_other, positions_sent = lax.optimization_barrier((swap_cores(student_sent), positions_sent))
    teacher_other, places_other = swap_cores(teacher_sent), swap_cores(positions_sent)
    up, down, across, student_other, teacher_other, places, places_other, student_held, teacher_held = (
        lax.optimization_barrier(
            (
                from_y_next(own), from_y_previous(own), from_x_near(own), student_other, teacher_other, positions,
                places_other, student_held, teacher_held,
            )
        )
    )
    other_sent = jnp.stack(
        [columns_of(student_held, 1 - which), columns_of(teacher_held, 1 - which)]
    ).astype(jnp.bfloat16)
    (
        up_two, across_down, across_up, passed_up, passed_down, across, other_sent, places, places_other, student_other,
        teacher_other, residual,
    ) = lax.optimization_barrier(
        (
            from_y_next(up), from_y_previous(across), from_x_near(up), from_z_next(up), from_z_previous(down), across,
            other_sent, places.reshape(token_count, 1), places_other.reshape(token_count, 1), student_other,
            teacher_other, residual,
        )
    )
    prepared = prepare_rows(
        order, student_mix, student_other, teacher_mix, teacher_other, residual, places, places_other
    )
    (
        across_two, passed_two, passed_across_up, passed_across_down, passed_across, prepared, other_sent, residual_sent
    ) = lax.optimization_barrier(
        (
            from_y_next(across_up), from_z_next(up_two), from_z_previous(across_up), from_x_near(passed_down),
            from_x_twin(across), prepared, other_sent, residual,
        )
    )
    student_early, teacher_early, student_late, teacher_late, picked, sent_mix, kept_mix = prepared
    passed_across_two = from_z_next(across_two)
    residual_other, picked_other, other = swap_cores(residual_sent), swap_cores(picked), swap_cores(other_sent)
    student_part, teacher_part = early_forward(
        (
            own, up, down, across, up_two, across_down, across_up, passed_up, passed_down, across_two, passed_two,
            passed_across_up, passed_across_down, passed_across,
        ),
        student_early,
        teacher_early,
    )
    student_out, matched, sums = late_forward(
        order, (other, passed_across_two), student_late, teacher_late, student_part, teacher_part, residual,
        residual_other, picked, picked_other, scale
    )
    *sent, held, tokens_own, tokens_other = send_grads(
        total_tokens, order, student_out, matched, sums, swap_cores(sums), scale, sent_mix
    )
    kept = keep_grads(held, kept_mix)
    student_tokens = join_columns(which, tokens_own, swap_cores(tokens_other))
    passed = lax.optimization_barrier((from_z_previous(sent[0]), from_z_next(sent[1]), from_x_twin(sent[2])))
    by_chip = lax.all_to_all(
        add_passed(kept, passed), ("xlo", "y", "xhi"), 0, 0, axis_index_groups=FSDP_GROUPS
    )
    by_chip, student_tokens = lax.optimization_barrier((by_chip, student_tokens))
    total = jnp.sum(by_chip.astype(jnp.float32), axis=0).astype(jnp.bfloat16)
    by_copy = lax.all_to_all(
        total.reshape(8, 16, half), ("z", "xlo"), 0, 0, axis_index_groups=DP_GROUPS
    )
    copy_rows = jnp.sum(by_copy.astype(jnp.float32), axis=0).astype(jnp.bfloat16)
    full = lax.all_to_all(jnp.broadcast_to(copy_rows[None], (16, 16, half)), ("z", "xlo"), 0, 0)
    flip = ((core + xhi) & 1).astype(jnp.int32).reshape(1)
    weight_next, teacher_next, first_next, squares_next = adamw_update(
        flip, full.reshape(8, 2, 16, half), student_weight, teacher_weight, moment, second
    )
    return (weight_next, teacher_next, first_next, squares_next, student_tokens)


def solution(mesh):
    split = Mesh(mesh.devices.reshape(8, 2, 4, 2, 2), AXES)
    tokens = P(AXES, None)
    owned = P(("y", "xhi", "core"), None)
    return jax.shard_map(
        shards,
        mesh=split,
        in_specs=(tokens, tokens, tokens, tokens, P(), owned, owned, owned, owned),
        out_specs=(owned, owned, owned, owned, tokens),
        check_vma=False,
    )
```

```python
import functools

import jax
import jax.numpy as jnp
from jax import lax
from jax.experimental import pallas as pl
from jax.experimental.pallas import tpu as pltpu
from jax.sharding import Mesh, PartitionSpec as P

KIN = 2048
DOUT = 2048
PATCHES = 144
EPS = 1e-06
AXES = ("z", "xlo", "y", "xhi", "core")
VMEM_LIMIT = 32 * 1024 * 1024

X_INDEX = (0, 2, 1, 3)
CORE_SWAP = ((0, 1), (1, 0))
X_NEAR = tuple((X_INDEX[a], X_INDEX[b]) for a, b in ((1, 2), (2, 1), (0, 3), (3, 0)))


def from_next(size):
    return tuple(((i + 1) % size, i) for i in range(size))


def from_previous(size):
    return tuple((i, (i + 1) % size) for i in range(size))


def with_core_flip(pairs):
    return tuple((2 * a + 1 - core, 2 * b + core) for a, b in pairs for core in range(2))


FSDP_GROUPS = tuple(
    tuple((xhi ^ side) * 8 + y * 2 + xhi for y in range(4) for xhi in range(2)) for side in range(2)
)
DP_GROUPS = tuple(tuple(z * 2 + ((z + side) & 1) for z in range(8)) for side in range(2))


def swap_cores(value):
    return lax.ppermute(value, "core", CORE_SWAP)


def from_y_next(value):
    return lax.ppermute(value, "y", from_next(4))


def from_y_previous(value):
    return lax.ppermute(value, "y", from_previous(4))


def from_x_near(value):
    return lax.ppermute(value, ("xlo", "xhi"), X_NEAR)


def from_z_next(value):
    return lax.ppermute(value, ("z", "core"), with_core_flip(from_next(8)))


def from_z_previous(value):
    return lax.ppermute(value, ("z", "core"), with_core_flip(from_previous(8)))


def from_x_twin(value):
    return lax.ppermute(value, ("xlo", "core"), with_core_flip(CORE_SWAP))


ORDER = (
    (0, 0, 0), (0, 1, 0), (0, 3, 0), (0, 0, 1), (0, 2, 0), (0, 3, 1), (0, 1, 1), (1, 1, 0), (1, 3, 0), (0, 2, 1),
    (1, 2, 0), (1, 1, 1), (1, 3, 1), (1, 0, 1), (1, 0, 0), (1, 2, 1),
)
EARLY = 14
LATE = len(ORDER) - EARLY
HALF_AT = len(ORDER)
CORE_AT = HALF_AT + 1
SENT = (3, 3, 2)


def prepare_kernel(
    order, student_own, student_other, teacher_own, teacher_other, residual, places_own, places_other, student_early,
    teacher_early, student_late, teacher_late, picked_out, sent_out, kept_out, turned, packed, gathered
):
    own, step = student_own.shape[0], pl.program_id(0)
    lane = lax.broadcasted_iota(jnp.int32, (PATCHES, PATCHES), 1)
    for side, (teacher, places) in enumerate(((teacher_own, places_own), (teacher_other, places_other))):
        for crop in range(own // PATCHES):
            rows = slice(crop * PATCHES, (crop + 1) * PATCHES)
            out_rows = slice(side * own + crop * PATCHES, side * own + (crop + 1) * PATCHES)
            pick = (places[rows, :] == lane).astype(jnp.float32).astype(jnp.bfloat16)
            gathered[out_rows, :] = jnp.dot(
                pick, teacher[rows, :], preferred_element_type=jnp.float32
            ).astype(jnp.bfloat16)
            if side == 0:
                picked_out[rows, :] = jnp.dot(
                    pick, residual[rows, :], preferred_element_type=jnp.float32
                ).astype(jnp.bfloat16)
    packed[:own, :] = student_own[...]
    packed[own:, :] = student_other[...]
    turned[...] = packed[...].T
    core = order[CORE_AT]
    kept_out[0] = turned[pl.ds(pl.multiple_of(core * 128, 128), 128), :]
    sent_out[0] = turned[pl.ds(pl.multiple_of((1 - core) * 128, 128), 128), :]
    for part in range(2):
        columns = slice(part * 128, (part + 1) * 128)
        for block in range(len(ORDER)):
            @pl.when(order[block] == 2 * step + part)
            def _():
                at = block if block < EARLY else block - EARLY
                spot = slice(at * 128, (at + 1) * 128)
                if block < EARLY:
                    student_early[:, spot] = packed[:, columns]
                    teacher_early[:, spot] = gathered[:, columns]
                else:
                    student_late[:, spot] = packed[:, columns]
                    teacher_late[:, spot] = gathered[:, columns]


def prepare_rows(order, student_own, student_other, teacher_own, teacher_other, residual, places, places_other):
    own, steps = student_own.shape[0], 8
    rows, width = 2 * own, KIN // steps
    mix = pl.BlockSpec((own, width), lambda i, order: (0, i))
    place = pl.BlockSpec((own, 1), lambda i, order: (0, 0))
    early = pl.BlockSpec((rows, EARLY * 128), lambda i, order: (0, 0))
    late = pl.BlockSpec((rows, LATE * 128), lambda i, order: (0, 0))
    turned = pl.BlockSpec((1, 128, rows), lambda i, order: (i, 0, 0))
    return pl.pallas_call(
        prepare_kernel,
        grid_spec=pltpu.PrefetchScalarGridSpec(
            num_scalar_prefetch=1,
            grid=(steps,),
            in_specs=[mix] * 5 + [place] * 2,
            out_specs=[early, early, late, late, mix, turned, turned],
            scratch_shapes=[
                pltpu.VMEM((width, rows), jnp.bfloat16),
                pltpu.VMEM((rows, width), jnp.bfloat16),
                pltpu.VMEM((rows, width), jnp.bfloat16),
            ],
        ),
        out_shape=[
            jax.ShapeDtypeStruct((rows, EARLY * 128), jnp.bfloat16),
            jax.ShapeDtypeStruct((rows, EARLY * 128), jnp.bfloat16),
            jax.ShapeDtypeStruct((rows, LATE * 128), jnp.bfloat16),
            jax.ShapeDtypeStruct((rows, LATE * 128), jnp.bfloat16),
            jax.ShapeDtypeStruct((own, DOUT), jnp.bfloat16),
            jax.ShapeDtypeStruct((8, 128, rows), jnp.bfloat16),
            jax.ShapeDtypeStruct((8, 128, rows), jnp.bfloat16),
        ],
        compiler_params=pltpu.CompilerParams(vmem_limit_bytes=VMEM_LIMIT),
        cost_estimate=pl.CostEstimate(
            flops=4 * rows * PATCHES * KIN, bytes_accessed=16 * 1024 * 1024, transcendentals=0
        ),
    )(order, student_own, student_other, teacher_own, teacher_other, residual, places, places_other)


def early_kernel(student_mix, teacher_mix, *refs):
    weights, (student_out, teacher_out, held) = refs[:EARLY], refs[EARLY:]
    for block in range(EARLY):
        rows = slice(block * 128, (block + 1) * 128)
        held[0, rows, :] = weights[block][0]
        held[1, rows, :] = weights[block][1]
    student_out[...] = jnp.dot(student_mix[...], held[0], preferred_element_type=jnp.float32)
    teacher_out[...] = jnp.dot(teacher_mix[...], held[1], preferred_element_type=jnp.float32)


def early_forward(pieces, student_mix, teacher_mix):
    rows, depth = student_mix.shape
    columns, width = pieces[0].shape[-1], 256
    whole = pl.BlockSpec((rows, depth), lambda j: (0, 0))
    column = pl.BlockSpec((rows, width), lambda j: (0, j))
    return pl.pallas_call(
        early_kernel,
        grid=(columns // width,),
        in_specs=[whole, whole] + [pl.BlockSpec((2, 128, width), lambda j: (0, 0, j))] * EARLY,
        out_specs=[column, column],
        out_shape=[jax.ShapeDtypeStruct((rows, columns), jnp.float32)] * 2,
        scratch_shapes=[pltpu.VMEM((2, depth, width), jnp.bfloat16)],
        compiler_params=pltpu.CompilerParams(vmem_limit_bytes=VMEM_LIMIT),
        cost_estimate=pl.CostEstimate(
            flops=4 * rows * depth * columns, bytes_accessed=17 * 1024 * 1024, transcendentals=0
        ),
    )(student_mix, teacher_mix, *pieces)


def late_kernel(
    order, student_mix, teacher_mix, student_part, teacher_part, residual_own, residual_other, picked_own, picked_other,
    scale, *refs
):
    weights, (student_out, matched_out, sums_out, held) = refs[:LATE], refs[LATE:]
    for block in range(LATE):
        rows = slice(block * 128, (block + 1) * 128)
        held[0, rows, :] = weights[block][0]
        held[1, rows, :] = weights[block][1]
    factor = scale[...] * (KIN ** (-0.5))
    student_sum = student_part[...] + jnp.dot(student_mix[...], held[0], preferred_element_type=jnp.float32)
    teacher_sum = teacher_part[...] + jnp.dot(teacher_mix[...], held[1], preferred_element_type=jnp.float32)
    own = residual_own.shape[0]
    first = pl.program_id(0) == 0
    for side, (residual, picked) in enumerate(((residual_own, picked_own), (residual_other, picked_other))):
        tokens = slice(side * own, (side + 1) * own)
        student = residual[...].astype(jnp.float32) + factor * student_sum[tokens]
        matched = picked[...].astype(jnp.float32) + factor * teacher_sum[tokens]
        student_out[tokens, :] = student
        matched_out[tokens, :] = matched
        spot = lax.broadcasted_iota(jnp.int32, (own, 128), 1)
        sums = jnp.where(
            spot == 0,
            jnp.sum(student * student, axis=-1, keepdims=True),
            jnp.where(
                spot == 1,
                jnp.sum(matched * matched, axis=-1, keepdims=True),
                jnp.where(spot == 2, jnp.sum(student * matched, axis=-1, keepdims=True), 0.0),
            ),
        )
        sums_out[tokens, :] = sums + jnp.where(first, 0.0, sums_out[tokens, :])


def late_forward(
    order, pieces, student_mix, teacher_mix, student_part, teacher_part, residual, residual_other, picked, picked_other,
    scale
):
    (rows, columns), own, width = student_part.shape, residual.shape[0], 256
    steps = columns // width
    whole = pl.BlockSpec((rows, LATE * 128), lambda j, order: (0, 0))
    column = pl.BlockSpec((rows, width), lambda j, order: (0, j))
    tokens = pl.BlockSpec((own, width), lambda j, order: (0, order[HALF_AT] * steps + j))
    return pl.pallas_call(
        late_kernel,
        grid_spec=pltpu.PrefetchScalarGridSpec(
            num_scalar_prefetch=1,
            grid=(steps,),
            in_specs=[whole, whole, column, column]
            + [tokens] * 4
            + [pl.BlockSpec((1, width), lambda j, order: (0, order[HALF_AT] * steps + j))]
            + [pl.BlockSpec((2, 128, width), lambda j, order: (0, 0, j))] * LATE,
            out_specs=[column, column, pl.BlockSpec((rows, 128), lambda j, order: (0, 0))],
            scratch_shapes=[pltpu.VMEM((2, LATE * 128, width), jnp.bfloat16)],
        ),
        out_shape=[
            jax.ShapeDtypeStruct((rows, columns), jnp.float32),
            jax.ShapeDtypeStruct((rows, columns), jnp.float32),
            jax.ShapeDtypeStruct((rows, 128), jnp.float32),
        ],
        compiler_params=pltpu.CompilerParams(vmem_limit_bytes=VMEM_LIMIT),
        cost_estimate=pl.CostEstimate(
            flops=4 * rows * LATE * 128 * columns, bytes_accessed=13 * 1024 * 1024, transcendentals=0
        ),
    )(
        order, student_mix, teacher_mix, student_part, teacher_part, residual, residual_other, picked, picked_other,
        scale, *pieces
    )


def send_kernel(
    total_tokens, order, student, matched, sums, more_sums, scale, mix, next_out, previous_out, twin_out, held_out,
    tokens_own, tokens_other
):
    own = more_sums.shape[0] // 2
    swapped = jnp.concatenate([more_sums[own:, :], more_sums[:own, :]], axis=0)
    total = (sums[...] + swapped) * (1.0 / DOUT)
    inverse_rms = lax.rsqrt(total[:, 0:1] + EPS)
    inverse_matched = lax.rsqrt(total[:, 1:2] + EPS)
    overlap = inverse_rms * inverse_matched * total[:, 2:3]
    shared = inverse_rms * (1.0 / total_tokens)
    student_part = shared * inverse_rms * (EPS * inverse_rms * inverse_rms + overlap)
    matched_part = shared * inverse_matched
    values = student[...]
    tokens = (values * inverse_rms).astype(jnp.bfloat16)
    tokens_own[...] = tokens[:own]
    tokens_other[...] = tokens[own:]
    factor = scale[...] * (KIN ** (-0.5))
    held_out[...] = (factor * (values * student_part - matched[...] * matched_part)).astype(jnp.bfloat16)
    at = 0
    for out in (next_out, previous_out, twin_out):
        count = out.shape[0]
        grad = jnp.dot(
            mix[at : at + count].reshape(count * 128, mix.shape[-1]),
            held_out[...],
            preferred_element_type=jnp.float32,
        )
        out[...] = grad.astype(jnp.bfloat16).reshape(out.shape)
        at += count


def send_grads(total_tokens, order, student, matched, sums, more_sums, scale, turned):
    (rows, columns), width = student.shape, 256
    steps = columns // width
    column = pl.BlockSpec((rows, width), lambda j, order: (0, j))
    narrow = pl.BlockSpec((rows, 128), lambda j, order: (0, 0))
    half = pl.BlockSpec((rows // 2, width), lambda j, order: (0, j))

    def blocks(count):
        return pl.BlockSpec((count, 128, width), lambda j, order: (0, 0, j))

    return pl.pallas_call(
        functools.partial(send_kernel, total_tokens),
        grid_spec=pltpu.PrefetchScalarGridSpec(
            num_scalar_prefetch=1,
            grid=(steps,),
            in_specs=[
                column,
                column,
                narrow,
                narrow,
                pl.BlockSpec((1, width), lambda j, order: (0, order[HALF_AT] * steps + j)),
                pl.BlockSpec((8, 128, rows), lambda j, order: (0, 0, 0)),
            ],
            out_specs=[blocks(count) for count in SENT] + [column, half, half],
        ),
        out_shape=[
            jax.ShapeDtypeStruct((count, 128, columns), jnp.bfloat16) for count in SENT
        ]
        + [
            jax.ShapeDtypeStruct((rows, columns), jnp.bfloat16),
            jax.ShapeDtypeStruct((rows // 2, columns), jnp.bfloat16),
            jax.ShapeDtypeStruct((rows // 2, columns), jnp.bfloat16),
        ],
        compiler_params=pltpu.CompilerParams(vmem_limit_bytes=VMEM_LIMIT),
        cost_estimate=pl.CostEstimate(
            flops=rows * KIN * columns, bytes_accessed=12 * 1024 * 1024, transcendentals=0
        ),
    )(order, student, matched, sums, more_sums, scale, turned)


def keep_kernel(held, mix, out):
    grad = jnp.dot(
        mix[...].reshape(8 * 128, mix.shape[-1]), held[...], preferred_element_type=jnp.float32
    )
    out[...] = grad.reshape(out.shape)


def keep_grads(held, kept):
    (rows, columns), width = held.shape, 256
    return pl.pallas_call(
        keep_kernel,
        grid=(columns // width,),
        in_specs=[
            pl.BlockSpec((rows, width), lambda j: (0, j)),
            pl.BlockSpec((8, 128, rows), lambda j: (0, 0, 0)),
        ],
        out_specs=pl.BlockSpec((8, 128, width), lambda j: (0, 0, j)),
        out_shape=jax.ShapeDtypeStruct((8, 128, columns), jnp.float32),
        compiler_params=pltpu.CompilerParams(vmem_limit_bytes=VMEM_LIMIT),
        cost_estimate=pl.CostEstimate(
            flops=rows * KIN * columns, bytes_accessed=7 * 1024 * 1024, transcendentals=0
        ),
    )(held, kept)


def add_kernel(kept, *refs):
    passed, out = refs[:-1], refs[-1]
    at = 0
    for part in passed:
        spot = slice(at, at + part.shape[0])
        out[spot] = (kept[spot] + part[...].astype(jnp.float32)).astype(jnp.bfloat16)
        at += part.shape[0]


def add_passed(kept, passed):
    width = 256

    def blocks(count):
        return pl.BlockSpec((count, 128, width), lambda j: (0, 0, j))

    return pl.pallas_call(
        add_kernel,
        grid=(kept.shape[-1] // width,),
        in_specs=[blocks(8)] + [blocks(count) for count in SENT],
        out_specs=blocks(8),
        out_shape=jax.ShapeDtypeStruct(kept.shape, jnp.bfloat16),
        compiler_params=pltpu.CompilerParams(vmem_limit_bytes=VMEM_LIMIT),
    )(kept, *passed)


def update_kernel(flip, grads, weight, teacher, first, squares, weight_out, teacher_out, first_out, squares_out):
    rows = []
    for index in range(grads.shape[0]):
        swap = ((flip[0] + index) & 1) == 1
        left = jnp.where(swap, grads[index, 1], grads[index, 0])
        right = jnp.where(swap, grads[index, 0], grads[index, 1])
        rows.append(jnp.concatenate([left, right], axis=1))
    grad = jnp.concatenate(rows, axis=0).astype(jnp.float32)
    first_next = 0.9 * first[...] + 0.1 * grad
    squares_next = 0.95 * squares[...] + 0.05 * grad * grad
    held = weight[...]
    weight_next = held - 0.1 * (first_next / (jnp.sqrt(squares_next) + 1e-08) + 0.04 * held)
    weight_out[...] = weight_next
    teacher_out[...] = 0.96 * teacher[...] + 0.04 * weight_next
    first_out[...] = first_next
    squares_out[...] = squares_next


def adamw_update(flip, grads, weight, teacher, first, squares):
    rows = pl.BlockSpec((32, DOUT), lambda i, flip: (i, 0))
    return pl.pallas_call(
        update_kernel,
        grid_spec=pltpu.PrefetchScalarGridSpec(
            num_scalar_prefetch=1,
            grid=(4,),
            in_specs=[pl.BlockSpec((2, 2, 16, DOUT // 2), lambda i, flip: (i, 0, 0, 0))] + [rows] * 4,
            out_specs=[rows] * 4,
        ),
        out_shape=[jax.ShapeDtypeStruct(weight.shape, jnp.float32)] * 4,
        compiler_params=pltpu.CompilerParams(vmem_limit_bytes=VMEM_LIMIT),
    )(flip, grads, weight, teacher, first, squares)


def join_columns(which, own, other):
    return jnp.where(
        which == 0, jnp.concatenate([own, other], axis=-1), jnp.concatenate([other, own], axis=-1)
    )


def shards(
    residual,
    student_mix,
    teacher_mix,
    positions,
    layer_scale,
    student_weight,
    teacher_weight,
    moment,
    second,
):
    half = DOUT // 2
    token_count = student_mix.shape[0]
    total_tokens = token_count * 256
    z, xlo, y, xhi, core = (lax.axis_index(name) for name in AXES)
    which = (core + z + xhi + xlo) & 1

    def columns_of(value, index):
        return lax.dynamic_slice_in_dim(value, index * half, half, axis=-1)

    def both_weights(index):
        return jnp.stack([columns_of(student_weight, index), columns_of(teacher_weight, index)]).astype(jnp.bfloat16)

    own = both_weights(which)
    order = jnp.stack(
        [(((y + dy) & 3) * 2 + (xhi ^ dx)) * 2 + (core ^ side) for side, dy, dx in ORDER] + [which, core]
    ).astype(jnp.int32)
    scale = layer_scale.reshape(1, DOUT)

    own, student_sent, teacher_sent, positions_sent, student_held, teacher_held, residual = lax.optimization_barrier(
        (own, student_mix, teacher_mix, positions, student_weight, teacher_weight, residual)
    )
    student_weight, teacher_weight = student_held, teacher_held
    student_other, positions_sent = lax.optimization_barrier((swap_cores(student_sent), positions_sent))
    teacher_other, places_other = swap_cores(teacher_sent), swap_cores(positions_sent)
    up, down, across, student_other, teacher_other, places, places_other, student_held, teacher_held = (
        lax.optimization_barrier(
            (
                from_y_next(own), from_y_previous(own), from_x_near(own), student_other, teacher_other, positions,
                places_other, student_held, teacher_held,
            )
        )
    )
    other_sent = jnp.stack(
        [columns_of(student_held, 1 - which), columns_of(teacher_held, 1 - which)]
    ).astype(jnp.bfloat16)
    (
        up_two, across_down, across_up, passed_up, passed_down, across, other_sent, places, places_other, student_other,
        teacher_other, residual,
    ) = lax.optimization_barrier(
        (
            from_y_next(up), from_y_previous(across), from_x_near(up), from_z_next(up), from_z_previous(down), across,
            other_sent, places.reshape(token_count, 1), places_other.reshape(token_count, 1), student_other,
            teacher_other, residual,
        )
    )
    prepared = prepare_rows(
        order, student_mix, student_other, teacher_mix, teacher_other, residual, places, places_other
    )
    (
        across_two, passed_two, passed_across_up, passed_across_down, passed_across, prepared, other_sent, residual_sent
    ) = lax.optimization_barrier(
        (
            from_y_next(across_up), from_z_next(up_two), from_z_previous(across_up), from_x_near(passed_down),
            from_x_twin(across), prepared, other_sent, residual,
        )
    )
    student_early, teacher_early, student_late, teacher_late, picked, sent_mix, kept_mix = prepared
    passed_across_two = from_z_next(across_two)
    residual_other, picked_other, other = swap_cores(residual_sent), swap_cores(picked), swap_cores(other_sent)
    student_part, teacher_part = early_forward(
        (
            own, up, down, across, up_two, across_down, across_up, passed_up, passed_down, across_two, passed_two,
            passed_across_up, passed_across_down, passed_across,
        ),
        student_early,
        teacher_early,
    )
    student_out, matched, sums = late_forward(
        order, (other, passed_across_two), student_late, teacher_late, student_part, teacher_part, residual,
        residual_other, picked, picked_other, scale
    )
    *sent, held, tokens_own, tokens_other = send_grads(
        total_tokens, order, student_out, matched, sums, swap_cores(sums), scale, sent_mix
    )
    kept = keep_grads(held, kept_mix)
    student_tokens = join_columns(which, tokens_own, swap_cores(tokens_other))
    passed = lax.optimization_barrier((from_z_previous(sent[0]), from_z_next(sent[1]), from_x_twin(sent[2])))
    by_chip = lax.all_to_all(
        add_passed(kept, passed), ("xlo", "y", "xhi"), 0, 0, axis_index_groups=FSDP_GROUPS
    )
    by_chip, student_tokens = lax.optimization_barrier((by_chip, student_tokens))
    total = jnp.sum(by_chip.astype(jnp.float32), axis=0).astype(jnp.bfloat16)
    by_copy = lax.all_to_all(
        total.reshape(8, 16, half), ("z", "xlo"), 0, 0, axis_index_groups=DP_GROUPS
    )
    copy_rows = jnp.sum(by_copy.astype(jnp.float32), axis=0).astype(jnp.bfloat16)
    full = lax.all_to_all(jnp.broadcast_to(copy_rows[None], (16, 16, half)), ("z", "xlo"), 0, 0)
    flip = ((core + xhi) & 1).astype(jnp.int32).reshape(1)
    weight_next, teacher_next, first_next, squares_next = adamw_update(
        flip, full.reshape(8, 2, 16, half), student_weight, teacher_weight, moment, second
    )
    return (weight_next, teacher_next, first_next, squares_next, student_tokens)


def solution(mesh):
    split = Mesh(mesh.devices.reshape(8, 2, 4, 2, 2), AXES)
    tokens = P(AXES, None)
    owned = P(("y", "xhi", "core"), None)
    return jax.shard_map(
        shards,
        mesh=split,
        in_specs=(tokens, tokens, tokens, tokens, P(), owned, owned, owned, owned),
        out_specs=(owned, owned, owned, owned, tokens),
        check_vma=False,
    )
```

```python
import functools

import jax
import jax.numpy as jnp
from jax import lax
from jax.experimental import pallas as pl
from jax.experimental.pallas import tpu as pltpu
from jax.sharding import Mesh, PartitionSpec as P

KIN = 2048
DOUT = 2048
PATCHES = 144
EPS = 1e-06
AXES = ("z", "xlo", "y", "xhi", "core")
VMEM_LIMIT = 32 * 1024 * 1024

X_INDEX = (0, 2, 1, 3)
CORE_SWAP = ((0, 1), (1, 0))
X_NEAR = tuple((X_INDEX[a], X_INDEX[b]) for a, b in ((1, 2), (2, 1), (0, 3), (3, 0)))


def from_next(size):
    return tuple(((i + 1) % size, i) for i in range(size))


def from_previous(size):
    return tuple((i, (i + 1) % size) for i in range(size))


def with_core_flip(pairs):
    return tuple((2 * a + 1 - core, 2 * b + core) for a, b in pairs for core in range(2))


FSDP_GROUPS = tuple(
    tuple((xhi ^ side) * 8 + y * 2 + xhi for y in range(4) for xhi in range(2)) for side in range(2)
)
DP_GROUPS = tuple(tuple(z * 2 + ((z + side) & 1) for z in range(8)) for side in range(2))


def swap_cores(value):
    return lax.ppermute(value, "core", CORE_SWAP)


def from_y_next(value):
    return lax.ppermute(value, "y", from_next(4))


def from_y_previous(value):
    return lax.ppermute(value, "y", from_previous(4))


def from_x_near(value):
    return lax.ppermute(value, ("xlo", "xhi"), X_NEAR)


def from_z_next(value):
    return lax.ppermute(value, ("z", "core"), with_core_flip(from_next(8)))


def from_z_previous(value):
    return lax.ppermute(value, ("z", "core"), with_core_flip(from_previous(8)))


def from_x_twin(value):
    return lax.ppermute(value, ("xlo", "core"), with_core_flip(CORE_SWAP))


ORDER = (
    (0, 0, 0), (0, 1, 0), (0, 3, 0), (0, 0, 1), (0, 2, 0), (0, 3, 1), (0, 1, 1), (1, 1, 0), (1, 3, 0), (0, 2, 1),
    (1, 2, 0), (1, 1, 1), (1, 3, 1), (1, 0, 1), (1, 0, 0), (1, 2, 1),
)
EARLY = 14
LATE = len(ORDER) - EARLY
HALF_AT = len(ORDER)
CORE_AT = HALF_AT + 1
SENT = (3, 3, 2)
PARTS = 2


def place_blocks(order, step, packed, early, late):
    for part in range(2):
        columns = slice(part * 128, (part + 1) * 128)
        for block in range(len(ORDER)):
            @pl.when(order[block] == 2 * step + part)
            def _():
                if block < EARLY:
                    early[:, block * 128 : (block + 1) * 128] = packed[:, columns]
                else:
                    late[:, (block - EARLY) * 128 : (block - EARLY + 1) * 128] = packed[:, columns]


def student_kernel(order, mix_own, mix_other, early, late, sent_out, kept_out, turned, packed):
    own = mix_own.shape[0]
    packed[:own, :] = mix_own[...]
    packed[own:, :] = mix_other[...]
    turned[...] = packed[...].T
    core = order[CORE_AT]
    kept_out[0] = turned[pl.ds(pl.multiple_of(core * 128, 128), 128), :]
    sent_out[0] = turned[pl.ds(pl.multiple_of((1 - core) * 128, 128), 128), :]
    place_blocks(order, pl.program_id(0), packed, early, late)


def teacher_kernel(
    order, mix_own, mix_other, residual, places_own, places_other, early, late, picked_out, packed, picks
):
    own, step = mix_own.shape[0], pl.program_id(0)
    crops = own // PATCHES

    @pl.when(step == 0)
    def _():
        lane = lax.broadcasted_iota(jnp.int32, (PATCHES, PATCHES), 1)
        for side, places in enumerate((places_own, places_other)):
            for crop in range(crops):
                rows = slice(crop * PATCHES, (crop + 1) * PATCHES)
                picks[side * crops + crop] = (places[rows, :] == lane).astype(jnp.float32).astype(jnp.bfloat16)

    for side, mix in enumerate((mix_own, mix_other)):
        for crop in range(crops):
            rows = slice(crop * PATCHES, (crop + 1) * PATCHES)
            at = side * crops + crop
            packed[at * PATCHES : (at + 1) * PATCHES, :] = jnp.dot(
                picks[at], mix[rows, :], preferred_element_type=jnp.float32
            ).astype(jnp.bfloat16)
            if side == 0:
                picked_out[rows, :] = jnp.dot(
                    picks[at], residual[rows, :], preferred_element_type=jnp.float32
                ).astype(jnp.bfloat16)
    place_blocks(order, step, packed, early, late)


def prepare_student(order, mix_own, mix_other):
    own, steps = mix_own.shape[0], 8
    rows, width = 2 * own, KIN // steps
    mix = pl.BlockSpec((own, width), lambda i, order: (0, i))
    turned = pl.BlockSpec((1, 128, rows), lambda i, order: (i, 0, 0))
    return pl.pallas_call(
        student_kernel,
        grid_spec=pltpu.PrefetchScalarGridSpec(
            num_scalar_prefetch=1,
            grid=(steps,),
            in_specs=[mix] * 2,
            out_specs=[
                pl.BlockSpec((rows, EARLY * 128), lambda i, order: (0, 0)),
                pl.BlockSpec((rows, LATE * 128), lambda i, order: (0, 0)),
                turned,
                turned,
            ],
            scratch_shapes=[pltpu.VMEM((width, rows), jnp.bfloat16), pltpu.VMEM((rows, width), jnp.bfloat16)],
        ),
        out_shape=[
            jax.ShapeDtypeStruct((rows, EARLY * 128), jnp.bfloat16),
            jax.ShapeDtypeStruct((rows, LATE * 128), jnp.bfloat16),
            jax.ShapeDtypeStruct((8, 128, rows), jnp.bfloat16),
            jax.ShapeDtypeStruct((8, 128, rows), jnp.bfloat16),
        ],
        compiler_params=pltpu.CompilerParams(vmem_limit_bytes=VMEM_LIMIT),
        cost_estimate=pl.CostEstimate(flops=0, bytes_accessed=7 * 1024 * 1024, transcendentals=0),
    )(order, mix_own, mix_other)


def prepare_teacher(order, mix_own, mix_other, residual, places, places_other):
    own, steps = mix_own.shape[0], 8
    rows, width = 2 * own, KIN // steps
    mix = pl.BlockSpec((own, width), lambda i, order: (0, i))
    place = pl.BlockSpec((own, 1), lambda i, order: (0, 0))
    return pl.pallas_call(
        teacher_kernel,
        grid_spec=pltpu.PrefetchScalarGridSpec(
            num_scalar_prefetch=1,
            grid=(steps,),
            in_specs=[mix] * 3 + [place] * 2,
            out_specs=[
                pl.BlockSpec((rows, EARLY * 128), lambda i, order: (0, 0)),
                pl.BlockSpec((rows, LATE * 128), lambda i, order: (0, 0)),
                mix,
            ],
            scratch_shapes=[
                pltpu.VMEM((rows, width), jnp.bfloat16),
                pltpu.VMEM((rows // PATCHES, PATCHES, PATCHES), jnp.bfloat16),
            ],
        ),
        out_shape=[
            jax.ShapeDtypeStruct((rows, EARLY * 128), jnp.bfloat16),
            jax.ShapeDtypeStruct((rows, LATE * 128), jnp.bfloat16),
            jax.ShapeDtypeStruct((own, DOUT), jnp.bfloat16),
        ],
        compiler_params=pltpu.CompilerParams(vmem_limit_bytes=VMEM_LIMIT),
        cost_estimate=pl.CostEstimate(
            flops=3 * rows * PATCHES * KIN, bytes_accessed=9 * 1024 * 1024, transcendentals=0
        ),
    )(order, mix_own, mix_other, residual, places, places_other)


def early_kernel(student_mix, teacher_mix, *refs):
    weights, (student_out, teacher_out, held) = refs[:EARLY], refs[EARLY:]
    for block in range(EARLY):
        rows = slice(block * 128, (block + 1) * 128)
        held[0, rows, :] = weights[block][0]
        held[1, rows, :] = weights[block][1]
    student_out[...] = jnp.dot(student_mix[...], held[0], preferred_element_type=jnp.float32)
    teacher_out[...] = jnp.dot(teacher_mix[...], held[1], preferred_element_type=jnp.float32)


def early_forward(pieces, student_mix, teacher_mix):
    rows, depth = student_mix.shape
    columns, width = pieces[0].shape[-1], 256
    whole = pl.BlockSpec((rows, depth), lambda j: (0, 0))
    column = pl.BlockSpec((rows, width), lambda j: (0, j))
    return pl.pallas_call(
        early_kernel,
        grid=(columns // width,),
        in_specs=[whole, whole] + [pl.BlockSpec((2, 128, width), lambda j: (0, 0, j))] * EARLY,
        out_specs=[column, column],
        out_shape=[jax.ShapeDtypeStruct((rows, columns), jnp.float32)] * 2,
        scratch_shapes=[pltpu.VMEM((2, depth, width), jnp.bfloat16)],
        compiler_params=pltpu.CompilerParams(vmem_limit_bytes=VMEM_LIMIT),
        cost_estimate=pl.CostEstimate(
            flops=4 * rows * depth * columns, bytes_accessed=17 * 1024 * 1024, transcendentals=0
        ),
    )(student_mix, teacher_mix, *pieces)


def late_kernel(
    order, student_mix, teacher_mix, student_part, teacher_part, residual_own, residual_other, picked_own, picked_other,
    scale, *refs
):
    weights, (student_out, matched_out, sums_out, held) = refs[:LATE], refs[LATE:]
    for block in range(LATE):
        rows = slice(block * 128, (block + 1) * 128)
        held[0, rows, :] = weights[block][0]
        held[1, rows, :] = weights[block][1]
    factor = scale[...] * (KIN ** (-0.5))
    student_sum = student_part[...] + jnp.dot(student_mix[...], held[0], preferred_element_type=jnp.float32)
    teacher_sum = teacher_part[...] + jnp.dot(teacher_mix[...], held[1], preferred_element_type=jnp.float32)
    own = residual_own.shape[0]
    first = pl.program_id(0) == 0
    for side, (residual, picked) in enumerate(((residual_own, picked_own), (residual_other, picked_other))):
        tokens = slice(side * own, (side + 1) * own)
        student = residual[...].astype(jnp.float32) + factor * student_sum[tokens]
        matched = picked[...].astype(jnp.float32) + factor * teacher_sum[tokens]
        student_out[tokens, :] = student
        matched_out[tokens, :] = matched
        spot = lax.broadcasted_iota(jnp.int32, (own, 128), 1)
        sums = jnp.where(
            spot == 0,
            jnp.sum(student * student, axis=-1, keepdims=True),
            jnp.where(
                spot == 1,
                jnp.sum(matched * matched, axis=-1, keepdims=True),
                jnp.where(spot == 2, jnp.sum(student * matched, axis=-1, keepdims=True), 0.0),
            ),
        )
        sums_out[tokens, :] = sums + jnp.where(first, 0.0, sums_out[tokens, :])


def late_forward(
    order, pieces, student_mix, teacher_mix, student_part, teacher_part, residual, residual_other, picked, picked_other,
    scale
):
    (rows, columns), own, width = student_part.shape, residual.shape[0], 256
    steps = columns // width
    whole = pl.BlockSpec((rows, LATE * 128), lambda j, order: (0, 0))
    column = pl.BlockSpec((rows, width), lambda j, order: (0, j))
    tokens = pl.BlockSpec((own, width), lambda j, order: (0, order[HALF_AT] * steps + j))
    return pl.pallas_call(
        late_kernel,
        grid_spec=pltpu.PrefetchScalarGridSpec(
            num_scalar_prefetch=1,
            grid=(steps,),
            in_specs=[whole, whole, column, column]
            + [tokens] * 4
            + [pl.BlockSpec((1, width), lambda j, order: (0, order[HALF_AT] * steps + j))]
            + [pl.BlockSpec((2, 128, width), lambda j, order: (0, 0, j))] * LATE,
            out_specs=[column, column, pl.BlockSpec((rows, 128), lambda j, order: (0, 0))],
            scratch_shapes=[pltpu.VMEM((2, LATE * 128, width), jnp.bfloat16)],
        ),
        out_shape=[
            jax.ShapeDtypeStruct((rows, columns), jnp.float32),
            jax.ShapeDtypeStruct((rows, columns), jnp.float32),
            jax.ShapeDtypeStruct((rows, 128), jnp.float32),
        ],
        compiler_params=pltpu.CompilerParams(vmem_limit_bytes=VMEM_LIMIT),
        cost_estimate=pl.CostEstimate(
            flops=4 * rows * LATE * 128 * columns, bytes_accessed=13 * 1024 * 1024, transcendentals=0
        ),
    )(
        order, student_mix, teacher_mix, student_part, teacher_part, residual, residual_other, picked, picked_other,
        scale, *pieces
    )


def send_kernel(
    total_tokens, order, student, matched, sums, more_sums, scale, mix, next_out, previous_out, twin_out, held_out,
    tokens_own, tokens_other
):
    own = more_sums.shape[0] // 2
    swapped = jnp.concatenate([more_sums[own:, :], more_sums[:own, :]], axis=0)
    total = (sums[...] + swapped) * (1.0 / DOUT)
    inverse_rms = lax.rsqrt(total[:, 0:1] + EPS)
    inverse_matched = lax.rsqrt(total[:, 1:2] + EPS)
    overlap = inverse_rms * inverse_matched * total[:, 2:3]
    shared = inverse_rms * (1.0 / total_tokens)
    student_part = shared * inverse_rms * (EPS * inverse_rms * inverse_rms + overlap)
    matched_part = shared * inverse_matched
    values = student[...]
    tokens = (values * inverse_rms).astype(jnp.bfloat16)
    tokens_own[...] = tokens[:own]
    tokens_other[...] = tokens[own:]
    factor = scale[...] * (KIN ** (-0.5))
    held_out[...] = (factor * (values * student_part - matched[...] * matched_part)).astype(jnp.bfloat16)
    at = 0
    for out in (next_out, previous_out, twin_out):
        count = out.shape[0]
        grad = jnp.dot(
            mix[at : at + count].reshape(count * 128, mix.shape[-1]),
            held_out[...],
            preferred_element_type=jnp.float32,
        )
        out[...] = grad.astype(jnp.bfloat16).reshape(out.shape)
        at += count


def send_grads(total_tokens, part, order, student, matched, sums, more_sums, scale, turned):
    (rows, columns), width = student.shape, 256
    steps = columns // width
    count = steps // PARTS
    column = pl.BlockSpec((rows, width), lambda j, order: (0, part * count + j))
    narrow = pl.BlockSpec((rows, 128), lambda j, order: (0, 0))
    out = pl.BlockSpec((rows, width), lambda j, order: (0, j))
    half = pl.BlockSpec((rows // 2, width), lambda j, order: (0, j))
    return pl.pallas_call(
        functools.partial(send_kernel, total_tokens),
        grid_spec=pltpu.PrefetchScalarGridSpec(
            num_scalar_prefetch=1,
            grid=(count,),
            in_specs=[
                column,
                column,
                narrow,
                narrow,
                pl.BlockSpec((1, width), lambda j, order: (0, order[HALF_AT] * steps + part * count + j)),
                pl.BlockSpec((8, 128, rows), lambda j, order: (0, 0, 0)),
            ],
            out_specs=[pl.BlockSpec((size, 128, width), lambda j, order: (0, 0, j)) for size in SENT]
            + [out, half, half],
        ),
        out_shape=[jax.ShapeDtypeStruct((size, 128, columns // PARTS), jnp.bfloat16) for size in SENT]
        + [
            jax.ShapeDtypeStruct((rows, columns // PARTS), jnp.bfloat16),
            jax.ShapeDtypeStruct((rows // 2, columns // PARTS), jnp.bfloat16),
            jax.ShapeDtypeStruct((rows // 2, columns // PARTS), jnp.bfloat16),
        ],
        compiler_params=pltpu.CompilerParams(vmem_limit_bytes=VMEM_LIMIT),
        cost_estimate=pl.CostEstimate(
            flops=rows * KIN * columns // PARTS, bytes_accessed=6 * 1024 * 1024, transcendentals=0
        ),
    )(order, student, matched, sums, more_sums, scale, turned)


def keep_kernel(held, mix, out):
    grad = jnp.dot(
        mix[...].reshape(8 * 128, mix.shape[-1]), held[...], preferred_element_type=jnp.float32
    )
    out[...] = grad.reshape(out.shape)


def keep_grads(held, kept):
    (rows, columns), width = held.shape, 256
    return pl.pallas_call(
        keep_kernel,
        grid=(columns // width,),
        in_specs=[
            pl.BlockSpec((rows, width), lambda j: (0, j)),
            pl.BlockSpec((8, 128, rows), lambda j: (0, 0, 0)),
        ],
        out_specs=pl.BlockSpec((8, 128, width), lambda j: (0, 0, j)),
        out_shape=jax.ShapeDtypeStruct((8, 128, columns), jnp.float32),
        compiler_params=pltpu.CompilerParams(vmem_limit_bytes=VMEM_LIMIT),
        cost_estimate=pl.CostEstimate(
            flops=rows * KIN * columns, bytes_accessed=7 * 1024 * 1024, transcendentals=0
        ),
    )(held, kept)


def add_kernel(kept, *refs):
    passed, out = refs[:-1], refs[-1]
    at = 0
    for part in passed:
        spot = slice(at, at + part.shape[0])
        out[spot] = (kept[spot] + part[...].astype(jnp.float32)).astype(jnp.bfloat16)
        at += part.shape[0]


def add_passed(kept, passed):
    width = 256

    def blocks(count):
        return pl.BlockSpec((count, 128, width), lambda j: (0, 0, j))

    return pl.pallas_call(
        add_kernel,
        grid=(kept.shape[-1] // width,),
        in_specs=[blocks(8)] + [blocks(count) for count in SENT],
        out_specs=blocks(8),
        out_shape=jax.ShapeDtypeStruct(kept.shape, jnp.bfloat16),
        compiler_params=pltpu.CompilerParams(vmem_limit_bytes=VMEM_LIMIT),
    )(kept, *passed)


def update_kernel(flip, grads, weight, teacher, first, squares, weight_out, teacher_out, first_out, squares_out):
    rows = []
    for index in range(grads.shape[0]):
        swap = ((flip[0] + index) & 1) == 1
        left = jnp.where(swap, grads[index, 1], grads[index, 0])
        right = jnp.where(swap, grads[index, 0], grads[index, 1])
        rows.append(jnp.concatenate([left, right], axis=1))
    grad = jnp.concatenate(rows, axis=0).astype(jnp.float32)
    first_next = 0.9 * first[...] + 0.1 * grad
    squares_next = 0.95 * squares[...] + 0.05 * grad * grad
    held = weight[...]
    weight_next = held - 0.1 * (first_next / (jnp.sqrt(squares_next) + 1e-08) + 0.04 * held)
    weight_out[...] = weight_next
    teacher_out[...] = 0.96 * teacher[...] + 0.04 * weight_next
    first_out[...] = first_next
    squares_out[...] = squares_next


def adamw_update(flip, grads, weight, teacher, first, squares):
    rows = pl.BlockSpec((32, DOUT), lambda i, flip: (i, 0))
    return pl.pallas_call(
        update_kernel,
        grid_spec=pltpu.PrefetchScalarGridSpec(
            num_scalar_prefetch=1,
            grid=(4,),
            in_specs=[pl.BlockSpec((2, 2, 16, DOUT // 2), lambda i, flip: (i, 0, 0, 0))] + [rows] * 4,
            out_specs=[rows] * 4,
        ),
        out_shape=[jax.ShapeDtypeStruct(weight.shape, jnp.float32)] * 4,
        compiler_params=pltpu.CompilerParams(vmem_limit_bytes=VMEM_LIMIT),
    )(flip, grads, weight, teacher, first, squares)


def join_columns(which, own, other):
    return jnp.where(
        which == 0, jnp.concatenate([own, other], axis=-1), jnp.concatenate([other, own], axis=-1)
    )


def shards(
    residual,
    student_mix,
    teacher_mix,
    positions,
    layer_scale,
    student_weight,
    teacher_weight,
    moment,
    second,
):
    half = DOUT // 2
    token_count = student_mix.shape[0]
    total_tokens = token_count * 256
    z, xlo, y, xhi, core = (lax.axis_index(name) for name in AXES)
    which = (core + z + xhi + xlo) & 1

    def columns_of(value, index):
        return lax.dynamic_slice_in_dim(value, index * half, half, axis=-1)

    def both_weights(index):
        return jnp.stack([columns_of(student_weight, index), columns_of(teacher_weight, index)]).astype(jnp.bfloat16)

    own = both_weights(which)
    order = jnp.stack(
        [(((y + dy) & 3) * 2 + (xhi ^ dx)) * 2 + (core ^ side) for side, dy, dx in ORDER] + [which, core]
    ).astype(jnp.int32)
    scale = layer_scale.reshape(1, DOUT)

    own, student_sent, teacher_sent, positions_sent, student_held, teacher_held, residual = lax.optimization_barrier(
        (own, student_mix, teacher_mix, positions, student_weight, teacher_weight, residual)
    )
    student_weight, teacher_weight = student_held, teacher_held
    student_other, positions_sent = lax.optimization_barrier((swap_cores(student_sent), positions_sent))
    teacher_other, places_other = swap_cores(teacher_sent), swap_cores(positions_sent)
    up, down, across, student_other, teacher_other, places, places_other, student_held, teacher_held = (
        lax.optimization_barrier(
            (
                from_y_next(own), from_y_previous(own), from_x_near(own), student_other, teacher_other, positions,
                places_other, student_held, teacher_held,
            )
        )
    )
    other_sent = jnp.stack(
        [columns_of(student_held, 1 - which), columns_of(teacher_held, 1 - which)]
    ).astype(jnp.bfloat16)
    student_prepared = prepare_student(order, student_mix, student_other)
    (
        up_two, across_down, across_up, passed_up, passed_down, across, other_sent, places, places_other,
        student_prepared, teacher_other, residual,
    ) = lax.optimization_barrier(
        (
            from_y_next(up), from_y_previous(across), from_x_near(up), from_z_next(up), from_z_previous(down), across,
            other_sent, places.reshape(token_count, 1), places_other.reshape(token_count, 1), student_prepared,
            teacher_other, residual,
        )
    )
    prepared = prepare_teacher(order, teacher_mix, teacher_other, residual, places, places_other)
    (
        across_two, passed_two, passed_across_up, passed_across_down, passed_across, prepared, other_sent, residual_sent
    ) = lax.optimization_barrier(
        (
            from_y_next(across_up), from_z_next(up_two), from_z_previous(across_up), from_x_near(passed_down),
            from_x_twin(across), prepared, other_sent, residual,
        )
    )
    student_early, student_late, sent_mix, kept_mix = student_prepared
    teacher_early, teacher_late, picked = prepared
    passed_across_two = from_z_next(across_two)
    residual_other, picked_other, other = swap_cores(residual_sent), swap_cores(picked), swap_cores(other_sent)
    student_part, teacher_part = early_forward(
        (
            own, up, down, across, up_two, across_down, across_up, passed_up, passed_down, across_two, passed_two,
            passed_across_up, passed_across_down, passed_across,
        ),
        student_early,
        teacher_early,
    )
    student_out, matched, sums = late_forward(
        order, (other, passed_across_two), student_late, teacher_late, student_part, teacher_part, residual,
        residual_other, picked, picked_other, scale
    )
    more_sums = swap_cores(sums)

    def to_neighbours(part, after):
        part_sums, after = lax.optimization_barrier((sums, after))
        *sent, held, tokens_own, tokens_other = send_grads(
            total_tokens, part, order, student_out, matched, part_sums, more_sums, scale, sent_mix
        )
        passed = (from_z_previous(sent[0]), from_z_next(sent[1]), from_x_twin(sent[2]))
        return sent, held, tokens_own, tokens_other, passed

    def over_fsdp(rows):
        return lax.all_to_all(rows, ("xlo", "y", "xhi"), 0, 0, axis_index_groups=FSDP_GROUPS)

    sent, first_held, first_own, first_other, first_passed = to_neighbours(0, more_sums)
    _, last_held, last_own, last_other, last_passed = to_neighbours(1, sent)
    first_kept, last_kept = keep_grads(first_held, kept_mix), keep_grads(last_held, kept_mix)
    first_passed, last_kept, last_other = lax.optimization_barrier((first_passed, last_kept, last_other))
    first_rows, last_kept, last_other = lax.optimization_barrier(
        (add_passed(first_kept, first_passed), last_kept, last_other)
    )
    swapped = swap_cores(jnp.concatenate([first_other, last_other], axis=1))
    tokens_own = jnp.concatenate([first_own, last_own], axis=1)
    first_chip, last_rows = lax.optimization_barrier((over_fsdp(first_rows), add_passed(last_kept, last_passed)))
    last_chip = over_fsdp(last_rows)
    student_tokens = join_columns(which, tokens_own, swapped)
    first_chip, last_chip, student_tokens = lax.optimization_barrier((first_chip, last_chip, student_tokens))
    total = jnp.concatenate(
        [jnp.sum(chip.astype(jnp.float32), axis=0).astype(jnp.bfloat16) for chip in (first_chip, last_chip)], axis=1
    )
    by_copy = lax.all_to_all(
        total.reshape(8, 16, half), ("z", "xlo"), 0, 0, axis_index_groups=DP_GROUPS
    )
    copy_rows = jnp.sum(by_copy.astype(jnp.float32), axis=0).astype(jnp.bfloat16)
    full = lax.all_to_all(jnp.broadcast_to(copy_rows[None], (16, 16, half)), ("z", "xlo"), 0, 0)
    flip = ((core + xhi) & 1).astype(jnp.int32).reshape(1)
    weight_next, teacher_next, first_next, squares_next = adamw_update(
        flip, full.reshape(8, 2, 16, half), student_weight, teacher_weight, moment, second
    )
    return (weight_next, teacher_next, first_next, squares_next, student_tokens)


def solution(mesh):
    split = Mesh(mesh.devices.reshape(8, 2, 4, 2, 2), AXES)
    tokens = P(AXES, None)
    owned = P(("y", "xhi", "core"), None)
    return jax.shard_map(
        shards,
        mesh=split,
        in_specs=(tokens, tokens, tokens, tokens, P(), owned, owned, owned, owned),
        out_specs=(owned, owned, owned, owned, tokens),
        check_vma=False,
    )
```

```python
import functools

import jax
import jax.numpy as jnp
from jax import lax
from jax.experimental import pallas as pl
from jax.experimental.pallas import tpu as pltpu
from jax.sharding import Mesh, PartitionSpec as P

KIN = 2048
DOUT = 2048
PATCHES = 144
EPS = 1e-06
AXES = ("z", "xlo", "y", "xhi", "core")
VMEM_LIMIT = 32 * 1024 * 1024
SMALL_LIMIT = 16 * 1024 * 1024

X_INDEX = (0, 2, 1, 3)
CORE_SWAP = ((0, 1), (1, 0))
X_NEAR = tuple((X_INDEX[a], X_INDEX[b]) for a, b in ((1, 2), (2, 1), (0, 3), (3, 0)))


def from_next(size):
    return tuple(((i + 1) % size, i) for i in range(size))


def from_previous(size):
    return tuple((i, (i + 1) % size) for i in range(size))


def with_core_flip(pairs):
    return tuple((2 * a + 1 - core, 2 * b + core) for a, b in pairs for core in range(2))


FSDP_GROUPS = tuple(
    tuple((xhi ^ side) * 8 + y * 2 + xhi for y in range(4) for xhi in range(2)) for side in range(2)
)
DP_GROUPS = tuple(tuple(z * 2 + ((z + side) & 1) for z in range(8)) for side in range(2))


def swap_cores(value):
    return lax.ppermute(value, "core", CORE_SWAP)


def from_y_next(value):
    return lax.ppermute(value, "y", from_next(4))


def from_y_previous(value):
    return lax.ppermute(value, "y", from_previous(4))


def from_x_near(value):
    return lax.ppermute(value, ("xlo", "xhi"), X_NEAR)


def from_z_next(value):
    return lax.ppermute(value, ("z", "core"), with_core_flip(from_next(8)))


def from_z_previous(value):
    return lax.ppermute(value, ("z", "core"), with_core_flip(from_previous(8)))


def from_x_twin(value):
    return lax.ppermute(value, ("xlo", "core"), with_core_flip(CORE_SWAP))


ORDER = (
    (0, 0, 0), (0, 1, 0), (0, 3, 0), (0, 0, 1), (0, 2, 0), (0, 3, 1), (0, 1, 1), (1, 1, 0), (1, 3, 0), (0, 2, 1),
    (1, 2, 0), (1, 1, 1), (1, 3, 1), (1, 0, 1), (1, 0, 0), (1, 2, 1),
)
EARLY = 14
LATE = len(ORDER) - EARLY
HALF_AT = len(ORDER)
CORE_AT = HALF_AT + 1
SENT = (3, 3, 2)
PARTS = 2


def split_kernel(order, student, teacher, out):
    out[0] = student[...].astype(jnp.bfloat16)
    out[1] = teacher[...].astype(jnp.bfloat16)


def split_weights(order, student, teacher):
    rows, width, steps = student.shape[0], 512, 2

    def half(j, order):
        return (0, (order[HALF_AT] ^ 1) * steps + j)

    return pl.pallas_call(
        split_kernel,
        grid_spec=pltpu.PrefetchScalarGridSpec(
            num_scalar_prefetch=1,
            grid=(steps,),
            in_specs=[pl.BlockSpec((rows, width), half)] * 2,
            out_specs=pl.BlockSpec((2, rows, width), lambda j, order: (0, 0, j)),
        ),
        out_shape=jax.ShapeDtypeStruct((2, rows, width * steps), jnp.bfloat16),
        compiler_params=pltpu.CompilerParams(vmem_limit_bytes=SMALL_LIMIT),
        cost_estimate=pl.CostEstimate(flops=0, bytes_accessed=1536 * 1024, transcendentals=0),
    )(order, student, teacher)


def place_blocks(order, step, packed, early, late):
    for part in range(2):
        columns = slice(part * 128, (part + 1) * 128)
        for block in range(len(ORDER)):
            @pl.when(order[block] == 2 * step + part)
            def _():
                if block < EARLY:
                    early[:, block * 128 : (block + 1) * 128] = packed[:, columns]
                else:
                    late[:, (block - EARLY) * 128 : (block - EARLY + 1) * 128] = packed[:, columns]


def student_kernel(order, mix_own, mix_other, early, late, sent_out, kept_out, turned, packed):
    own = mix_own.shape[0]
    packed[:own, :] = mix_own[...]
    packed[own:, :] = mix_other[...]
    turned[...] = packed[...].T
    core = order[CORE_AT]
    kept_out[0] = turned[pl.ds(pl.multiple_of(core * 128, 128), 128), :]
    sent_out[0] = turned[pl.ds(pl.multiple_of((1 - core) * 128, 128), 128), :]
    place_blocks(order, pl.program_id(0), packed, early, late)


def teacher_kernel(
    order, mix_own, mix_other, residual, places_own, places_other, early, late, picked_out, packed, picks
):
    own, step = mix_own.shape[0], pl.program_id(0)
    crops = own // PATCHES

    @pl.when(step == 0)
    def _():
        source = lax.broadcasted_iota(jnp.int32, (PATCHES, PATCHES), 0)
        for side, places in enumerate((places_own, places_other)):
            for crop in range(crops):
                chosen = jnp.where(places[crop : crop + 1, :] == source, 1.0, 0.0)
                picks[side * crops + crop] = chosen.T.astype(jnp.bfloat16)

    for side, mix in enumerate((mix_own, mix_other)):
        for crop in range(crops):
            rows = slice(crop * PATCHES, (crop + 1) * PATCHES)
            at = side * crops + crop
            packed[at * PATCHES : (at + 1) * PATCHES, :] = jnp.dot(
                picks[at], mix[rows, :], preferred_element_type=jnp.float32
            ).astype(jnp.bfloat16)
            if side == 0:
                picked_out[rows, :] = jnp.dot(
                    picks[at], residual[rows, :], preferred_element_type=jnp.float32
                ).astype(jnp.bfloat16)
    place_blocks(order, step, packed, early, late)


def prepare_student(order, mix_own, mix_other):
    own, steps = mix_own.shape[0], 8
    rows, width = 2 * own, KIN // steps
    mix = pl.BlockSpec((own, width), lambda i, order: (0, i))
    turned = pl.BlockSpec((1, 128, rows), lambda i, order: (i, 0, 0))
    return pl.pallas_call(
        student_kernel,
        grid_spec=pltpu.PrefetchScalarGridSpec(
            num_scalar_prefetch=1,
            grid=(steps,),
            in_specs=[mix] * 2,
            out_specs=[
                pl.BlockSpec((rows, EARLY * 128), lambda i, order: (0, 0)),
                pl.BlockSpec((rows, LATE * 128), lambda i, order: (0, 0)),
                turned,
                turned,
            ],
            scratch_shapes=[pltpu.VMEM((width, rows), jnp.bfloat16), pltpu.VMEM((rows, width), jnp.bfloat16)],
        ),
        out_shape=[
            jax.ShapeDtypeStruct((rows, EARLY * 128), jnp.bfloat16),
            jax.ShapeDtypeStruct((rows, LATE * 128), jnp.bfloat16),
            jax.ShapeDtypeStruct((8, 128, rows), jnp.bfloat16),
            jax.ShapeDtypeStruct((8, 128, rows), jnp.bfloat16),
        ],
        compiler_params=pltpu.CompilerParams(vmem_limit_bytes=VMEM_LIMIT),
        cost_estimate=pl.CostEstimate(flops=0, bytes_accessed=7 * 1024 * 1024, transcendentals=0),
    )(order, mix_own, mix_other)


def prepare_teacher(order, mix_own, mix_other, residual, places, places_other):
    own, steps = mix_own.shape[0], 8
    rows, width = 2 * own, KIN // steps
    mix = pl.BlockSpec((own, width), lambda i, order: (0, i))
    place = pl.BlockSpec(places.shape, lambda i, order: (0, 0))
    return pl.pallas_call(
        teacher_kernel,
        grid_spec=pltpu.PrefetchScalarGridSpec(
            num_scalar_prefetch=1,
            grid=(steps,),
            in_specs=[mix] * 3 + [place] * 2,
            out_specs=[
                pl.BlockSpec((rows, EARLY * 128), lambda i, order: (0, 0)),
                pl.BlockSpec((rows, LATE * 128), lambda i, order: (0, 0)),
                mix,
            ],
            scratch_shapes=[
                pltpu.VMEM((rows, width), jnp.bfloat16),
                pltpu.VMEM((rows // PATCHES, PATCHES, PATCHES), jnp.bfloat16),
            ],
        ),
        out_shape=[
            jax.ShapeDtypeStruct((rows, EARLY * 128), jnp.bfloat16),
            jax.ShapeDtypeStruct((rows, LATE * 128), jnp.bfloat16),
            jax.ShapeDtypeStruct((own, DOUT), jnp.bfloat16),
        ],
        compiler_params=pltpu.CompilerParams(vmem_limit_bytes=VMEM_LIMIT),
        cost_estimate=pl.CostEstimate(
            flops=3 * rows * PATCHES * KIN, bytes_accessed=9 * 1024 * 1024, transcendentals=0
        ),
    )(order, mix_own, mix_other, residual, places, places_other)


def early_kernel(student_mix, teacher_mix, *refs):
    weights, (student_out, teacher_out, held) = refs[:EARLY], refs[EARLY:]
    for block in range(EARLY):
        rows = slice(block * 128, (block + 1) * 128)
        held[0, rows, :] = weights[block][0]
        held[1, rows, :] = weights[block][1]
    student_out[...] = jnp.dot(student_mix[...], held[0], preferred_element_type=jnp.float32)
    teacher_out[...] = jnp.dot(teacher_mix[...], held[1], preferred_element_type=jnp.float32)


def early_forward(pieces, student_mix, teacher_mix):
    rows, depth = student_mix.shape
    columns, width = pieces[0].shape[-1], 256
    whole = pl.BlockSpec((rows, depth), lambda j: (0, 0))
    column = pl.BlockSpec((rows, width), lambda j: (0, j))
    return pl.pallas_call(
        early_kernel,
        grid=(columns // width,),
        in_specs=[whole, whole] + [pl.BlockSpec((2, 128, width), lambda j: (0, 0, j))] * EARLY,
        out_specs=[column, column],
        out_shape=[jax.ShapeDtypeStruct((rows, columns), jnp.float32)] * 2,
        scratch_shapes=[pltpu.VMEM((2, depth, width), jnp.bfloat16)],
        compiler_params=pltpu.CompilerParams(vmem_limit_bytes=VMEM_LIMIT),
        cost_estimate=pl.CostEstimate(
            flops=4 * rows * depth * columns, bytes_accessed=17 * 1024 * 1024, transcendentals=0
        ),
    )(student_mix, teacher_mix, *pieces)


def late_kernel(
    order, student_mix, teacher_mix, student_part, teacher_part, residual_own, residual_other, picked_own, picked_other,
    scale, *refs
):
    weights, (student_out, matched_out, sums_out, held) = refs[:LATE], refs[LATE:]
    for block in range(LATE):
        rows = slice(block * 128, (block + 1) * 128)
        held[0, rows, :] = weights[block][0]
        held[1, rows, :] = weights[block][1]
    factor = scale[...] * (KIN ** (-0.5))
    student_sum = student_part[...] + jnp.dot(student_mix[...], held[0], preferred_element_type=jnp.float32)
    teacher_sum = teacher_part[...] + jnp.dot(teacher_mix[...], held[1], preferred_element_type=jnp.float32)
    own = residual_own.shape[0]
    first = pl.program_id(0) == 0
    for side, (residual, picked) in enumerate(((residual_own, picked_own), (residual_other, picked_other))):
        tokens = slice(side * own, (side + 1) * own)
        student = residual[...].astype(jnp.float32) + factor * student_sum[tokens]
        matched = picked[...].astype(jnp.float32) + factor * teacher_sum[tokens]
        student_out[tokens, :] = student
        matched_out[tokens, :] = matched
        spot = lax.broadcasted_iota(jnp.int32, (own, 128), 1)
        sums = jnp.where(
            spot == 0,
            jnp.sum(student * student, axis=-1, keepdims=True),
            jnp.where(
                spot == 1,
                jnp.sum(matched * matched, axis=-1, keepdims=True),
                jnp.where(spot == 2, jnp.sum(student * matched, axis=-1, keepdims=True), 0.0),
            ),
        )
        sums_out[tokens, :] = sums + jnp.where(first, 0.0, sums_out[tokens, :])


def late_forward(
    order, pieces, student_mix, teacher_mix, student_part, teacher_part, residual, residual_other, picked, picked_other,
    scale
):
    (rows, columns), own, width = student_part.shape, residual.shape[0], 256
    steps = columns // width
    whole = pl.BlockSpec((rows, LATE * 128), lambda j, order: (0, 0))
    column = pl.BlockSpec((rows, width), lambda j, order: (0, j))
    tokens = pl.BlockSpec((own, width), lambda j, order: (0, order[HALF_AT] * steps + j))
    return pl.pallas_call(
        late_kernel,
        grid_spec=pltpu.PrefetchScalarGridSpec(
            num_scalar_prefetch=1,
            grid=(steps,),
            in_specs=[whole, whole, column, column]
            + [tokens] * 4
            + [pl.BlockSpec((1, width), lambda j, order: (0, order[HALF_AT] * steps + j))]
            + [pl.BlockSpec((2, 128, width), lambda j, order: (0, 0, j))] * LATE,
            out_specs=[column, column, pl.BlockSpec((rows, 128), lambda j, order: (0, 0))],
            scratch_shapes=[pltpu.VMEM((2, LATE * 128, width), jnp.bfloat16)],
        ),
        out_shape=[
            jax.ShapeDtypeStruct((rows, columns), jnp.float32),
            jax.ShapeDtypeStruct((rows, columns), jnp.float32),
            jax.ShapeDtypeStruct((rows, 128), jnp.float32),
        ],
        compiler_params=pltpu.CompilerParams(vmem_limit_bytes=VMEM_LIMIT),
        cost_estimate=pl.CostEstimate(
            flops=4 * rows * LATE * 128 * columns, bytes_accessed=13 * 1024 * 1024, transcendentals=0
        ),
    )(
        order, student_mix, teacher_mix, student_part, teacher_part, residual, residual_other, picked, picked_other,
        scale, *pieces
    )


def send_kernel(
    total_tokens, order, student, matched, sums, more_sums, scale, mix, next_out, previous_out, twin_out, held_out,
    tokens_own, tokens_other
):
    own = more_sums.shape[0] // 2
    swapped = jnp.concatenate([more_sums[own:, :], more_sums[:own, :]], axis=0)
    total = (sums[...] + swapped) * (1.0 / DOUT)
    inverse_rms = lax.rsqrt(total[:, 0:1] + EPS)
    inverse_matched = lax.rsqrt(total[:, 1:2] + EPS)
    overlap = inverse_rms * inverse_matched * total[:, 2:3]
    shared = inverse_rms * (1.0 / total_tokens)
    student_part = shared * inverse_rms * (EPS * inverse_rms * inverse_rms + overlap)
    matched_part = shared * inverse_matched
    values = student[...]
    tokens = (values * inverse_rms).astype(jnp.bfloat16)
    tokens_own[...] = tokens[:own]
    tokens_other[...] = tokens[own:]
    factor = scale[...] * (KIN ** (-0.5))
    held_out[...] = (factor * (values * student_part - matched[...] * matched_part)).astype(jnp.bfloat16)
    at = 0
    for out in (next_out, previous_out, twin_out):
        count = out.shape[0]
        grad = jnp.dot(
            mix[at : at + count].reshape(count * 128, mix.shape[-1]),
            held_out[...],
            preferred_element_type=jnp.float32,
        )
        out[...] = grad.astype(jnp.bfloat16).reshape(out.shape)
        at += count


def send_grads(total_tokens, part, order, student, matched, sums, more_sums, scale, turned):
    (rows, columns), width = student.shape, 256
    steps = columns // width
    count = steps // PARTS
    column = pl.BlockSpec((rows, width), lambda j, order: (0, part * count + j))
    narrow = pl.BlockSpec((rows, 128), lambda j, order: (0, 0))
    out = pl.BlockSpec((rows, width), lambda j, order: (0, j))
    half = pl.BlockSpec((rows // 2, width), lambda j, order: (0, j))
    return pl.pallas_call(
        functools.partial(send_kernel, total_tokens),
        grid_spec=pltpu.PrefetchScalarGridSpec(
            num_scalar_prefetch=1,
            grid=(count,),
            in_specs=[
                column,
                column,
                narrow,
                narrow,
                pl.BlockSpec((1, width), lambda j, order: (0, order[HALF_AT] * steps + part * count + j)),
                pl.BlockSpec((8, 128, rows), lambda j, order: (0, 0, 0)),
            ],
            out_specs=[pl.BlockSpec((size, 128, width), lambda j, order: (0, 0, j)) for size in SENT]
            + [out, half, half],
        ),
        out_shape=[jax.ShapeDtypeStruct((size, 128, columns // PARTS), jnp.bfloat16) for size in SENT]
        + [
            jax.ShapeDtypeStruct((rows, columns // PARTS), jnp.bfloat16),
            jax.ShapeDtypeStruct((rows // 2, columns // PARTS), jnp.bfloat16),
            jax.ShapeDtypeStruct((rows // 2, columns // PARTS), jnp.bfloat16),
        ],
        compiler_params=pltpu.CompilerParams(vmem_limit_bytes=VMEM_LIMIT),
        cost_estimate=pl.CostEstimate(
            flops=rows * KIN * columns // PARTS, bytes_accessed=6 * 1024 * 1024, transcendentals=0
        ),
    )(order, student, matched, sums, more_sums, scale, turned)


def keep_kernel(held, mix, out):
    grad = jnp.dot(
        mix[...].reshape(8 * 128, mix.shape[-1]), held[...], preferred_element_type=jnp.float32
    )
    out[...] = grad.reshape(out.shape)


def keep_grads(held, kept):
    (rows, columns), width = held.shape, 256
    return pl.pallas_call(
        keep_kernel,
        grid=(columns // width,),
        in_specs=[
            pl.BlockSpec((rows, width), lambda j: (0, j)),
            pl.BlockSpec((8, 128, rows), lambda j: (0, 0, 0)),
        ],
        out_specs=pl.BlockSpec((8, 128, width), lambda j: (0, 0, j)),
        out_shape=jax.ShapeDtypeStruct((8, 128, columns), jnp.float32),
        compiler_params=pltpu.CompilerParams(vmem_limit_bytes=VMEM_LIMIT),
        cost_estimate=pl.CostEstimate(
            flops=rows * KIN * columns, bytes_accessed=7 * 1024 * 1024, transcendentals=0
        ),
    )(held, kept)


def add_kernel(kept, *refs):
    passed, out = refs[:-1], refs[-1]
    at = 0
    for part in passed:
        spot = slice(at, at + part.shape[0])
        out[spot] = (kept[spot] + part[...].astype(jnp.float32)).astype(jnp.bfloat16)
        at += part.shape[0]


def add_passed(kept, passed):
    width = 256

    def blocks(count):
        return pl.BlockSpec((count, 128, width), lambda j: (0, 0, j))

    return pl.pallas_call(
        add_kernel,
        grid=(kept.shape[-1] // width,),
        in_specs=[blocks(8)] + [blocks(count) for count in SENT],
        out_specs=blocks(8),
        out_shape=jax.ShapeDtypeStruct(kept.shape, jnp.bfloat16),
        compiler_params=pltpu.CompilerParams(vmem_limit_bytes=VMEM_LIMIT),
    )(kept, *passed)


def join_kernel(order, first_own, last_own, first_other, last_other, out):
    step = pl.program_id(0)
    for at, half in enumerate((first_own, last_own, first_other, last_other)):
        @pl.when(step == (at ^ (2 * order[HALF_AT])))
        def _():
            out[...] = half[...]


def join_tokens(order, *halves):
    rows, width = halves[0].shape
    return pl.pallas_call(
        join_kernel,
        grid_spec=pltpu.PrefetchScalarGridSpec(
            num_scalar_prefetch=1,
            grid=(4,),
            in_specs=[pl.BlockSpec((rows, width), lambda j, order: (0, 0))] * 4,
            out_specs=pl.BlockSpec((rows, width), lambda j, order: (0, j)),
        ),
        out_shape=jax.ShapeDtypeStruct((rows, 4 * width), jnp.bfloat16),
        compiler_params=pltpu.CompilerParams(vmem_limit_bytes=SMALL_LIMIT),
        cost_estimate=pl.CostEstimate(flops=0, bytes_accessed=2400 * 1024, transcendentals=0),
    )(order, *halves)


def total_kernel(first, last, out):
    width = first.shape[-1]
    for at, chips in enumerate((first, last)):
        total = chips[0].astype(jnp.float32)
        for chip in range(1, chips.shape[0]):
            total = total + chips[chip].astype(jnp.float32)
        out[:, at * width : (at + 1) * width] = total.astype(jnp.bfloat16)


def total_rows(first, last):
    chips, rows, width = first.shape
    block = pl.BlockSpec((chips, rows // 2, width), lambda i: (0, i, 0))
    return pl.pallas_call(
        total_kernel,
        grid=(2,),
        in_specs=[block, block],
        out_specs=pl.BlockSpec((rows // 2, 2 * width), lambda i: (i, 0)),
        out_shape=jax.ShapeDtypeStruct((rows, 2 * width), jnp.bfloat16),
        compiler_params=pltpu.CompilerParams(vmem_limit_bytes=SMALL_LIMIT),
        cost_estimate=pl.CostEstimate(flops=0, bytes_accessed=2400 * 1024, transcendentals=0),
    )(first, last)


def spread_kernel(copies, out):
    total = copies[0].astype(jnp.float32)
    for copy in range(1, copies.shape[0]):
        total = total + copies[copy].astype(jnp.float32)
    out[...] = jnp.broadcast_to(total.astype(jnp.bfloat16)[None], out.shape)


def spread_rows(copies, count):
    _, rows, columns = copies.shape
    return pl.pallas_call(
        spread_kernel,
        out_shape=jax.ShapeDtypeStruct((count, rows, columns), jnp.bfloat16),
        compiler_params=pltpu.CompilerParams(vmem_limit_bytes=SMALL_LIMIT),
        cost_estimate=pl.CostEstimate(flops=0, bytes_accessed=800 * 1024, transcendentals=0),
    )(copies)


def update_kernel(flip, grads, weight, teacher, first, squares, weight_out, teacher_out, first_out, squares_out):
    rows = []
    for index in range(grads.shape[0]):
        swap = ((flip[0] + index) & 1) == 1
        left = jnp.where(swap, grads[index, 1], grads[index, 0])
        right = jnp.where(swap, grads[index, 0], grads[index, 1])
        rows.append(jnp.concatenate([left, right], axis=1))
    grad = jnp.concatenate(rows, axis=0).astype(jnp.float32)
    first_next = 0.9 * first[...] + 0.1 * grad
    squares_next = 0.95 * squares[...] + 0.05 * grad * grad
    held = weight[...]
    weight_next = held - 0.1 * (first_next / (jnp.sqrt(squares_next) + 1e-08) + 0.04 * held)
    weight_out[...] = weight_next
    teacher_out[...] = 0.96 * teacher[...] + 0.04 * weight_next
    first_out[...] = first_next
    squares_out[...] = squares_next


def adamw_update(flip, grads, weight, teacher, first, squares):
    rows = pl.BlockSpec((32, DOUT), lambda i, flip: (i, 0))
    return pl.pallas_call(
        update_kernel,
        grid_spec=pltpu.PrefetchScalarGridSpec(
            num_scalar_prefetch=1,
            grid=(4,),
            in_specs=[pl.BlockSpec((2, 2, 16, DOUT // 2), lambda i, flip: (i, 0, 0, 0))] + [rows] * 4,
            out_specs=[rows] * 4,
        ),
        out_shape=[jax.ShapeDtypeStruct(weight.shape, jnp.float32)] * 4,
        compiler_params=pltpu.CompilerParams(vmem_limit_bytes=VMEM_LIMIT),
    )(flip, grads, weight, teacher, first, squares)


def shards(
    residual,
    student_mix,
    teacher_mix,
    positions,
    layer_scale,
    student_weight,
    teacher_weight,
    moment,
    second,
):
    half = DOUT // 2
    token_count = student_mix.shape[0]
    total_tokens = token_count * 256
    z, xlo, y, xhi, core = (lax.axis_index(name) for name in AXES)
    which = (core + z + xhi + xlo) & 1

    order = jnp.stack(
        [(((y + dy) & 3) * 2 + (xhi ^ dx)) * 2 + (core ^ side) for side, dy, dx in ORDER] + [which, core]
    ).astype(jnp.int32)
    scale = layer_scale.reshape(1, DOUT)
    own = jnp.stack(
        [
            lax.dynamic_slice_in_dim(weight, which * half, half, axis=-1)
            for weight in (student_weight, teacher_weight)
        ]
    ).astype(jnp.bfloat16)

    own, student_sent, teacher_sent, positions_sent, student_held, teacher_held, residual = lax.optimization_barrier(
        (own, student_mix, teacher_mix, positions, student_weight, teacher_weight, residual)
    )
    student_weight, teacher_weight = student_held, teacher_held
    student_other, positions_sent = lax.optimization_barrier((swap_cores(student_sent), positions_sent))
    teacher_other, places_other = swap_cores(teacher_sent), swap_cores(positions_sent)
    up, down, across, student_other, teacher_other, places, places_other, student_held, teacher_held = (
        lax.optimization_barrier(
            (
                from_y_next(own), from_y_previous(own), from_x_near(own), student_other, teacher_other, positions,
                places_other, student_held, teacher_held,
            )
        )
    )
    other_sent = split_weights(order, student_held, teacher_held)
    student_prepared = prepare_student(order, student_mix, student_other)
    (
        up_two, across_down, across_up, passed_up, passed_down, across, other_sent, places, places_other,
        student_prepared, teacher_other, residual,
    ) = lax.optimization_barrier(
        (
            from_y_next(up), from_y_previous(across), from_x_near(up), from_z_next(up), from_z_previous(down), across,
            other_sent, places, places_other, student_prepared,
            teacher_other, residual,
        )
    )
    prepared = prepare_teacher(order, teacher_mix, teacher_other, residual, places, places_other)
    (
        across_two, passed_two, passed_across_up, passed_across_down, passed_across, prepared, other_sent, residual_sent
    ) = lax.optimization_barrier(
        (
            from_y_next(across_up), from_z_next(up_two), from_z_previous(across_up), from_x_near(passed_down),
            from_x_twin(across), prepared, other_sent, residual,
        )
    )
    student_early, student_late, sent_mix, kept_mix = student_prepared
    teacher_early, teacher_late, picked = prepared
    passed_across_two = from_z_next(across_two)
    residual_other, picked_other, other = swap_cores(residual_sent), swap_cores(picked), swap_cores(other_sent)
    student_part, teacher_part = early_forward(
        (
            own, up, down, across, up_two, across_down, across_up, passed_up, passed_down, across_two, passed_two,
            passed_across_up, passed_across_down, passed_across,
        ),
        student_early,
        teacher_early,
    )
    student_out, matched, sums = late_forward(
        order, (other, passed_across_two), student_late, teacher_late, student_part, teacher_part, residual,
        residual_other, picked, picked_other, scale
    )
    more_sums = swap_cores(sums)

    def to_neighbours(part, after):
        part_sums, after = lax.optimization_barrier((sums, after))
        *sent, held, tokens_own, tokens_other = send_grads(
            total_tokens, part, order, student_out, matched, part_sums, more_sums, scale, sent_mix
        )
        passed = (from_z_previous(sent[0]), from_z_next(sent[1]), from_x_twin(sent[2]))
        return sent, held, tokens_own, tokens_other, passed

    def over_fsdp(rows):
        return lax.all_to_all(rows, ("xlo", "y", "xhi"), 0, 0, axis_index_groups=FSDP_GROUPS)

    sent, first_held, first_own, first_other, first_passed = to_neighbours(0, more_sums)
    _, last_held, last_own, last_other, last_passed = to_neighbours(1, sent)
    first_kept, last_kept = keep_grads(first_held, kept_mix), keep_grads(last_held, kept_mix)
    first_passed, last_kept, last_other = lax.optimization_barrier((first_passed, last_kept, last_other))
    first_rows, last_kept, last_other = lax.optimization_barrier(
        (add_passed(first_kept, first_passed), last_kept, last_other)
    )
    swapped = swap_cores(first_other), swap_cores(last_other)
    first_chip, last_rows = lax.optimization_barrier((over_fsdp(first_rows), add_passed(last_kept, last_passed)))
    last_chip = over_fsdp(last_rows)
    student_tokens = join_tokens(order, first_own, last_own, *swapped)
    first_chip, last_chip, student_tokens = lax.optimization_barrier((first_chip, last_chip, student_tokens))
    total = total_rows(first_chip, last_chip)
    by_copy = lax.all_to_all(
        total.reshape(8, 16, half), ("z", "xlo"), 0, 0, axis_index_groups=DP_GROUPS
    )
    full = lax.all_to_all(spread_rows(by_copy, 16), ("z", "xlo"), 0, 0)
    flip = ((core + xhi) & 1).astype(jnp.int32).reshape(1)
    weight_next, teacher_next, first_next, squares_next = adamw_update(
        flip, full.reshape(8, 2, 16, half), student_weight, teacher_weight, moment, second
    )
    return (weight_next, teacher_next, first_next, squares_next, student_tokens)


def solution(mesh):
    split = Mesh(mesh.devices.reshape(8, 2, 4, 2, 2), AXES)
    tokens = P(AXES, None)
    owned = P(("y", "xhi", "core"), None)
    return jax.shard_map(
        shards,
        mesh=split,
        in_specs=(tokens, tokens, tokens, tokens, P(), owned, owned, owned, owned),
        out_specs=(owned, owned, owned, owned, tokens),
        check_vma=False,
    )
```

```python
import functools

import jax
import jax.numpy as jnp
from jax import lax
from jax.experimental import pallas as pl
from jax.experimental.pallas import tpu as pltpu
from jax.sharding import Mesh, PartitionSpec as P

KIN = 2048
DOUT = 2048
PATCHES = 144
EPS = 1e-06
AXES = ("z", "xlo", "y", "xhi", "core")
VMEM_LIMIT = 32 * 1024 * 1024
SMALL_LIMIT = 16 * 1024 * 1024

X_INDEX = (0, 2, 1, 3)
CORE_SWAP = ((0, 1), (1, 0))
X_NEAR = tuple((X_INDEX[a], X_INDEX[b]) for a, b in ((1, 2), (2, 1), (0, 3), (3, 0)))


def from_next(size):
    return tuple(((i + 1) % size, i) for i in range(size))


def from_previous(size):
    return tuple((i, (i + 1) % size) for i in range(size))


def with_core_flip(pairs):
    return tuple((2 * a + 1 - core, 2 * b + core) for a, b in pairs for core in range(2))


FSDP_GROUPS = tuple(
    tuple((xhi ^ side) * 8 + y * 2 + xhi for y in range(4) for xhi in range(2)) for side in range(2)
)
DP_GROUPS = tuple(tuple(z * 2 + ((z + side) & 1) for z in range(8)) for side in range(2))


def swap_cores(value):
    return lax.ppermute(value, "core", CORE_SWAP)


def from_y_next(value):
    return lax.ppermute(value, "y", from_next(4))


def from_y_previous(value):
    return lax.ppermute(value, "y", from_previous(4))


def from_x_near(value):
    return lax.ppermute(value, ("xlo", "xhi"), X_NEAR)


def from_z_next(value):
    return lax.ppermute(value, ("z", "core"), with_core_flip(from_next(8)))


def from_z_previous(value):
    return lax.ppermute(value, ("z", "core"), with_core_flip(from_previous(8)))


def from_x_twin(value):
    return lax.ppermute(value, ("xlo", "core"), with_core_flip(CORE_SWAP))


ORDER = (
    (0, 0, 0), (0, 1, 0), (0, 3, 0), (0, 0, 1), (0, 2, 0), (0, 3, 1), (0, 1, 1), (1, 1, 0), (1, 3, 0), (0, 2, 1),
    (1, 2, 0), (1, 1, 1), (1, 3, 1), (1, 0, 1), (1, 0, 0), (1, 2, 1),
)
EARLY = 14
LATE = len(ORDER) - EARLY
HALF_AT = len(ORDER)
CORE_AT = HALF_AT + 1
SENT = (3, 3, 2)
TILE = 256
PARTS = (3, 1)


def split_kernel(order, student, teacher, out):
    out[0] = student[...].astype(jnp.bfloat16)
    out[1] = teacher[...].astype(jnp.bfloat16)


def split_weights(order, student, teacher):
    rows, width, steps = student.shape[0], 512, 2

    def half(j, order):
        return (0, (order[HALF_AT] ^ 1) * steps + j)

    return pl.pallas_call(
        split_kernel,
        grid_spec=pltpu.PrefetchScalarGridSpec(
            num_scalar_prefetch=1,
            grid=(steps,),
            in_specs=[pl.BlockSpec((rows, width), half)] * 2,
            out_specs=pl.BlockSpec((2, rows, width), lambda j, order: (0, 0, j)),
        ),
        out_shape=jax.ShapeDtypeStruct((2, rows, width * steps), jnp.bfloat16),
        compiler_params=pltpu.CompilerParams(vmem_limit_bytes=SMALL_LIMIT),
        cost_estimate=pl.CostEstimate(flops=0, bytes_accessed=1536 * 1024, transcendentals=0),
    )(order, student, teacher)


def place_blocks(order, step, packed, early, late):
    for part in range(2):
        columns = slice(part * 128, (part + 1) * 128)
        for block in range(len(ORDER)):
            @pl.when(order[block] == 2 * step + part)
            def _():
                if block < EARLY:
                    early[:, block * 128 : (block + 1) * 128] = packed[:, columns]
                else:
                    late[:, (block - EARLY) * 128 : (block - EARLY + 1) * 128] = packed[:, columns]


def student_kernel(order, mix_own, mix_other, early, late, sent_out, kept_out, turned, packed):
    own = mix_own.shape[0]
    packed[:own, :] = mix_own[...]
    packed[own:, :] = mix_other[...]
    turned[...] = packed[...].T
    core = order[CORE_AT]
    kept_out[0] = turned[pl.ds(pl.multiple_of(core * 128, 128), 128), :]
    sent_out[0] = turned[pl.ds(pl.multiple_of((1 - core) * 128, 128), 128), :]
    place_blocks(order, pl.program_id(0), packed, early, late)


def teacher_kernel(
    order, mix_own, mix_other, residual, places_own, places_other, early, late, picked_out, packed, picks
):
    own, step = mix_own.shape[0], pl.program_id(0)
    crops = own // PATCHES

    @pl.when(step == 0)
    def _():
        source = lax.broadcasted_iota(jnp.int32, (PATCHES, PATCHES), 0)
        for side, places in enumerate((places_own, places_other)):
            for crop in range(crops):
                chosen = jnp.where(places[crop : crop + 1, :] == source, 1.0, 0.0)
                picks[side * crops + crop] = chosen.T.astype(jnp.bfloat16)

    for side, mix in enumerate((mix_own, mix_other)):
        for crop in range(crops):
            rows = slice(crop * PATCHES, (crop + 1) * PATCHES)
            at = side * crops + crop
            packed[at * PATCHES : (at + 1) * PATCHES, :] = jnp.dot(
                picks[at], mix[rows, :], preferred_element_type=jnp.float32
            ).astype(jnp.bfloat16)
            if side == 0:
                picked_out[rows, :] = jnp.dot(
                    picks[at], residual[rows, :], preferred_element_type=jnp.float32
                ).astype(jnp.bfloat16)
    place_blocks(order, step, packed, early, late)


def prepare_student(order, mix_own, mix_other):
    own, steps = mix_own.shape[0], 8
    rows, width = 2 * own, KIN // steps
    mix = pl.BlockSpec((own, width), lambda i, order: (0, i))
    turned = pl.BlockSpec((1, 128, rows), lambda i, order: (i, 0, 0))
    return pl.pallas_call(
        student_kernel,
        grid_spec=pltpu.PrefetchScalarGridSpec(
            num_scalar_prefetch=1,
            grid=(steps,),
            in_specs=[mix] * 2,
            out_specs=[
                pl.BlockSpec((rows, EARLY * 128), lambda i, order: (0, 0)),
                pl.BlockSpec((rows, LATE * 128), lambda i, order: (0, 0)),
                turned,
                turned,
            ],
            scratch_shapes=[pltpu.VMEM((width, rows), jnp.bfloat16), pltpu.VMEM((rows, width), jnp.bfloat16)],
        ),
        out_shape=[
            jax.ShapeDtypeStruct((rows, EARLY * 128), jnp.bfloat16),
            jax.ShapeDtypeStruct((rows, LATE * 128), jnp.bfloat16),
            jax.ShapeDtypeStruct((8, 128, rows), jnp.bfloat16),
            jax.ShapeDtypeStruct((8, 128, rows), jnp.bfloat16),
        ],
        compiler_params=pltpu.CompilerParams(vmem_limit_bytes=VMEM_LIMIT),
        cost_estimate=pl.CostEstimate(flops=0, bytes_accessed=7 * 1024 * 1024, transcendentals=0),
    )(order, mix_own, mix_other)


def prepare_teacher(order, mix_own, mix_other, residual, places, places_other):
    own, steps = mix_own.shape[0], 8
    rows, width = 2 * own, KIN // steps
    mix = pl.BlockSpec((own, width), lambda i, order: (0, i))
    place = pl.BlockSpec(places.shape, lambda i, order: (0, 0))
    return pl.pallas_call(
        teacher_kernel,
        grid_spec=pltpu.PrefetchScalarGridSpec(
            num_scalar_prefetch=1,
            grid=(steps,),
            in_specs=[mix] * 3 + [place] * 2,
            out_specs=[
                pl.BlockSpec((rows, EARLY * 128), lambda i, order: (0, 0)),
                pl.BlockSpec((rows, LATE * 128), lambda i, order: (0, 0)),
                mix,
            ],
            scratch_shapes=[
                pltpu.VMEM((rows, width), jnp.bfloat16),
                pltpu.VMEM((rows // PATCHES, PATCHES, PATCHES), jnp.bfloat16),
            ],
        ),
        out_shape=[
            jax.ShapeDtypeStruct((rows, EARLY * 128), jnp.bfloat16),
            jax.ShapeDtypeStruct((rows, LATE * 128), jnp.bfloat16),
            jax.ShapeDtypeStruct((own, DOUT), jnp.bfloat16),
        ],
        compiler_params=pltpu.CompilerParams(vmem_limit_bytes=VMEM_LIMIT),
        cost_estimate=pl.CostEstimate(
            flops=3 * rows * PATCHES * KIN, bytes_accessed=9 * 1024 * 1024, transcendentals=0
        ),
    )(order, mix_own, mix_other, residual, places, places_other)


def early_kernel(student_mix, teacher_mix, *refs):
    weights, (student_out, teacher_out, held) = refs[:EARLY], refs[EARLY:]
    for block in range(EARLY):
        rows = slice(block * 128, (block + 1) * 128)
        held[0, rows, :] = weights[block][0]
        held[1, rows, :] = weights[block][1]
    student_out[...] = jnp.dot(student_mix[...], held[0], preferred_element_type=jnp.float32)
    teacher_out[...] = jnp.dot(teacher_mix[...], held[1], preferred_element_type=jnp.float32)


def early_forward(pieces, student_mix, teacher_mix):
    rows, depth = student_mix.shape
    columns, width = pieces[0].shape[-1], 256
    whole = pl.BlockSpec((rows, depth), lambda j: (0, 0))
    column = pl.BlockSpec((rows, width), lambda j: (0, j))
    return pl.pallas_call(
        early_kernel,
        grid=(columns // width,),
        in_specs=[whole, whole] + [pl.BlockSpec((2, 128, width), lambda j: (0, 0, j))] * EARLY,
        out_specs=[column, column],
        out_shape=[jax.ShapeDtypeStruct((rows, columns), jnp.float32)] * 2,
        scratch_shapes=[pltpu.VMEM((2, depth, width), jnp.bfloat16)],
        compiler_params=pltpu.CompilerParams(vmem_limit_bytes=VMEM_LIMIT),
        cost_estimate=pl.CostEstimate(
            flops=4 * rows * depth * columns, bytes_accessed=17 * 1024 * 1024, transcendentals=0
        ),
    )(student_mix, teacher_mix, *pieces)


def late_kernel(
    order, student_mix, teacher_mix, student_part, teacher_part, residual_own, residual_other, picked_own, picked_other,
    scale, *refs
):
    weights, (student_out, matched_out, sums_out, held) = refs[:LATE], refs[LATE:]
    for block in range(LATE):
        rows = slice(block * 128, (block + 1) * 128)
        held[0, rows, :] = weights[block][0]
        held[1, rows, :] = weights[block][1]
    factor = scale[...] * (KIN ** (-0.5))
    student_sum = student_part[...] + jnp.dot(student_mix[...], held[0], preferred_element_type=jnp.float32)
    teacher_sum = teacher_part[...] + jnp.dot(teacher_mix[...], held[1], preferred_element_type=jnp.float32)
    own = residual_own.shape[0]
    first = pl.program_id(0) == 0
    for side, (residual, picked) in enumerate(((residual_own, picked_own), (residual_other, picked_other))):
        tokens = slice(side * own, (side + 1) * own)
        student = residual[...].astype(jnp.float32) + factor * student_sum[tokens]
        matched = picked[...].astype(jnp.float32) + factor * teacher_sum[tokens]
        student_out[tokens, :] = student
        matched_out[tokens, :] = matched
        spot = lax.broadcasted_iota(jnp.int32, (own, 128), 1)
        sums = jnp.where(
            spot == 0,
            jnp.sum(student * student, axis=-1, keepdims=True),
            jnp.where(
                spot == 1,
                jnp.sum(matched * matched, axis=-1, keepdims=True),
                jnp.where(spot == 2, jnp.sum(student * matched, axis=-1, keepdims=True), 0.0),
            ),
        )
        sums_out[tokens, :] = sums + jnp.where(first, 0.0, sums_out[tokens, :])


def late_forward(
    order, pieces, student_mix, teacher_mix, student_part, teacher_part, residual, residual_other, picked, picked_other,
    scale
):
    (rows, columns), own, width = student_part.shape, residual.shape[0], 256
    steps = columns // width
    whole = pl.BlockSpec((rows, LATE * 128), lambda j, order: (0, 0))
    column = pl.BlockSpec((rows, width), lambda j, order: (0, j))
    tokens = pl.BlockSpec((own, width), lambda j, order: (0, order[HALF_AT] * steps + j))
    return pl.pallas_call(
        late_kernel,
        grid_spec=pltpu.PrefetchScalarGridSpec(
            num_scalar_prefetch=1,
            grid=(steps,),
            in_specs=[whole, whole, column, column]
            + [tokens] * 4
            + [pl.BlockSpec((1, width), lambda j, order: (0, order[HALF_AT] * steps + j))]
            + [pl.BlockSpec((2, 128, width), lambda j, order: (0, 0, j))] * LATE,
            out_specs=[column, column, pl.BlockSpec((rows, 128), lambda j, order: (0, 0))],
            scratch_shapes=[pltpu.VMEM((2, LATE * 128, width), jnp.bfloat16)],
        ),
        out_shape=[
            jax.ShapeDtypeStruct((rows, columns), jnp.float32),
            jax.ShapeDtypeStruct((rows, columns), jnp.float32),
            jax.ShapeDtypeStruct((rows, 128), jnp.float32),
        ],
        compiler_params=pltpu.CompilerParams(vmem_limit_bytes=VMEM_LIMIT),
        cost_estimate=pl.CostEstimate(
            flops=4 * rows * LATE * 128 * columns, bytes_accessed=13 * 1024 * 1024, transcendentals=0
        ),
    )(
        order, student_mix, teacher_mix, student_part, teacher_part, residual, residual_other, picked, picked_other,
        scale, *pieces
    )


def send_kernel(
    total_tokens, order, student, matched, sums, more_sums, scale, mix, next_out, previous_out, twin_out, held_out,
    tokens_own, tokens_other
):
    own = more_sums.shape[0] // 2
    swapped = jnp.concatenate([more_sums[own:, :], more_sums[:own, :]], axis=0)
    total = (sums[...] + swapped) * (1.0 / DOUT)
    inverse_rms = lax.rsqrt(total[:, 0:1] + EPS)
    inverse_matched = lax.rsqrt(total[:, 1:2] + EPS)
    overlap = inverse_rms * inverse_matched * total[:, 2:3]
    shared = inverse_rms * (1.0 / total_tokens)
    student_part = shared * inverse_rms * (EPS * inverse_rms * inverse_rms + overlap)
    matched_part = shared * inverse_matched
    values = student[...]
    tokens = (values * inverse_rms).astype(jnp.bfloat16)
    tokens_own[...] = tokens[:own]
    tokens_other[...] = tokens[own:]
    factor = scale[...] * (KIN ** (-0.5))
    held_out[...] = (factor * (values * student_part - matched[...] * matched_part)).astype(jnp.bfloat16)
    at = 0
    for out in (next_out, previous_out, twin_out):
        count = out.shape[0]
        grad = jnp.dot(
            mix[at : at + count].reshape(count * 128, mix.shape[-1]),
            held_out[...],
            preferred_element_type=jnp.float32,
        )
        out[...] = grad.astype(jnp.bfloat16).reshape(out.shape)
        at += count


def send_grads(total_tokens, part, order, student, matched, sums, more_sums, scale, turned):
    rows, columns = student.shape
    steps, count, first = columns // TILE, PARTS[part], sum(PARTS[:part])
    column = pl.BlockSpec((rows, TILE), lambda j, order: (0, first + j))
    narrow = pl.BlockSpec((rows, 128), lambda j, order: (0, 0))
    out = pl.BlockSpec((rows, TILE), lambda j, order: (0, j))
    half = pl.BlockSpec((rows // 2, TILE), lambda j, order: (0, j))
    return pl.pallas_call(
        functools.partial(send_kernel, total_tokens),
        grid_spec=pltpu.PrefetchScalarGridSpec(
            num_scalar_prefetch=1,
            grid=(count,),
            in_specs=[
                column,
                column,
                narrow,
                narrow,
                pl.BlockSpec((1, TILE), lambda j, order: (0, order[HALF_AT] * steps + first + j)),
                pl.BlockSpec((8, 128, rows), lambda j, order: (0, 0, 0)),
            ],
            out_specs=[pl.BlockSpec((size, 128, TILE), lambda j, order: (0, 0, j)) for size in SENT]
            + [out, half, half],
        ),
        out_shape=[jax.ShapeDtypeStruct((size, 128, count * TILE), jnp.bfloat16) for size in SENT]
        + [
            jax.ShapeDtypeStruct((rows, count * TILE), jnp.bfloat16),
            jax.ShapeDtypeStruct((rows // 2, count * TILE), jnp.bfloat16),
            jax.ShapeDtypeStruct((rows // 2, count * TILE), jnp.bfloat16),
        ],
        compiler_params=pltpu.CompilerParams(vmem_limit_bytes=VMEM_LIMIT),
        cost_estimate=pl.CostEstimate(
            flops=rows * KIN * count * TILE, bytes_accessed=3 * count * 1024 * 1024, transcendentals=0
        ),
    )(order, student, matched, sums, more_sums, scale, turned)


def keep_kernel(held, mix, out):
    grad = jnp.dot(
        mix[...].reshape(8 * 128, mix.shape[-1]), held[...], preferred_element_type=jnp.float32
    )
    out[...] = grad.reshape(out.shape)


def keep_grads(held, kept):
    (rows, columns), width = held.shape, 256
    return pl.pallas_call(
        keep_kernel,
        grid=(columns // width,),
        in_specs=[
            pl.BlockSpec((rows, width), lambda j: (0, j)),
            pl.BlockSpec((8, 128, rows), lambda j: (0, 0, 0)),
        ],
        out_specs=pl.BlockSpec((8, 128, width), lambda j: (0, 0, j)),
        out_shape=jax.ShapeDtypeStruct((8, 128, columns), jnp.float32),
        compiler_params=pltpu.CompilerParams(vmem_limit_bytes=VMEM_LIMIT),
        cost_estimate=pl.CostEstimate(
            flops=rows * KIN * columns, bytes_accessed=7 * 1024 * 1024, transcendentals=0
        ),
    )(held, kept)


def add_kernel(kept, *refs):
    passed, out = refs[:-1], refs[-1]
    at = 0
    for part in passed:
        spot = slice(at, at + part.shape[0])
        out[spot] = (kept[spot] + part[...].astype(jnp.float32)).astype(jnp.bfloat16)
        at += part.shape[0]


def add_passed(kept, passed):
    width = 256

    def blocks(count):
        return pl.BlockSpec((count, 128, width), lambda j: (0, 0, j))

    return pl.pallas_call(
        add_kernel,
        grid=(kept.shape[-1] // width,),
        in_specs=[blocks(8)] + [blocks(count) for count in SENT],
        out_specs=blocks(8),
        out_shape=jax.ShapeDtypeStruct(kept.shape, jnp.bfloat16),
        compiler_params=pltpu.CompilerParams(vmem_limit_bytes=VMEM_LIMIT),
    )(kept, *passed)


def join_kernel(order, first_own, last_own, first_other, last_other, out):
    step, width = pl.program_id(0), first_own.shape[1]
    for at, (first, last) in enumerate(((first_own, last_own), (first_other, last_other))):
        @pl.when(step == (at ^ order[HALF_AT]))
        def _():
            out[:, :width] = first[...]
            out[:, width:] = last[...]


def join_tokens(order, first_own, last_own, first_other, last_other):
    rows, half = first_own.shape[0], first_own.shape[1] + last_own.shape[1]
    first = pl.BlockSpec(first_own.shape, lambda j, order: (0, 0))
    last = pl.BlockSpec(last_own.shape, lambda j, order: (0, 0))
    return pl.pallas_call(
        join_kernel,
        grid_spec=pltpu.PrefetchScalarGridSpec(
            num_scalar_prefetch=1,
            grid=(2,),
            in_specs=[first, last, first, last],
            out_specs=pl.BlockSpec((rows, half), lambda j, order: (0, j)),
        ),
        out_shape=jax.ShapeDtypeStruct((rows, 2 * half), jnp.bfloat16),
        compiler_params=pltpu.CompilerParams(vmem_limit_bytes=SMALL_LIMIT),
        cost_estimate=pl.CostEstimate(flops=0, bytes_accessed=2400 * 1024, transcendentals=0),
    )(order, first_own, last_own, first_other, last_other)


def total_kernel(first, last, out):
    at = 0
    for chips in (first, last):
        total = chips[0].astype(jnp.float32)
        for chip in range(1, chips.shape[0]):
            total = total + chips[chip].astype(jnp.float32)
        out[:, at : at + total.shape[1]] = total.astype(jnp.bfloat16)
        at += total.shape[1]


def total_rows(first, last):
    chips, rows, _ = first.shape
    parts = [pl.BlockSpec((chips, rows // 2, part.shape[-1]), lambda i: (0, i, 0)) for part in (first, last)]
    columns = first.shape[-1] + last.shape[-1]
    return pl.pallas_call(
        total_kernel,
        grid=(2,),
        in_specs=parts,
        out_specs=pl.BlockSpec((rows // 2, columns), lambda i: (i, 0)),
        out_shape=jax.ShapeDtypeStruct((rows, columns), jnp.bfloat16),
        compiler_params=pltpu.CompilerParams(vmem_limit_bytes=SMALL_LIMIT),
        cost_estimate=pl.CostEstimate(flops=0, bytes_accessed=2400 * 1024, transcendentals=0),
    )(first, last)


def spread_kernel(copies, out):
    total = copies[0].astype(jnp.float32)
    for copy in range(1, copies.shape[0]):
        total = total + copies[copy].astype(jnp.float32)
    out[...] = jnp.broadcast_to(total.astype(jnp.bfloat16)[None], out.shape)


def spread_rows(copies, count):
    _, rows, columns = copies.shape
    return pl.pallas_call(
        spread_kernel,
        out_shape=jax.ShapeDtypeStruct((count, rows, columns), jnp.bfloat16),
        compiler_params=pltpu.CompilerParams(vmem_limit_bytes=SMALL_LIMIT),
        cost_estimate=pl.CostEstimate(flops=0, bytes_accessed=800 * 1024, transcendentals=0),
    )(copies)


def moments_kernel(first, squares, first_out, squares_out):
    first_out[...] = 0.9 * first[...]
    squares_out[...] = 0.95 * squares[...]


def scale_moments(first, squares):
    rows = pl.BlockSpec((64, DOUT), lambda i: (i, 0))
    return pl.pallas_call(
        moments_kernel,
        grid=(2,),
        in_specs=[rows, rows],
        out_specs=[rows, rows],
        out_shape=[jax.ShapeDtypeStruct(first.shape, jnp.float32)] * 2,
        compiler_params=pltpu.CompilerParams(vmem_limit_bytes=SMALL_LIMIT),
        cost_estimate=pl.CostEstimate(flops=0, bytes_accessed=4 * 1024 * 1024, transcendentals=0),
    )(first, squares)


def update_kernel(flip, grads, weight, teacher, first, squares, weight_out, teacher_out, first_out, squares_out):
    rows = []
    for index in range(grads.shape[0]):
        swap = ((flip[0] + index) & 1) == 1
        left = jnp.where(swap, grads[index, 1], grads[index, 0])
        right = jnp.where(swap, grads[index, 0], grads[index, 1])
        rows.append(jnp.concatenate([left, right], axis=1))
    grad = jnp.concatenate(rows, axis=0).astype(jnp.float32)
    first_next = first[...] + 0.1 * grad
    squares_next = squares[...] + 0.05 * grad * grad
    held = weight[...]
    weight_next = held - 0.1 * (first_next / (jnp.sqrt(squares_next) + 1e-08) + 0.04 * held)
    weight_out[...] = weight_next
    teacher_out[...] = 0.96 * teacher[...] + 0.04 * weight_next
    first_out[...] = first_next
    squares_out[...] = squares_next


def adamw_update(flip, grads, weight, teacher, first, squares):
    rows = pl.BlockSpec((32, DOUT), lambda i, flip: (i, 0))
    return pl.pallas_call(
        update_kernel,
        grid_spec=pltpu.PrefetchScalarGridSpec(
            num_scalar_prefetch=1,
            grid=(4,),
            in_specs=[pl.BlockSpec((2, 2, 16, DOUT // 2), lambda i, flip: (i, 0, 0, 0))] + [rows] * 4,
            out_specs=[rows] * 4,
        ),
        out_shape=[jax.ShapeDtypeStruct(weight.shape, jnp.float32)] * 4,
        compiler_params=pltpu.CompilerParams(vmem_limit_bytes=VMEM_LIMIT),
    )(flip, grads, weight, teacher, first, squares)


def shards(
    residual,
    student_mix,
    teacher_mix,
    positions,
    layer_scale,
    student_weight,
    teacher_weight,
    moment,
    second,
):
    half = DOUT // 2
    token_count = student_mix.shape[0]
    total_tokens = token_count * 256
    z, xlo, y, xhi, core = (lax.axis_index(name) for name in AXES)
    which = (core + z + xhi + xlo) & 1

    order = jnp.stack(
        [(((y + dy) & 3) * 2 + (xhi ^ dx)) * 2 + (core ^ side) for side, dy, dx in ORDER] + [which, core]
    ).astype(jnp.int32)
    scale = layer_scale.reshape(1, DOUT)
    own = jnp.stack(
        [
            lax.dynamic_slice_in_dim(weight, which * half, half, axis=-1)
            for weight in (student_weight, teacher_weight)
        ]
    ).astype(jnp.bfloat16)

    own, student_sent, teacher_sent, positions_sent, student_held, teacher_held, residual = lax.optimization_barrier(
        (own, student_mix, teacher_mix, positions, student_weight, teacher_weight, residual)
    )
    student_weight, teacher_weight = student_held, teacher_held
    student_other, positions_sent = lax.optimization_barrier((swap_cores(student_sent), positions_sent))
    teacher_other, places_other = swap_cores(teacher_sent), swap_cores(positions_sent)
    up, down, across, student_other, teacher_other, places, places_other, student_held, teacher_held = (
        lax.optimization_barrier(
            (
                from_y_next(own), from_y_previous(own), from_x_near(own), student_other, teacher_other, positions,
                places_other, student_held, teacher_held,
            )
        )
    )
    other_sent = split_weights(order, student_held, teacher_held)
    student_prepared = prepare_student(order, student_mix, student_other)
    (
        up_two, across_down, across_up, passed_up, passed_down, across, other_sent, places, places_other,
        student_prepared, teacher_other, residual,
    ) = lax.optimization_barrier(
        (
            from_y_next(up), from_y_previous(across), from_x_near(up), from_z_next(up), from_z_previous(down), across,
            other_sent, places, places_other, student_prepared,
            teacher_other, residual,
        )
    )
    prepared = prepare_teacher(order, teacher_mix, teacher_other, residual, places, places_other)
    (
        across_two, passed_two, passed_across_up, passed_across_down, passed_across, prepared, other_sent, residual_sent
    ) = lax.optimization_barrier(
        (
            from_y_next(across_up), from_z_next(up_two), from_z_previous(across_up), from_x_near(passed_down),
            from_x_twin(across), prepared, other_sent, residual,
        )
    )
    student_early, student_late, sent_mix, kept_mix = student_prepared
    teacher_early, teacher_late, picked = prepared
    passed_across_two = from_z_next(across_two)
    residual_other, picked_other, other = swap_cores(residual_sent), swap_cores(picked), swap_cores(other_sent)
    student_part, teacher_part = early_forward(
        (
            own, up, down, across, up_two, across_down, across_up, passed_up, passed_down, across_two, passed_two,
            passed_across_up, passed_across_down, passed_across,
        ),
        student_early,
        teacher_early,
    )
    student_out, matched, sums = late_forward(
        order, (other, passed_across_two), student_late, teacher_late, student_part, teacher_part, residual,
        residual_other, picked, picked_other, scale
    )
    more_sums = swap_cores(sums)

    def to_neighbours(part, after):
        part_sums, after = lax.optimization_barrier((sums, after))
        *sent, held, tokens_own, tokens_other = send_grads(
            total_tokens, part, order, student_out, matched, part_sums, more_sums, scale, sent_mix
        )
        passed = (from_z_previous(sent[0]), from_z_next(sent[1]), from_x_twin(sent[2]))
        return sent, held, tokens_own, tokens_other, passed

    def over_fsdp(rows):
        return lax.all_to_all(rows, ("xlo", "y", "xhi"), 0, 0, axis_index_groups=FSDP_GROUPS)

    sent, first_held, first_own, first_other, first_passed = to_neighbours(0, more_sums)
    _, last_held, last_own, last_other, last_passed = to_neighbours(1, sent)
    first_kept, last_kept = keep_grads(first_held, kept_mix), keep_grads(last_held, kept_mix)
    first_passed, last_kept, last_other = lax.optimization_barrier((first_passed, last_kept, last_other))
    first_rows, last_kept, last_other = lax.optimization_barrier(
        (add_passed(first_kept, first_passed), last_kept, last_other)
    )
    swapped = swap_cores(first_other), swap_cores(last_other)
    first_chip, last_rows = lax.optimization_barrier((over_fsdp(first_rows), add_passed(last_kept, last_passed)))
    last_chip = over_fsdp(last_rows)
    student_tokens = join_tokens(order, first_own, last_own, *swapped)
    moment_held, second_held, first_chip = lax.optimization_barrier((moment, second, first_chip))
    moments = scale_moments(moment_held, second_held)
    first_chip, last_chip, student_tokens, moments = lax.optimization_barrier(
        (first_chip, last_chip, student_tokens, moments)
    )
    total = total_rows(first_chip, last_chip)
    by_copy = lax.all_to_all(
        total.reshape(8, 16, half), ("z", "xlo"), 0, 0, axis_index_groups=DP_GROUPS
    )
    full = lax.all_to_all(spread_rows(by_copy, 16), ("z", "xlo"), 0, 0)
    flip = ((core + xhi) & 1).astype(jnp.int32).reshape(1)
    weight_next, teacher_next, first_next, squares_next = adamw_update(
        flip, full.reshape(8, 2, 16, half), student_weight, teacher_weight, *moments
    )
    return (weight_next, teacher_next, first_next, squares_next, student_tokens)


def solution(mesh):
    split = Mesh(mesh.devices.reshape(8, 2, 4, 2, 2), AXES)
    tokens = P(AXES, None)
    owned = P(("y", "xhi", "core"), None)
    return jax.shard_map(
        shards,
        mesh=split,
        in_specs=(tokens, tokens, tokens, tokens, P(), owned, owned, owned, owned),
        out_specs=(owned, owned, owned, owned, tokens),
        check_vma=False,
    )
```

```python
import functools

import jax
import jax.numpy as jnp
from jax import lax
from jax.experimental import pallas as pl
from jax.experimental.pallas import tpu as pltpu
from jax.sharding import Mesh, PartitionSpec as P

KIN = 2048
DOUT = 2048
PATCHES = 144
EPS = 1e-06
AXES = ("z", "xlo", "y", "xhi", "core")
VMEM_LIMIT = 32 * 1024 * 1024
SMALL_LIMIT = 16 * 1024 * 1024

X_INDEX = (0, 2, 1, 3)
CORE_SWAP = ((0, 1), (1, 0))
X_NEAR = tuple((X_INDEX[a], X_INDEX[b]) for a, b in ((1, 2), (2, 1), (0, 3), (3, 0)))


def from_next(size):
    return tuple(((i + 1) % size, i) for i in range(size))


def from_previous(size):
    return tuple((i, (i + 1) % size) for i in range(size))


def with_core_flip(pairs):
    return tuple((2 * a + 1 - core, 2 * b + core) for a, b in pairs for core in range(2))


FSDP_GROUPS = tuple(
    tuple((xhi ^ side) * 8 + y * 2 + xhi for y in range(4) for xhi in range(2)) for side in range(2)
)
DP_GROUPS = tuple(tuple(z * 2 + ((z + side) & 1) for z in range(8)) for side in range(2))


def swap_cores(value):
    return lax.ppermute(value, "core", CORE_SWAP)


def from_y_next(value):
    return lax.ppermute(value, "y", from_next(4))


def from_y_previous(value):
    return lax.ppermute(value, "y", from_previous(4))


def from_x_near(value):
    return lax.ppermute(value, ("xlo", "xhi"), X_NEAR)


def from_z_next(value):
    return lax.ppermute(value, ("z", "core"), with_core_flip(from_next(8)))


def from_z_previous(value):
    return lax.ppermute(value, ("z", "core"), with_core_flip(from_previous(8)))


def from_x_twin(value):
    return lax.ppermute(value, ("xlo", "core"), with_core_flip(CORE_SWAP))


ORDER = (
    (0, 0, 0), (0, 1, 0), (0, 3, 0), (0, 0, 1), (0, 2, 0), (0, 3, 1), (0, 1, 1), (1, 1, 0), (1, 3, 0), (0, 2, 1),
    (1, 2, 0), (1, 1, 1), (1, 3, 1), (1, 0, 1), (1, 0, 0), (1, 2, 1),
)
EARLY = 14
LATE = len(ORDER) - EARLY
HALF_AT = len(ORDER)
CORE_AT = HALF_AT + 1
SENT = (3, 3, 2)
PARTS = 2


def split_kernel(order, student, teacher, out):
    out[0] = student[...].astype(jnp.bfloat16)
    out[1] = teacher[...].astype(jnp.bfloat16)


def split_weights(order, student, teacher):
    rows, width, steps = student.shape[0], 512, 2

    def half(j, order):
        return (0, (order[HALF_AT] ^ 1) * steps + j)

    return pl.pallas_call(
        split_kernel,
        grid_spec=pltpu.PrefetchScalarGridSpec(
            num_scalar_prefetch=1,
            grid=(steps,),
            in_specs=[pl.BlockSpec((rows, width), half)] * 2,
            out_specs=pl.BlockSpec((2, rows, width), lambda j, order: (0, 0, j)),
        ),
        out_shape=jax.ShapeDtypeStruct((2, rows, width * steps), jnp.bfloat16),
        compiler_params=pltpu.CompilerParams(vmem_limit_bytes=SMALL_LIMIT),
        cost_estimate=pl.CostEstimate(flops=0, bytes_accessed=1536 * 1024, transcendentals=0),
    )(order, student, teacher)


def halves_kernel(pair, first, second):
    first[...] = pair[0]
    second[...] = pair[1]


def both_halves(pair):
    _, rows, columns = pair.shape
    return pl.pallas_call(
        halves_kernel,
        out_shape=[jax.ShapeDtypeStruct((rows, columns), pair.dtype)] * 2,
        compiler_params=pltpu.CompilerParams(vmem_limit_bytes=SMALL_LIMIT),
        cost_estimate=pl.CostEstimate(flops=0, bytes_accessed=1024 * 1024, transcendentals=0),
    )(pair)


def place_blocks(order, step, packed, early, late):
    for part in range(2):
        columns = slice(part * 128, (part + 1) * 128)
        for block in range(len(ORDER)):
            @pl.when(order[block] == 2 * step + part)
            def _():
                if block < EARLY:
                    early[:, block * 128 : (block + 1) * 128] = packed[:, columns]
                else:
                    late[:, (block - EARLY) * 128 : (block - EARLY + 1) * 128] = packed[:, columns]


def student_kernel(order, mix_own, mix_other, early, late, sent_out, kept_out, turned, packed):
    own = mix_own.shape[0]
    packed[:own, :] = mix_own[...]
    packed[own:, :] = mix_other[...]
    turned[...] = packed[...].T
    core = order[CORE_AT]
    kept_out[0] = turned[pl.ds(pl.multiple_of(core * 128, 128), 128), :]
    sent_out[0] = turned[pl.ds(pl.multiple_of((1 - core) * 128, 128), 128), :]
    place_blocks(order, pl.program_id(0), packed, early, late)


def teacher_kernel(
    order, mix_own, mix_other, residual, places_own, places_other, early, late, picked_out, packed, picks
):
    own, step = mix_own.shape[0], pl.program_id(0)
    crops = own // PATCHES

    @pl.when(step == 0)
    def _():
        source = lax.broadcasted_iota(jnp.int32, (PATCHES, PATCHES), 0)
        for side, places in enumerate((places_own, places_other)):
            for crop in range(crops):
                chosen = jnp.where(places[crop : crop + 1, :] == source, 1.0, 0.0)
                picks[side * crops + crop] = chosen.T.astype(jnp.bfloat16)

    for side, mix in enumerate((mix_own, mix_other)):
        for crop in range(crops):
            rows = slice(crop * PATCHES, (crop + 1) * PATCHES)
            at = side * crops + crop
            packed[at * PATCHES : (at + 1) * PATCHES, :] = jnp.dot(
                picks[at], mix[rows, :], preferred_element_type=jnp.float32
            ).astype(jnp.bfloat16)
            if side == 0:
                picked_out[rows, :] = jnp.dot(
                    picks[at], residual[rows, :], preferred_element_type=jnp.float32
                ).astype(jnp.bfloat16)
    place_blocks(order, step, packed, early, late)


def prepare_student(order, mix_own, mix_other):
    own, steps = mix_own.shape[0], 8
    rows, width = 2 * own, KIN // steps
    mix = pl.BlockSpec((own, width), lambda i, order: (0, i))
    turned = pl.BlockSpec((1, 128, rows), lambda i, order: (i, 0, 0))
    return pl.pallas_call(
        student_kernel,
        grid_spec=pltpu.PrefetchScalarGridSpec(
            num_scalar_prefetch=1,
            grid=(steps,),
            in_specs=[mix] * 2,
            out_specs=[
                pl.BlockSpec((rows, EARLY * 128), lambda i, order: (0, 0)),
                pl.BlockSpec((rows, LATE * 128), lambda i, order: (0, 0)),
                turned,
                turned,
            ],
            scratch_shapes=[pltpu.VMEM((width, rows), jnp.bfloat16), pltpu.VMEM((rows, width), jnp.bfloat16)],
        ),
        out_shape=[
            jax.ShapeDtypeStruct((rows, EARLY * 128), jnp.bfloat16),
            jax.ShapeDtypeStruct((rows, LATE * 128), jnp.bfloat16),
            jax.ShapeDtypeStruct((8, 128, rows), jnp.bfloat16),
            jax.ShapeDtypeStruct((8, 128, rows), jnp.bfloat16),
        ],
        compiler_params=pltpu.CompilerParams(vmem_limit_bytes=VMEM_LIMIT),
        cost_estimate=pl.CostEstimate(flops=0, bytes_accessed=7 * 1024 * 1024, transcendentals=0),
    )(order, mix_own, mix_other)


def prepare_teacher(order, mix_own, mix_other, residual, places, places_other):
    own, steps = mix_own.shape[0], 8
    rows, width = 2 * own, KIN // steps
    mix = pl.BlockSpec((own, width), lambda i, order: (0, i))
    place = pl.BlockSpec(places.shape, lambda i, order: (0, 0))
    return pl.pallas_call(
        teacher_kernel,
        grid_spec=pltpu.PrefetchScalarGridSpec(
            num_scalar_prefetch=1,
            grid=(steps,),
            in_specs=[mix] * 3 + [place] * 2,
            out_specs=[
                pl.BlockSpec((rows, EARLY * 128), lambda i, order: (0, 0)),
                pl.BlockSpec((rows, LATE * 128), lambda i, order: (0, 0)),
                mix,
            ],
            scratch_shapes=[
                pltpu.VMEM((rows, width), jnp.bfloat16),
                pltpu.VMEM((rows // PATCHES, PATCHES, PATCHES), jnp.bfloat16),
            ],
        ),
        out_shape=[
            jax.ShapeDtypeStruct((rows, EARLY * 128), jnp.bfloat16),
            jax.ShapeDtypeStruct((rows, LATE * 128), jnp.bfloat16),
            jax.ShapeDtypeStruct((own, DOUT), jnp.bfloat16),
        ],
        compiler_params=pltpu.CompilerParams(vmem_limit_bytes=VMEM_LIMIT),
        cost_estimate=pl.CostEstimate(
            flops=3 * rows * PATCHES * KIN, bytes_accessed=9 * 1024 * 1024, transcendentals=0
        ),
    )(order, mix_own, mix_other, residual, places, places_other)


def early_kernel(student_mix, teacher_mix, *refs):
    weights, (student_out, teacher_out, held) = refs[:EARLY], refs[EARLY:]
    for block in range(EARLY):
        rows = slice(block * 128, (block + 1) * 128)
        held[0, rows, :] = weights[block][0]
        held[1, rows, :] = weights[block][1]
    student_out[...] = jnp.dot(student_mix[...], held[0], preferred_element_type=jnp.float32)
    teacher_out[...] = jnp.dot(teacher_mix[...], held[1], preferred_element_type=jnp.float32)


def early_forward(pieces, student_mix, teacher_mix):
    rows, depth = student_mix.shape
    columns, width = pieces[0].shape[-1], 256
    whole = pl.BlockSpec((rows, depth), lambda j: (0, 0))
    column = pl.BlockSpec((rows, width), lambda j: (0, j))
    return pl.pallas_call(
        early_kernel,
        grid=(columns // width,),
        in_specs=[whole, whole] + [pl.BlockSpec((2, 128, width), lambda j: (0, 0, j))] * EARLY,
        out_specs=[column, column],
        out_shape=[jax.ShapeDtypeStruct((rows, columns), jnp.float32)] * 2,
        scratch_shapes=[pltpu.VMEM((2, depth, width), jnp.bfloat16)],
        compiler_params=pltpu.CompilerParams(vmem_limit_bytes=VMEM_LIMIT),
        cost_estimate=pl.CostEstimate(
            flops=4 * rows * depth * columns, bytes_accessed=17 * 1024 * 1024, transcendentals=0
        ),
    )(student_mix, teacher_mix, *pieces)


def late_kernel(
    order, student_mix, teacher_mix, student_part, teacher_part, residual_own, residual_other, picked_own, picked_other,
    scale, *refs
):
    pair, student_weight, teacher_weight, student_out, matched_out, sums_out, held = refs
    held[:, :128, :] = pair[...]
    held[0, 128:, :] = student_weight[...]
    held[1, 128:, :] = teacher_weight[...]
    factor = scale[...] * (KIN ** (-0.5))
    student_sum = student_part[...] + jnp.dot(student_mix[...], held[0], preferred_element_type=jnp.float32)
    teacher_sum = teacher_part[...] + jnp.dot(teacher_mix[...], held[1], preferred_element_type=jnp.float32)
    own = residual_own.shape[0]
    first = pl.program_id(0) == 0
    for side, (residual, picked) in enumerate(((residual_own, picked_own), (residual_other, picked_other))):
        tokens = slice(side * own, (side + 1) * own)
        student = residual[...].astype(jnp.float32) + factor * student_sum[tokens]
        matched = picked[...].astype(jnp.float32) + factor * teacher_sum[tokens]
        student_out[tokens, :] = student
        matched_out[tokens, :] = matched
        spot = lax.broadcasted_iota(jnp.int32, (own, 128), 1)
        sums = jnp.where(
            spot == 0,
            jnp.sum(student * student, axis=-1, keepdims=True),
            jnp.where(
                spot == 1,
                jnp.sum(matched * matched, axis=-1, keepdims=True),
                jnp.where(spot == 2, jnp.sum(student * matched, axis=-1, keepdims=True), 0.0),
            ),
        )
        sums_out[tokens, :] = sums + jnp.where(first, 0.0, sums_out[tokens, :])


def late_forward(
    order, pieces, student_mix, teacher_mix, student_part, teacher_part, residual, residual_other, picked, picked_other,
    scale
):
    (rows, columns), own, width = student_part.shape, residual.shape[0], 256
    steps = columns // width
    whole = pl.BlockSpec((rows, LATE * 128), lambda j, order: (0, 0))
    column = pl.BlockSpec((rows, width), lambda j, order: (0, j))
    tokens = pl.BlockSpec((own, width), lambda j, order: (0, order[HALF_AT] * steps + j))
    return pl.pallas_call(
        late_kernel,
        grid_spec=pltpu.PrefetchScalarGridSpec(
            num_scalar_prefetch=1,
            grid=(steps,),
            in_specs=[whole, whole, column, column]
            + [tokens] * 4
            + [pl.BlockSpec((1, width), lambda j, order: (0, order[HALF_AT] * steps + j))]
            + [pl.BlockSpec((2, 128, width), lambda j, order: (0, 0, j))]
            + [pl.BlockSpec((128, width), lambda j, order: (0, j))] * 2,
            out_specs=[column, column, pl.BlockSpec((rows, 128), lambda j, order: (0, 0))],
            scratch_shapes=[pltpu.VMEM((2, LATE * 128, width), jnp.bfloat16)],
        ),
        out_shape=[
            jax.ShapeDtypeStruct((rows, columns), jnp.float32),
            jax.ShapeDtypeStruct((rows, columns), jnp.float32),
            jax.ShapeDtypeStruct((rows, 128), jnp.float32),
        ],
        compiler_params=pltpu.CompilerParams(vmem_limit_bytes=VMEM_LIMIT),
        cost_estimate=pl.CostEstimate(
            flops=4 * rows * LATE * 128 * columns, bytes_accessed=13 * 1024 * 1024, transcendentals=0
        ),
    )(
        order, student_mix, teacher_mix, student_part, teacher_part, residual, residual_other, picked, picked_other,
        scale, *pieces
    )


def send_kernel(
    total_tokens, order, student, matched, sums, more_sums, scale, mix, next_out, previous_out, twin_out, held_out,
    tokens_own, tokens_other
):
    own = more_sums.shape[0] // 2
    swapped = jnp.concatenate([more_sums[own:, :], more_sums[:own, :]], axis=0)
    total = (sums[...] + swapped) * (1.0 / DOUT)
    inverse_rms = lax.rsqrt(total[:, 0:1] + EPS)
    inverse_matched = lax.rsqrt(total[:, 1:2] + EPS)
    overlap = inverse_rms * inverse_matched * total[:, 2:3]
    shared = inverse_rms * (1.0 / total_tokens)
    student_part = shared * inverse_rms * (EPS * inverse_rms * inverse_rms + overlap)
    matched_part = shared * inverse_matched
    values = student[...]
    tokens = (values * inverse_rms).astype(jnp.bfloat16)
    tokens_own[...] = tokens[:own]
    tokens_other[...] = tokens[own:]
    factor = scale[...] * (KIN ** (-0.5))
    held_out[...] = (factor * (values * student_part - matched[...] * matched_part)).astype(jnp.bfloat16)
    at = 0
    for out in (next_out, previous_out, twin_out):
        count = out.shape[0]
        grad = jnp.dot(
            mix[at : at + count].reshape(count * 128, mix.shape[-1]),
            held_out[...],
            preferred_element_type=jnp.float32,
        )
        out[...] = grad.astype(jnp.bfloat16).reshape(out.shape)
        at += count


def send_grads(total_tokens, part, order, student, matched, sums, more_sums, scale, turned):
    (rows, columns), width = student.shape, 256
    steps = columns // width
    count = steps // PARTS
    column = pl.BlockSpec((rows, width), lambda j, order: (0, part * count + j))
    narrow = pl.BlockSpec((rows, 128), lambda j, order: (0, 0))
    out = pl.BlockSpec((rows, width), lambda j, order: (0, j))
    half = pl.BlockSpec((rows // 2, width), lambda j, order: (0, j))
    return pl.pallas_call(
        functools.partial(send_kernel, total_tokens),
        grid_spec=pltpu.PrefetchScalarGridSpec(
            num_scalar_prefetch=1,
            grid=(count,),
            in_specs=[
                column,
                column,
                narrow,
                narrow,
                pl.BlockSpec((1, width), lambda j, order: (0, order[HALF_AT] * steps + part * count + j)),
                pl.BlockSpec((8, 128, rows), lambda j, order: (0, 0, 0)),
            ],
            out_specs=[pl.BlockSpec((size, 128, width), lambda j, order: (0, 0, j)) for size in SENT]
            + [out, half, half],
        ),
        out_shape=[jax.ShapeDtypeStruct((size, 128, columns // PARTS), jnp.bfloat16) for size in SENT]
        + [
            jax.ShapeDtypeStruct((rows, columns // PARTS), jnp.bfloat16),
            jax.ShapeDtypeStruct((rows // 2, columns // PARTS), jnp.bfloat16),
            jax.ShapeDtypeStruct((rows // 2, columns // PARTS), jnp.bfloat16),
        ],
        compiler_params=pltpu.CompilerParams(vmem_limit_bytes=VMEM_LIMIT),
        cost_estimate=pl.CostEstimate(
            flops=rows * KIN * columns // PARTS, bytes_accessed=6 * 1024 * 1024, transcendentals=0
        ),
    )(order, student, matched, sums, more_sums, scale, turned)


def keep_kernel(held, mix, out):
    grad = jnp.dot(
        mix[...].reshape(8 * 128, mix.shape[-1]), held[...], preferred_element_type=jnp.float32
    )
    out[...] = grad.reshape(out.shape)


def keep_grads(held, kept):
    (rows, columns), width = held.shape, 256
    return pl.pallas_call(
        keep_kernel,
        grid=(columns // width,),
        in_specs=[
            pl.BlockSpec((rows, width), lambda j: (0, j)),
            pl.BlockSpec((8, 128, rows), lambda j: (0, 0, 0)),
        ],
        out_specs=pl.BlockSpec((8, 128, width), lambda j: (0, 0, j)),
        out_shape=jax.ShapeDtypeStruct((8, 128, columns), jnp.float32),
        compiler_params=pltpu.CompilerParams(vmem_limit_bytes=VMEM_LIMIT),
        cost_estimate=pl.CostEstimate(
            flops=rows * KIN * columns, bytes_accessed=7 * 1024 * 1024, transcendentals=0
        ),
    )(held, kept)


def add_kernel(kept, *refs):
    passed, out = refs[:-1], refs[-1]
    at = 0
    for part in passed:
        spot = slice(at, at + part.shape[0])
        out[spot] = (kept[spot] + part[...].astype(jnp.float32)).astype(jnp.bfloat16)
        at += part.shape[0]


def add_passed(kept, passed):
    width = 256

    def blocks(count):
        return pl.BlockSpec((count, 128, width), lambda j: (0, 0, j))

    return pl.pallas_call(
        add_kernel,
        grid=(kept.shape[-1] // width,),
        in_specs=[blocks(8)] + [blocks(count) for count in SENT],
        out_specs=blocks(8),
        out_shape=jax.ShapeDtypeStruct(kept.shape, jnp.bfloat16),
        compiler_params=pltpu.CompilerParams(vmem_limit_bytes=VMEM_LIMIT),
    )(kept, *passed)


def join_kernel(order, first_own, last_own, first_other, last_other, out):
    step = pl.program_id(0)
    for at, half in enumerate((first_own, last_own, first_other, last_other)):
        @pl.when(step == (at ^ (2 * order[HALF_AT])))
        def _():
            out[...] = half[...]


def join_tokens(order, *halves):
    rows, width = halves[0].shape
    return pl.pallas_call(
        join_kernel,
        grid_spec=pltpu.PrefetchScalarGridSpec(
            num_scalar_prefetch=1,
            grid=(4,),
            in_specs=[pl.BlockSpec((rows, width), lambda j, order: (0, 0))] * 4,
            out_specs=pl.BlockSpec((rows, width), lambda j, order: (0, j)),
        ),
        out_shape=jax.ShapeDtypeStruct((rows, 4 * width), jnp.bfloat16),
        compiler_params=pltpu.CompilerParams(vmem_limit_bytes=SMALL_LIMIT),
        cost_estimate=pl.CostEstimate(flops=0, bytes_accessed=2400 * 1024, transcendentals=0),
    )(order, *halves)


def total_kernel(first, last, out):
    width = first.shape[-1]
    for at, chips in enumerate((first, last)):
        total = chips[0].astype(jnp.float32)
        for chip in range(1, chips.shape[0]):
            total = total + chips[chip].astype(jnp.float32)
        out[:, at * width : (at + 1) * width] = total.astype(jnp.bfloat16)


def total_rows(first, last):
    chips, rows, width = first.shape
    block = pl.BlockSpec((chips, rows // 2, width), lambda i: (0, i, 0))
    return pl.pallas_call(
        total_kernel,
        grid=(2,),
        in_specs=[block, block],
        out_specs=pl.BlockSpec((rows // 2, 2 * width), lambda i: (i, 0)),
        out_shape=jax.ShapeDtypeStruct((rows, 2 * width), jnp.bfloat16),
        compiler_params=pltpu.CompilerParams(vmem_limit_bytes=SMALL_LIMIT),
        cost_estimate=pl.CostEstimate(flops=0, bytes_accessed=2400 * 1024, transcendentals=0),
    )(first, last)


def spread_kernel(copies, out):
    total = copies[0].astype(jnp.float32)
    for copy in range(1, copies.shape[0]):
        total = total + copies[copy].astype(jnp.float32)
    out[...] = jnp.broadcast_to(total.astype(jnp.bfloat16)[None], out.shape)


def spread_rows(copies, count):
    _, rows, columns = copies.shape
    return pl.pallas_call(
        spread_kernel,
        out_shape=jax.ShapeDtypeStruct((count, rows, columns), jnp.bfloat16),
        compiler_params=pltpu.CompilerParams(vmem_limit_bytes=SMALL_LIMIT),
        cost_estimate=pl.CostEstimate(flops=0, bytes_accessed=800 * 1024, transcendentals=0),
    )(copies)


def update_kernel(flip, grads, weight, teacher, first, squares, weight_out, teacher_out, first_out, squares_out):
    rows = []
    for index in range(grads.shape[0]):
        swap = ((flip[0] + index) & 1) == 1
        left = jnp.where(swap, grads[index, 1], grads[index, 0])
        right = jnp.where(swap, grads[index, 0], grads[index, 1])
        rows.append(jnp.concatenate([left, right], axis=1))
    grad = jnp.concatenate(rows, axis=0).astype(jnp.float32)
    first_next = 0.9 * first[...] + 0.1 * grad
    squares_next = 0.95 * squares[...] + 0.05 * grad * grad
    held = weight[...]
    weight_next = held - 0.1 * (first_next / (jnp.sqrt(squares_next) + 1e-08) + 0.04 * held)
    weight_out[...] = weight_next
    teacher_out[...] = 0.96 * teacher[...] + 0.04 * weight_next
    first_out[...] = first_next
    squares_out[...] = squares_next


def adamw_update(flip, grads, weight, teacher, first, squares):
    rows = pl.BlockSpec((32, DOUT), lambda i, flip: (i, 0))
    return pl.pallas_call(
        update_kernel,
        grid_spec=pltpu.PrefetchScalarGridSpec(
            num_scalar_prefetch=1,
            grid=(4,),
            in_specs=[pl.BlockSpec((2, 2, 16, DOUT // 2), lambda i, flip: (i, 0, 0, 0))] + [rows] * 4,
            out_specs=[rows] * 4,
        ),
        out_shape=[jax.ShapeDtypeStruct(weight.shape, jnp.float32)] * 4,
        compiler_params=pltpu.CompilerParams(vmem_limit_bytes=VMEM_LIMIT),
    )(flip, grads, weight, teacher, first, squares)


def shards(
    residual,
    student_mix,
    teacher_mix,
    positions,
    layer_scale,
    student_weight,
    teacher_weight,
    moment,
    second,
):
    half = DOUT // 2
    token_count = student_mix.shape[0]
    total_tokens = token_count * 256
    z, xlo, y, xhi, core = (lax.axis_index(name) for name in AXES)
    which = (core + z + xhi + xlo) & 1

    order = jnp.stack(
        [(((y + dy) & 3) * 2 + (xhi ^ dx)) * 2 + (core ^ side) for side, dy, dx in ORDER] + [which, core]
    ).astype(jnp.int32)
    scale = layer_scale.reshape(1, DOUT)
    own = jnp.stack(
        [
            lax.dynamic_slice_in_dim(weight, which * half, half, axis=-1)
            for weight in (student_weight, teacher_weight)
        ]
    ).astype(jnp.bfloat16)

    own, student_sent, teacher_sent, positions_sent, student_held, teacher_held, residual = lax.optimization_barrier(
        (own, student_mix, teacher_mix, positions, student_weight, teacher_weight, residual)
    )
    student_weight, teacher_weight = student_held, teacher_held
    student_other, positions_sent = lax.optimization_barrier((swap_cores(student_sent), positions_sent))
    teacher_other, places_other = swap_cores(teacher_sent), swap_cores(positions_sent)
    up, down, across, student_other, teacher_other, places, places_other, student_held, teacher_held = (
        lax.optimization_barrier(
            (
                from_y_next(own), from_y_previous(own), from_x_near(own), student_other, teacher_other, positions,
                places_other, student_held, teacher_held,
            )
        )
    )
    other_sent = split_weights(order, student_held, teacher_held)
    student_prepared = prepare_student(order, student_mix, student_other)
    (
        up_two, across_down, across_up, passed_up, passed_down, across, other_sent, places, places_other,
        student_prepared, teacher_other, residual,
    ) = lax.optimization_barrier(
        (
            from_y_next(up), from_y_previous(across), from_x_near(up), from_z_next(up), from_z_previous(down), across,
            other_sent, places, places_other, student_prepared,
            teacher_other, residual,
        )
    )
    prepared = prepare_teacher(order, teacher_mix, teacher_other, residual, places, places_other)
    across_two = from_y_next(across_up)
    (
        (student_two, teacher_two), passed_two, passed_across_up, passed_across_down, passed_across, prepared,
        other_sent, residual_sent,
    ) = lax.optimization_barrier(
        (
            both_halves(across_two), from_z_next(up_two), from_z_previous(across_up), from_x_near(passed_down),
            from_x_twin(across), prepared, other_sent, residual,
        )
    )
    student_early, student_late, sent_mix, kept_mix = student_prepared
    teacher_early, teacher_late, picked = prepared
    student_two, teacher_two = from_z_next(student_two), from_z_previous(teacher_two)
    residual_other, picked_other, other = swap_cores(residual_sent), swap_cores(picked), swap_cores(other_sent)
    student_part, teacher_part = early_forward(
        (
            own, up, down, across, up_two, across_down, across_up, passed_up, passed_down, across_two, passed_two,
            passed_across_up, passed_across_down, passed_across,
        ),
        student_early,
        teacher_early,
    )
    student_out, matched, sums = late_forward(
        order, (other, student_two, teacher_two), student_late, teacher_late, student_part, teacher_part, residual,
        residual_other, picked, picked_other, scale
    )
    more_sums = swap_cores(sums)

    def to_neighbours(part, after):
        part_sums, after = lax.optimization_barrier((sums, after))
        *sent, held, tokens_own, tokens_other = send_grads(
            total_tokens, part, order, student_out, matched, part_sums, more_sums, scale, sent_mix
        )
        passed = (from_z_previous(sent[0]), from_z_next(sent[1]), from_x_twin(sent[2]))
        return sent, held, tokens_own, tokens_other, passed

    def over_fsdp(rows):
        return lax.all_to_all(rows, ("xlo", "y", "xhi"), 0, 0, axis_index_groups=FSDP_GROUPS)

    sent, first_held, first_own, first_other, first_passed = to_neighbours(0, more_sums)
    _, last_held, last_own, last_other, last_passed = to_neighbours(1, sent)
    first_kept, last_kept = keep_grads(first_held, kept_mix), keep_grads(last_held, kept_mix)
    first_passed, last_kept, last_other = lax.optimization_barrier((first_passed, last_kept, last_other))
    first_rows, last_kept, last_other = lax.optimization_barrier(
        (add_passed(first_kept, first_passed), last_kept, last_other)
    )
    swapped = swap_cores(first_other), swap_cores(last_other)
    first_chip, last_rows = lax.optimization_barrier((over_fsdp(first_rows), add_passed(last_kept, last_passed)))
    last_chip = over_fsdp(last_rows)
    student_tokens = join_tokens(order, first_own, last_own, *swapped)
    first_chip, last_chip, student_tokens = lax.optimization_barrier((first_chip, last_chip, student_tokens))
    total = total_rows(first_chip, last_chip)
    by_copy = lax.all_to_all(
        total.reshape(8, 16, half), ("z", "xlo"), 0, 0, axis_index_groups=DP_GROUPS
    )
    full = lax.all_to_all(spread_rows(by_copy, 16), ("z", "xlo"), 0, 0)
    flip = ((core + xhi) & 1).astype(jnp.int32).reshape(1)
    weight_next, teacher_next, first_next, squares_next = adamw_update(
        flip, full.reshape(8, 2, 16, half), student_weight, teacher_weight, moment, second
    )
    return (weight_next, teacher_next, first_next, squares_next, student_tokens)


def solution(mesh):
    split = Mesh(mesh.devices.reshape(8, 2, 4, 2, 2), AXES)
    tokens = P(AXES, None)
    owned = P(("y", "xhi", "core"), None)
    return jax.shard_map(
        shards,
        mesh=split,
        in_specs=(tokens, tokens, tokens, tokens, P(), owned, owned, owned, owned),
        out_specs=(owned, owned, owned, owned, tokens),
        check_vma=False,
    )
```

```python
import functools

import jax
import jax.numpy as jnp
from jax import lax
from jax.experimental import pallas as pl
from jax.experimental.pallas import tpu as pltpu
from jax.sharding import Mesh, PartitionSpec as P

KIN = 2048
DOUT = 2048
PATCHES = 144
EPS = 1e-06
AXES = ("z", "xlo", "y", "xhi", "core")
VMEM_LIMIT = 32 * 1024 * 1024
SMALL_LIMIT = 16 * 1024 * 1024

X_INDEX = (0, 2, 1, 3)
CORE_SWAP = ((0, 1), (1, 0))
X_NEAR = tuple((X_INDEX[a], X_INDEX[b]) for a, b in ((1, 2), (2, 1), (0, 3), (3, 0)))


def from_next(size):
    return tuple(((i + 1) % size, i) for i in range(size))


def from_previous(size):
    return tuple((i, (i + 1) % size) for i in range(size))


def with_core_flip(pairs):
    return tuple((2 * a + 1 - core, 2 * b + core) for a, b in pairs for core in range(2))


FSDP_GROUPS = tuple(
    tuple((xhi ^ side) * 8 + y * 2 + xhi for y in range(4) for xhi in range(2)) for side in range(2)
)
DP_GROUPS = tuple(tuple(z * 2 + ((z + side) & 1) for z in range(8)) for side in range(2))


def swap_cores(value):
    return lax.ppermute(value, "core", CORE_SWAP)


def from_y_next(value):
    return lax.ppermute(value, "y", from_next(4))


def from_y_previous(value):
    return lax.ppermute(value, "y", from_previous(4))


def from_x_near(value):
    return lax.ppermute(value, ("xlo", "xhi"), X_NEAR)


def from_z_next(value):
    return lax.ppermute(value, ("z", "core"), with_core_flip(from_next(8)))


def from_z_previous(value):
    return lax.ppermute(value, ("z", "core"), with_core_flip(from_previous(8)))


def from_x_twin(value):
    return lax.ppermute(value, ("xlo", "core"), with_core_flip(CORE_SWAP))


ORDER = (
    (0, 0, 0), (0, 1, 0), (0, 3, 0), (0, 0, 1), (0, 2, 0), (0, 3, 1), (0, 1, 1), (1, 1, 0), (1, 3, 0), (0, 2, 1),
    (1, 2, 0), (1, 1, 1), (1, 3, 1), (1, 0, 1), (1, 0, 0), (1, 2, 1),
)
EARLY = 14
LATE = len(ORDER) - EARLY
HALF_AT = len(ORDER)
CORE_AT = HALF_AT + 1
SENT = (3, 3, 2)
TILE = 256
PARTS = (1, 3)


def split_kernel(order, student, teacher, out):
    out[0] = student[...].astype(jnp.bfloat16)
    out[1] = teacher[...].astype(jnp.bfloat16)


def split_weights(order, student, teacher):
    rows, width, steps = student.shape[0], 512, 2

    def half(j, order):
        return (0, (order[HALF_AT] ^ 1) * steps + j)

    return pl.pallas_call(
        split_kernel,
        grid_spec=pltpu.PrefetchScalarGridSpec(
            num_scalar_prefetch=1,
            grid=(steps,),
            in_specs=[pl.BlockSpec((rows, width), half)] * 2,
            out_specs=pl.BlockSpec((2, rows, width), lambda j, order: (0, 0, j)),
        ),
        out_shape=jax.ShapeDtypeStruct((2, rows, width * steps), jnp.bfloat16),
        compiler_params=pltpu.CompilerParams(vmem_limit_bytes=SMALL_LIMIT),
        cost_estimate=pl.CostEstimate(flops=0, bytes_accessed=1536 * 1024, transcendentals=0),
    )(order, student, teacher)


def halves_kernel(pair, first, second):
    first[...] = pair[0]
    second[...] = pair[1]


def both_halves(pair):
    _, rows, columns = pair.shape
    return pl.pallas_call(
        halves_kernel,
        out_shape=[jax.ShapeDtypeStruct((rows, columns), pair.dtype)] * 2,
        compiler_params=pltpu.CompilerParams(vmem_limit_bytes=SMALL_LIMIT),
        cost_estimate=pl.CostEstimate(flops=0, bytes_accessed=1024 * 1024, transcendentals=0),
    )(pair)


def place_blocks(order, step, packed, early, late):
    for part in range(2):
        columns = slice(part * 128, (part + 1) * 128)
        for block in range(len(ORDER)):
            @pl.when(order[block] == 2 * step + part)
            def _():
                if block < EARLY:
                    early[:, block * 128 : (block + 1) * 128] = packed[:, columns]
                else:
                    late[:, (block - EARLY) * 128 : (block - EARLY + 1) * 128] = packed[:, columns]


def student_kernel(order, mix_own, mix_other, early, late, sent_out, kept_out, turned, packed):
    own = mix_own.shape[0]
    packed[:own, :] = mix_own[...]
    packed[own:, :] = mix_other[...]
    turned[...] = packed[...].T
    core = order[CORE_AT]
    kept_out[0] = turned[pl.ds(pl.multiple_of(core * 128, 128), 128), :]
    sent_out[0] = turned[pl.ds(pl.multiple_of((1 - core) * 128, 128), 128), :]
    place_blocks(order, pl.program_id(0), packed, early, late)


def teacher_kernel(
    order, mix_own, mix_other, residual, places_own, places_other, early, late, picked_out, packed, picks
):
    own, step = mix_own.shape[0], pl.program_id(0)
    crops = own // PATCHES

    @pl.when(step == 0)
    def _():
        source = lax.broadcasted_iota(jnp.int32, (PATCHES, PATCHES), 0)
        for side, places in enumerate((places_own, places_other)):
            for crop in range(crops):
                chosen = jnp.where(places[crop : crop + 1, :] == source, 1.0, 0.0)
                picks[side * crops + crop] = chosen.T.astype(jnp.bfloat16)

    for side, mix in enumerate((mix_own, mix_other)):
        for crop in range(crops):
            rows = slice(crop * PATCHES, (crop + 1) * PATCHES)
            at = side * crops + crop
            packed[at * PATCHES : (at + 1) * PATCHES, :] = jnp.dot(
                picks[at], mix[rows, :], preferred_element_type=jnp.float32
            ).astype(jnp.bfloat16)
            if side == 0:
                picked_out[rows, :] = jnp.dot(
                    picks[at], residual[rows, :], preferred_element_type=jnp.float32
                ).astype(jnp.bfloat16)
    place_blocks(order, step, packed, early, late)


def prepare_student(order, mix_own, mix_other):
    own, steps = mix_own.shape[0], 8
    rows, width = 2 * own, KIN // steps
    mix = pl.BlockSpec((own, width), lambda i, order: (0, i))
    turned = pl.BlockSpec((1, 128, rows), lambda i, order: (i, 0, 0))
    return pl.pallas_call(
        student_kernel,
        grid_spec=pltpu.PrefetchScalarGridSpec(
            num_scalar_prefetch=1,
            grid=(steps,),
            in_specs=[mix] * 2,
            out_specs=[
                pl.BlockSpec((rows, EARLY * 128), lambda i, order: (0, 0)),
                pl.BlockSpec((rows, LATE * 128), lambda i, order: (0, 0)),
                turned,
                turned,
            ],
            scratch_shapes=[pltpu.VMEM((width, rows), jnp.bfloat16), pltpu.VMEM((rows, width), jnp.bfloat16)],
        ),
        out_shape=[
            jax.ShapeDtypeStruct((rows, EARLY * 128), jnp.bfloat16),
            jax.ShapeDtypeStruct((rows, LATE * 128), jnp.bfloat16),
            jax.ShapeDtypeStruct((8, 128, rows), jnp.bfloat16),
            jax.ShapeDtypeStruct((8, 128, rows), jnp.bfloat16),
        ],
        compiler_params=pltpu.CompilerParams(vmem_limit_bytes=VMEM_LIMIT),
        cost_estimate=pl.CostEstimate(flops=0, bytes_accessed=7 * 1024 * 1024, transcendentals=0),
    )(order, mix_own, mix_other)


def prepare_teacher(order, mix_own, mix_other, residual, places, places_other):
    own, steps = mix_own.shape[0], 8
    rows, width = 2 * own, KIN // steps
    mix = pl.BlockSpec((own, width), lambda i, order: (0, i))
    place = pl.BlockSpec(places.shape, lambda i, order: (0, 0))
    return pl.pallas_call(
        teacher_kernel,
        grid_spec=pltpu.PrefetchScalarGridSpec(
            num_scalar_prefetch=1,
            grid=(steps,),
            in_specs=[mix] * 3 + [place] * 2,
            out_specs=[
                pl.BlockSpec((rows, EARLY * 128), lambda i, order: (0, 0)),
                pl.BlockSpec((rows, LATE * 128), lambda i, order: (0, 0)),
                mix,
            ],
            scratch_shapes=[
                pltpu.VMEM((rows, width), jnp.bfloat16),
                pltpu.VMEM((rows // PATCHES, PATCHES, PATCHES), jnp.bfloat16),
            ],
        ),
        out_shape=[
            jax.ShapeDtypeStruct((rows, EARLY * 128), jnp.bfloat16),
            jax.ShapeDtypeStruct((rows, LATE * 128), jnp.bfloat16),
            jax.ShapeDtypeStruct((own, DOUT), jnp.bfloat16),
        ],
        compiler_params=pltpu.CompilerParams(vmem_limit_bytes=VMEM_LIMIT),
        cost_estimate=pl.CostEstimate(
            flops=3 * rows * PATCHES * KIN, bytes_accessed=9 * 1024 * 1024, transcendentals=0
        ),
    )(order, mix_own, mix_other, residual, places, places_other)


def early_kernel(student_mix, teacher_mix, *refs):
    weights, (student_out, teacher_out, held) = refs[:EARLY], refs[EARLY:]
    for block in range(EARLY):
        rows = slice(block * 128, (block + 1) * 128)
        held[0, rows, :] = weights[block][0]
        held[1, rows, :] = weights[block][1]
    student_out[...] = jnp.dot(student_mix[...], held[0], preferred_element_type=jnp.float32)
    teacher_out[...] = jnp.dot(teacher_mix[...], held[1], preferred_element_type=jnp.float32)


def early_forward(pieces, student_mix, teacher_mix):
    rows, depth = student_mix.shape
    columns, width = pieces[0].shape[-1], 256
    whole = pl.BlockSpec((rows, depth), lambda j: (0, 0))
    column = pl.BlockSpec((rows, width), lambda j: (0, j))
    return pl.pallas_call(
        early_kernel,
        grid=(columns // width,),
        in_specs=[whole, whole] + [pl.BlockSpec((2, 128, width), lambda j: (0, 0, j))] * EARLY,
        out_specs=[column, column],
        out_shape=[jax.ShapeDtypeStruct((rows, columns), jnp.float32)] * 2,
        scratch_shapes=[pltpu.VMEM((2, depth, width), jnp.bfloat16)],
        compiler_params=pltpu.CompilerParams(vmem_limit_bytes=VMEM_LIMIT),
        cost_estimate=pl.CostEstimate(
            flops=4 * rows * depth * columns, bytes_accessed=17 * 1024 * 1024, transcendentals=0
        ),
    )(student_mix, teacher_mix, *pieces)


def late_kernel(
    order, student_mix, teacher_mix, student_part, teacher_part, residual_own, residual_other, picked_own, picked_other,
    scale, *refs
):
    pair, student_weight, teacher_weight, student_out, matched_out, sums_out, held = refs
    held[:, :128, :] = pair[...]
    held[0, 128:, :] = student_weight[...]
    held[1, 128:, :] = teacher_weight[...]
    factor = scale[...] * (KIN ** (-0.5))
    student_sum = student_part[...] + jnp.dot(student_mix[...], held[0], preferred_element_type=jnp.float32)
    teacher_sum = teacher_part[...] + jnp.dot(teacher_mix[...], held[1], preferred_element_type=jnp.float32)
    own = residual_own.shape[0]
    first = pl.program_id(0) == 0
    for side, (residual, picked) in enumerate(((residual_own, picked_own), (residual_other, picked_other))):
        tokens = slice(side * own, (side + 1) * own)
        student = residual[...].astype(jnp.float32) + factor * student_sum[tokens]
        matched = picked[...].astype(jnp.float32) + factor * teacher_sum[tokens]
        student_out[tokens, :] = student
        matched_out[tokens, :] = matched
        spot = lax.broadcasted_iota(jnp.int32, (own, 128), 1)
        sums = jnp.where(
            spot == 0,
            jnp.sum(student * student, axis=-1, keepdims=True),
            jnp.where(
                spot == 1,
                jnp.sum(matched * matched, axis=-1, keepdims=True),
                jnp.where(spot == 2, jnp.sum(student * matched, axis=-1, keepdims=True), 0.0),
            ),
        )
        sums_out[tokens, :] = sums + jnp.where(first, 0.0, sums_out[tokens, :])


def late_forward(
    order, pieces, student_mix, teacher_mix, student_part, teacher_part, residual, residual_other, picked, picked_other,
    scale
):
    (rows, columns), own, width = student_part.shape, residual.shape[0], 256
    steps = columns // width
    whole = pl.BlockSpec((rows, LATE * 128), lambda j, order: (0, 0))
    column = pl.BlockSpec((rows, width), lambda j, order: (0, j))
    tokens = pl.BlockSpec((own, width), lambda j, order: (0, order[HALF_AT] * steps + j))
    return pl.pallas_call(
        late_kernel,
        grid_spec=pltpu.PrefetchScalarGridSpec(
            num_scalar_prefetch=1,
            grid=(steps,),
            in_specs=[whole, whole, column, column]
            + [tokens] * 4
            + [pl.BlockSpec((1, width), lambda j, order: (0, order[HALF_AT] * steps + j))]
            + [pl.BlockSpec((2, 128, width), lambda j, order: (0, 0, j))]
            + [pl.BlockSpec((128, width), lambda j, order: (0, j))] * 2,
            out_specs=[column, column, pl.BlockSpec((rows, 128), lambda j, order: (0, 0))],
            scratch_shapes=[pltpu.VMEM((2, LATE * 128, width), jnp.bfloat16)],
        ),
        out_shape=[
            jax.ShapeDtypeStruct((rows, columns), jnp.float32),
            jax.ShapeDtypeStruct((rows, columns), jnp.float32),
            jax.ShapeDtypeStruct((rows, 128), jnp.float32),
        ],
        compiler_params=pltpu.CompilerParams(vmem_limit_bytes=VMEM_LIMIT),
        cost_estimate=pl.CostEstimate(
            flops=4 * rows * LATE * 128 * columns, bytes_accessed=13 * 1024 * 1024, transcendentals=0
        ),
    )(
        order, student_mix, teacher_mix, student_part, teacher_part, residual, residual_other, picked, picked_other,
        scale, *pieces
    )


def send_kernel(
    total_tokens, order, student, matched, sums, more_sums, scale, mix, next_out, previous_out, twin_out, held_out,
    tokens_own, tokens_other
):
    own = more_sums.shape[0] // 2
    swapped = jnp.concatenate([more_sums[own:, :], more_sums[:own, :]], axis=0)
    total = (sums[...] + swapped) * (1.0 / DOUT)
    inverse_rms = lax.rsqrt(total[:, 0:1] + EPS)
    inverse_matched = lax.rsqrt(total[:, 1:2] + EPS)
    overlap = inverse_rms * inverse_matched * total[:, 2:3]
    shared = inverse_rms * (1.0 / total_tokens)
    student_part = shared * inverse_rms * (EPS * inverse_rms * inverse_rms + overlap)
    matched_part = shared * inverse_matched
    values = student[...]
    tokens = (values * inverse_rms).astype(jnp.bfloat16)
    tokens_own[...] = tokens[:own]
    tokens_other[...] = tokens[own:]
    factor = scale[...] * (KIN ** (-0.5))
    held_out[...] = (factor * (values * student_part - matched[...] * matched_part)).astype(jnp.bfloat16)
    at = 0
    for out in (next_out, previous_out, twin_out):
        count = out.shape[0]
        grad = jnp.dot(
            mix[at : at + count].reshape(count * 128, mix.shape[-1]),
            held_out[...],
            preferred_element_type=jnp.float32,
        )
        out[...] = grad.astype(jnp.bfloat16).reshape(out.shape)
        at += count


def send_grads(total_tokens, part, order, student, matched, sums, more_sums, scale, turned):
    rows, columns = student.shape
    steps, count, first = columns // TILE, PARTS[part], sum(PARTS[:part])
    column = pl.BlockSpec((rows, TILE), lambda j, order: (0, first + j))
    narrow = pl.BlockSpec((rows, 128), lambda j, order: (0, 0))
    out = pl.BlockSpec((rows, TILE), lambda j, order: (0, j))
    half = pl.BlockSpec((rows // 2, TILE), lambda j, order: (0, j))
    return pl.pallas_call(
        functools.partial(send_kernel, total_tokens),
        grid_spec=pltpu.PrefetchScalarGridSpec(
            num_scalar_prefetch=1,
            grid=(count,),
            in_specs=[
                column,
                column,
                narrow,
                narrow,
                pl.BlockSpec((1, TILE), lambda j, order: (0, order[HALF_AT] * steps + first + j)),
                pl.BlockSpec((8, 128, rows), lambda j, order: (0, 0, 0)),
            ],
            out_specs=[pl.BlockSpec((size, 128, TILE), lambda j, order: (0, 0, j)) for size in SENT]
            + [out, half, half],
        ),
        out_shape=[jax.ShapeDtypeStruct((size, 128, count * TILE), jnp.bfloat16) for size in SENT]
        + [
            jax.ShapeDtypeStruct((rows, count * TILE), jnp.bfloat16),
            jax.ShapeDtypeStruct((rows // 2, count * TILE), jnp.bfloat16),
            jax.ShapeDtypeStruct((rows // 2, count * TILE), jnp.bfloat16),
        ],
        compiler_params=pltpu.CompilerParams(vmem_limit_bytes=VMEM_LIMIT),
        cost_estimate=pl.CostEstimate(
            flops=rows * KIN * count * TILE, bytes_accessed=3 * count * 1024 * 1024, transcendentals=0
        ),
    )(order, student, matched, sums, more_sums, scale, turned)


def keep_kernel(held, mix, out):
    grad = jnp.dot(
        mix[...].reshape(8 * 128, mix.shape[-1]), held[...], preferred_element_type=jnp.float32
    )
    out[...] = grad.reshape(out.shape)


def keep_grads(held, kept):
    (rows, columns), width = held.shape, 256
    return pl.pallas_call(
        keep_kernel,
        grid=(columns // width,),
        in_specs=[
            pl.BlockSpec((rows, width), lambda j: (0, j)),
            pl.BlockSpec((8, 128, rows), lambda j: (0, 0, 0)),
        ],
        out_specs=pl.BlockSpec((8, 128, width), lambda j: (0, 0, j)),
        out_shape=jax.ShapeDtypeStruct((8, 128, columns), jnp.float32),
        compiler_params=pltpu.CompilerParams(vmem_limit_bytes=VMEM_LIMIT),
        cost_estimate=pl.CostEstimate(
            flops=rows * KIN * columns, bytes_accessed=7 * 1024 * 1024, transcendentals=0
        ),
    )(held, kept)


def add_kernel(kept, *refs):
    passed, out = refs[:-1], refs[-1]
    at = 0
    for part in passed:
        spot = slice(at, at + part.shape[0])
        out[spot] = (kept[spot] + part[...].astype(jnp.float32)).astype(jnp.bfloat16)
        at += part.shape[0]


def add_passed(kept, passed):
    width = 256

    def blocks(count):
        return pl.BlockSpec((count, 128, width), lambda j: (0, 0, j))

    return pl.pallas_call(
        add_kernel,
        grid=(kept.shape[-1] // width,),
        in_specs=[blocks(8)] + [blocks(count) for count in SENT],
        out_specs=blocks(8),
        out_shape=jax.ShapeDtypeStruct(kept.shape, jnp.bfloat16),
        compiler_params=pltpu.CompilerParams(vmem_limit_bytes=VMEM_LIMIT),
    )(kept, *passed)


def join_kernel(order, first_own, last_own, first_other, last_other, out):
    step, width = pl.program_id(0), first_own.shape[1]
    for at, (first, last) in enumerate(((first_own, last_own), (first_other, last_other))):
        @pl.when(step == (at ^ order[HALF_AT]))
        def _():
            out[:, :width] = first[...]
            out[:, width:] = last[...]


def join_tokens(order, first_own, last_own, first_other, last_other):
    rows, half = first_own.shape[0], first_own.shape[1] + last_own.shape[1]
    first = pl.BlockSpec(first_own.shape, lambda j, order: (0, 0))
    last = pl.BlockSpec(last_own.shape, lambda j, order: (0, 0))
    return pl.pallas_call(
        join_kernel,
        grid_spec=pltpu.PrefetchScalarGridSpec(
            num_scalar_prefetch=1,
            grid=(2,),
            in_specs=[first, last, first, last],
            out_specs=pl.BlockSpec((rows, half), lambda j, order: (0, j)),
        ),
        out_shape=jax.ShapeDtypeStruct((rows, 2 * half), jnp.bfloat16),
        compiler_params=pltpu.CompilerParams(vmem_limit_bytes=SMALL_LIMIT),
        cost_estimate=pl.CostEstimate(flops=0, bytes_accessed=2400 * 1024, transcendentals=0),
    )(order, first_own, last_own, first_other, last_other)


def total_kernel(first, last, out):
    at = 0
    for chips in (first, last):
        total = chips[0].astype(jnp.float32)
        for chip in range(1, chips.shape[0]):
            total = total + chips[chip].astype(jnp.float32)
        out[:, at : at + total.shape[1]] = total.astype(jnp.bfloat16)
        at += total.shape[1]


def total_rows(first, last):
    chips, rows, _ = first.shape
    parts = [pl.BlockSpec((chips, rows // 2, part.shape[-1]), lambda i: (0, i, 0)) for part in (first, last)]
    columns = first.shape[-1] + last.shape[-1]
    return pl.pallas_call(
        total_kernel,
        grid=(2,),
        in_specs=parts,
        out_specs=pl.BlockSpec((rows // 2, columns), lambda i: (i, 0)),
        out_shape=jax.ShapeDtypeStruct((rows, columns), jnp.bfloat16),
        compiler_params=pltpu.CompilerParams(vmem_limit_bytes=SMALL_LIMIT),
        cost_estimate=pl.CostEstimate(flops=0, bytes_accessed=2400 * 1024, transcendentals=0),
    )(first, last)


def spread_kernel(copies, out):
    total = copies[0].astype(jnp.float32)
    for copy in range(1, copies.shape[0]):
        total = total + copies[copy].astype(jnp.float32)
    out[...] = jnp.broadcast_to(total.astype(jnp.bfloat16)[None], out.shape)


def spread_rows(copies, count):
    _, rows, columns = copies.shape
    return pl.pallas_call(
        spread_kernel,
        out_shape=jax.ShapeDtypeStruct((count, rows, columns), jnp.bfloat16),
        compiler_params=pltpu.CompilerParams(vmem_limit_bytes=SMALL_LIMIT),
        cost_estimate=pl.CostEstimate(flops=0, bytes_accessed=800 * 1024, transcendentals=0),
    )(copies)


def update_kernel(flip, grads, weight, teacher, first, squares, weight_out, teacher_out, first_out, squares_out):
    rows = []
    for index in range(grads.shape[0]):
        swap = ((flip[0] + index) & 1) == 1
        left = jnp.where(swap, grads[index, 1], grads[index, 0])
        right = jnp.where(swap, grads[index, 0], grads[index, 1])
        rows.append(jnp.concatenate([left, right], axis=1))
    grad = jnp.concatenate(rows, axis=0).astype(jnp.float32)
    first_next = 0.9 * first[...] + 0.1 * grad
    squares_next = 0.95 * squares[...] + 0.05 * grad * grad
    held = weight[...]
    weight_next = held - 0.1 * (first_next / (jnp.sqrt(squares_next) + 1e-08) + 0.04 * held)
    weight_out[...] = weight_next
    teacher_out[...] = 0.96 * teacher[...] + 0.04 * weight_next
    first_out[...] = first_next
    squares_out[...] = squares_next


def adamw_update(flip, grads, weight, teacher, first, squares):
    rows = pl.BlockSpec((32, DOUT), lambda i, flip: (i, 0))
    return pl.pallas_call(
        update_kernel,
        grid_spec=pltpu.PrefetchScalarGridSpec(
            num_scalar_prefetch=1,
            grid=(4,),
            in_specs=[pl.BlockSpec((2, 2, 16, DOUT // 2), lambda i, flip: (i, 0, 0, 0))] + [rows] * 4,
            out_specs=[rows] * 4,
        ),
        out_shape=[jax.ShapeDtypeStruct(weight.shape, jnp.float32)] * 4,
        compiler_params=pltpu.CompilerParams(vmem_limit_bytes=VMEM_LIMIT),
    )(flip, grads, weight, teacher, first, squares)


def shards(
    residual,
    student_mix,
    teacher_mix,
    positions,
    layer_scale,
    student_weight,
    teacher_weight,
    moment,
    second,
):
    half = DOUT // 2
    token_count = student_mix.shape[0]
    total_tokens = token_count * 256
    z, xlo, y, xhi, core = (lax.axis_index(name) for name in AXES)
    which = (core + z + xhi + xlo) & 1

    order = jnp.stack(
        [(((y + dy) & 3) * 2 + (xhi ^ dx)) * 2 + (core ^ side) for side, dy, dx in ORDER] + [which, core]
    ).astype(jnp.int32)
    scale = layer_scale.reshape(1, DOUT)
    own = jnp.stack(
        [
            lax.dynamic_slice_in_dim(weight, which * half, half, axis=-1)
            for weight in (student_weight, teacher_weight)
        ]
    ).astype(jnp.bfloat16)

    own, student_sent, teacher_sent, positions_sent, student_held, teacher_held, residual = lax.optimization_barrier(
        (own, student_mix, teacher_mix, positions, student_weight, teacher_weight, residual)
    )
    student_weight, teacher_weight = student_held, teacher_held
    student_other, positions_sent = lax.optimization_barrier((swap_cores(student_sent), positions_sent))
    teacher_other, places_other = swap_cores(teacher_sent), swap_cores(positions_sent)
    up, down, across, student_other, teacher_other, places, places_other, student_held, teacher_held = (
        lax.optimization_barrier(
            (
                from_y_next(own), from_y_previous(own), from_x_near(own), student_other, teacher_other, positions,
                places_other, student_held, teacher_held,
            )
        )
    )
    other_sent = split_weights(order, student_held, teacher_held)
    student_prepared = prepare_student(order, student_mix, student_other)
    (
        up_two, across_down, across_up, passed_up, passed_down, across, other_sent, places, places_other,
        student_prepared, teacher_other, residual,
    ) = lax.optimization_barrier(
        (
            from_y_next(up), from_y_previous(across), from_x_near(up), from_z_next(up), from_z_previous(down), across,
            other_sent, places, places_other, student_prepared,
            teacher_other, residual,
        )
    )
    prepared = prepare_teacher(order, teacher_mix, teacher_other, residual, places, places_other)
    across_two = from_y_next(across_up)
    (
        (student_two, teacher_two), passed_two, passed_across_up, passed_across_down, passed_across, prepared,
        other_sent, residual_sent,
    ) = lax.optimization_barrier(
        (
            both_halves(across_two), from_z_next(up_two), from_z_previous(across_up), from_x_near(passed_down),
            from_x_twin(across), prepared, other_sent, residual,
        )
    )
    student_early, student_late, sent_mix, kept_mix = student_prepared
    teacher_early, teacher_late, picked = prepared
    student_two, teacher_two = from_z_next(student_two), from_z_previous(teacher_two)
    residual_other, picked_other, other = swap_cores(residual_sent), swap_cores(picked), swap_cores(other_sent)
    student_part, teacher_part = early_forward(
        (
            own, up, down, across, up_two, across_down, across_up, passed_up, passed_down, across_two, passed_two,
            passed_across_up, passed_across_down, passed_across,
        ),
        student_early,
        teacher_early,
    )
    student_out, matched, sums = late_forward(
        order, (other, student_two, teacher_two), student_late, teacher_late, student_part, teacher_part, residual,
        residual_other, picked, picked_other, scale
    )
    more_sums = swap_cores(sums)

    def to_neighbours(part, after):
        part_sums, after = lax.optimization_barrier((sums, after))
        *sent, held, tokens_own, tokens_other = send_grads(
            total_tokens, part, order, student_out, matched, part_sums, more_sums, scale, sent_mix
        )
        passed = (from_z_previous(sent[0]), from_z_next(sent[1]), from_x_twin(sent[2]))
        return sent, held, tokens_own, tokens_other, passed

    def over_fsdp(rows):
        return lax.all_to_all(rows, ("xlo", "y", "xhi"), 0, 0, axis_index_groups=FSDP_GROUPS)

    sent, first_held, first_own, first_other, first_passed = to_neighbours(0, more_sums)
    _, last_held, last_own, last_other, last_passed = to_neighbours(1, sent)
    first_kept, last_kept = keep_grads(first_held, kept_mix), keep_grads(last_held, kept_mix)
    first_passed, last_kept, last_other = lax.optimization_barrier((first_passed, last_kept, last_other))
    first_rows, last_kept, last_other = lax.optimization_barrier(
        (add_passed(first_kept, first_passed), last_kept, last_other)
    )
    swapped = swap_cores(first_other), swap_cores(last_other)
    first_chip, last_rows = lax.optimization_barrier((over_fsdp(first_rows), add_passed(last_kept, last_passed)))
    last_chip = over_fsdp(last_rows)
    student_tokens = join_tokens(order, first_own, last_own, *swapped)
    first_chip, last_chip, student_tokens = lax.optimization_barrier((first_chip, last_chip, student_tokens))
    total = total_rows(first_chip, last_chip)
    by_copy = lax.all_to_all(
        total.reshape(8, 16, half), ("z", "xlo"), 0, 0, axis_index_groups=DP_GROUPS
    )
    full = lax.all_to_all(spread_rows(by_copy, 16), ("z", "xlo"), 0, 0)
    flip = ((core + xhi) & 1).astype(jnp.int32).reshape(1)
    weight_next, teacher_next, first_next, squares_next = adamw_update(
        flip, full.reshape(8, 2, 16, half), student_weight, teacher_weight, moment, second
    )
    return (weight_next, teacher_next, first_next, squares_next, student_tokens)


def solution(mesh):
    split = Mesh(mesh.devices.reshape(8, 2, 4, 2, 2), AXES)
    tokens = P(AXES, None)
    owned = P(("y", "xhi", "core"), None)
    return jax.shard_map(
        shards,
        mesh=split,
        in_specs=(tokens, tokens, tokens, tokens, P(), owned, owned, owned, owned),
        out_specs=(owned, owned, owned, owned, tokens),
        check_vma=False,
    )
```

```python
import functools

import jax
import jax.numpy as jnp
from jax import lax
from jax.experimental import pallas as pl
from jax.experimental.pallas import tpu as pltpu
from jax.sharding import Mesh, PartitionSpec as P

KIN = 2048
DOUT = 2048
PATCHES = 144
EPS = 1e-06
AXES = ("z", "xlo", "y", "xhi", "core")
VMEM_LIMIT = 32 * 1024 * 1024
SMALL_LIMIT = 16 * 1024 * 1024

X_INDEX = (0, 2, 1, 3)
CORE_SWAP = ((0, 1), (1, 0))
X_NEAR = tuple((X_INDEX[a], X_INDEX[b]) for a, b in ((1, 2), (2, 1), (0, 3), (3, 0)))


def from_next(size):
    return tuple(((i + 1) % size, i) for i in range(size))


def from_previous(size):
    return tuple((i, (i + 1) % size) for i in range(size))


def with_core_flip(pairs):
    return tuple((2 * a + 1 - core, 2 * b + core) for a, b in pairs for core in range(2))


FSDP_GROUPS = tuple(
    tuple((xhi ^ side) * 8 + y * 2 + xhi for y in range(4) for xhi in range(2)) for side in range(2)
)
DP_GROUPS = tuple(tuple(z * 2 + ((z + side) & 1) for z in range(8)) for side in range(2))


def swap_cores(value):
    return lax.ppermute(value, "core", CORE_SWAP)


def from_y_next(value):
    return lax.ppermute(value, "y", from_next(4))


def from_y_previous(value):
    return lax.ppermute(value, "y", from_previous(4))


def from_x_near(value):
    return lax.ppermute(value, ("xlo", "xhi"), X_NEAR)


def from_z_next(value):
    return lax.ppermute(value, ("z", "core"), with_core_flip(from_next(8)))


def from_z_previous(value):
    return lax.ppermute(value, ("z", "core"), with_core_flip(from_previous(8)))


def from_x_twin(value):
    return lax.ppermute(value, ("xlo", "core"), with_core_flip(CORE_SWAP))


ORDER = (
    (0, 0, 0), (0, 1, 0), (0, 3, 0), (0, 0, 1), (0, 2, 0), (0, 3, 1), (0, 1, 1), (1, 1, 0), (1, 3, 0), (0, 2, 1),
    (1, 2, 0), (1, 1, 1), (1, 3, 1), (1, 0, 1), (1, 0, 0), (1, 2, 1),
)
EARLY = 14
LATE = len(ORDER) - EARLY
HALF_AT = len(ORDER)
CORE_AT = HALF_AT + 1
SENT = (3, 3, 2)
PADDED = (SENT, (3, 3, 3))
TILE = 256
PARTS = (1, 3)


def split_kernel(order, student, teacher, out):
    out[0] = student[...].astype(jnp.bfloat16)
    out[1] = teacher[...].astype(jnp.bfloat16)


def split_weights(order, student, teacher):
    rows, width, steps = student.shape[0], 512, 2

    def half(j, order):
        return (0, (order[HALF_AT] ^ 1) * steps + j)

    return pl.pallas_call(
        split_kernel,
        grid_spec=pltpu.PrefetchScalarGridSpec(
            num_scalar_prefetch=1,
            grid=(steps,),
            in_specs=[pl.BlockSpec((rows, width), half)] * 2,
            out_specs=pl.BlockSpec((2, rows, width), lambda j, order: (0, 0, j)),
        ),
        out_shape=jax.ShapeDtypeStruct((2, rows, width * steps), jnp.bfloat16),
        compiler_params=pltpu.CompilerParams(vmem_limit_bytes=SMALL_LIMIT),
        cost_estimate=pl.CostEstimate(flops=0, bytes_accessed=1536 * 1024, transcendentals=0),
    )(order, student, teacher)


def halves_kernel(pair, first, second):
    first[...] = pair[0]
    second[...] = pair[1]


def both_halves(pair):
    _, rows, columns = pair.shape
    return pl.pallas_call(
        halves_kernel,
        out_shape=[jax.ShapeDtypeStruct((rows, columns), pair.dtype)] * 2,
        compiler_params=pltpu.CompilerParams(vmem_limit_bytes=SMALL_LIMIT),
        cost_estimate=pl.CostEstimate(flops=0, bytes_accessed=1024 * 1024, transcendentals=0),
    )(pair)


def place_blocks(order, step, packed, early, late):
    for part in range(2):
        columns = slice(part * 128, (part + 1) * 128)
        for block in range(len(ORDER)):
            @pl.when(order[block] == 2 * step + part)
            def _():
                if block < EARLY:
                    early[:, block * 128 : (block + 1) * 128] = packed[:, columns]
                else:
                    late[:, (block - EARLY) * 128 : (block - EARLY + 1) * 128] = packed[:, columns]


def student_kernel(order, mix_own, mix_other, early, late, sent_out, kept_out, turned, packed):
    own = mix_own.shape[0]
    packed[:own, :] = mix_own[...]
    packed[own:, :] = mix_other[...]
    turned[...] = packed[...].T
    core = order[CORE_AT]
    kept_out[0] = turned[pl.ds(pl.multiple_of(core * 128, 128), 128), :]
    sent_out[0] = turned[pl.ds(pl.multiple_of((1 - core) * 128, 128), 128), :]
    place_blocks(order, pl.program_id(0), packed, early, late)


def teacher_kernel(
    order, mix_own, mix_other, residual, places_own, places_other, early, late, picked_out, packed, picks
):
    own, step = mix_own.shape[0], pl.program_id(0)
    crops = own // PATCHES

    @pl.when(step == 0)
    def _():
        source = lax.broadcasted_iota(jnp.int32, (PATCHES, PATCHES), 0)
        for side, places in enumerate((places_own, places_other)):
            for crop in range(crops):
                chosen = jnp.where(places[crop : crop + 1, :] == source, 1.0, 0.0)
                picks[side * crops + crop] = chosen.T.astype(jnp.bfloat16)

    for side, mix in enumerate((mix_own, mix_other)):
        for crop in range(crops):
            rows = slice(crop * PATCHES, (crop + 1) * PATCHES)
            at = side * crops + crop
            packed[at * PATCHES : (at + 1) * PATCHES, :] = jnp.dot(
                picks[at], mix[rows, :], preferred_element_type=jnp.float32
            ).astype(jnp.bfloat16)
            if side == 0:
                picked_out[rows, :] = jnp.dot(
                    picks[at], residual[rows, :], preferred_element_type=jnp.float32
                ).astype(jnp.bfloat16)
    place_blocks(order, step, packed, early, late)


def prepare_student(order, mix_own, mix_other):
    own, steps = mix_own.shape[0], 8
    rows, width = 2 * own, KIN // steps
    mix = pl.BlockSpec((own, width), lambda i, order: (0, i))
    turned = pl.BlockSpec((1, 128, rows), lambda i, order: (i, 0, 0))
    return pl.pallas_call(
        student_kernel,
        grid_spec=pltpu.PrefetchScalarGridSpec(
            num_scalar_prefetch=1,
            grid=(steps,),
            in_specs=[mix] * 2,
            out_specs=[
                pl.BlockSpec((rows, EARLY * 128), lambda i, order: (0, 0)),
                pl.BlockSpec((rows, LATE * 128), lambda i, order: (0, 0)),
                turned,
                turned,
            ],
            scratch_shapes=[pltpu.VMEM((width, rows), jnp.bfloat16), pltpu.VMEM((rows, width), jnp.bfloat16)],
        ),
        out_shape=[
            jax.ShapeDtypeStruct((rows, EARLY * 128), jnp.bfloat16),
            jax.ShapeDtypeStruct((rows, LATE * 128), jnp.bfloat16),
            jax.ShapeDtypeStruct((8, 128, rows), jnp.bfloat16),
            jax.ShapeDtypeStruct((8, 128, rows), jnp.bfloat16),
        ],
        compiler_params=pltpu.CompilerParams(vmem_limit_bytes=VMEM_LIMIT),
        cost_estimate=pl.CostEstimate(flops=0, bytes_accessed=7 * 1024 * 1024, transcendentals=0),
    )(order, mix_own, mix_other)


def prepare_teacher(order, mix_own, mix_other, residual, places, places_other):
    own, steps = mix_own.shape[0], 8
    rows, width = 2 * own, KIN // steps
    mix = pl.BlockSpec((own, width), lambda i, order: (0, i))
    place = pl.BlockSpec(places.shape, lambda i, order: (0, 0))
    return pl.pallas_call(
        teacher_kernel,
        grid_spec=pltpu.PrefetchScalarGridSpec(
            num_scalar_prefetch=1,
            grid=(steps,),
            in_specs=[mix] * 3 + [place] * 2,
            out_specs=[
                pl.BlockSpec((rows, EARLY * 128), lambda i, order: (0, 0)),
                pl.BlockSpec((rows, LATE * 128), lambda i, order: (0, 0)),
                mix,
            ],
            scratch_shapes=[
                pltpu.VMEM((rows, width), jnp.bfloat16),
                pltpu.VMEM((rows // PATCHES, PATCHES, PATCHES), jnp.bfloat16),
            ],
        ),
        out_shape=[
            jax.ShapeDtypeStruct((rows, EARLY * 128), jnp.bfloat16),
            jax.ShapeDtypeStruct((rows, LATE * 128), jnp.bfloat16),
            jax.ShapeDtypeStruct((own, DOUT), jnp.bfloat16),
        ],
        compiler_params=pltpu.CompilerParams(vmem_limit_bytes=VMEM_LIMIT),
        cost_estimate=pl.CostEstimate(
            flops=3 * rows * PATCHES * KIN, bytes_accessed=9 * 1024 * 1024, transcendentals=0
        ),
    )(order, mix_own, mix_other, residual, places, places_other)


def early_kernel(student_mix, teacher_mix, *refs):
    weights, (student_out, teacher_out, held) = refs[:EARLY], refs[EARLY:]
    for block in range(EARLY):
        rows = slice(block * 128, (block + 1) * 128)
        held[0, rows, :] = weights[block][0]
        held[1, rows, :] = weights[block][1]
    student_out[...] = jnp.dot(student_mix[...], held[0], preferred_element_type=jnp.float32)
    teacher_out[...] = jnp.dot(teacher_mix[...], held[1], preferred_element_type=jnp.float32)


def early_forward(pieces, student_mix, teacher_mix):
    rows, depth = student_mix.shape
    columns, width = pieces[0].shape[-1], 256
    whole = pl.BlockSpec((rows, depth), lambda j: (0, 0))
    column = pl.BlockSpec((rows, width), lambda j: (0, j))
    return pl.pallas_call(
        early_kernel,
        grid=(columns // width,),
        in_specs=[whole, whole] + [pl.BlockSpec((2, 128, width), lambda j: (0, 0, j))] * EARLY,
        out_specs=[column, column],
        out_shape=[jax.ShapeDtypeStruct((rows, columns), jnp.float32)] * 2,
        scratch_shapes=[pltpu.VMEM((2, depth, width), jnp.bfloat16)],
        compiler_params=pltpu.CompilerParams(vmem_limit_bytes=VMEM_LIMIT),
        cost_estimate=pl.CostEstimate(
            flops=4 * rows * depth * columns, bytes_accessed=17 * 1024 * 1024, transcendentals=0
        ),
    )(student_mix, teacher_mix, *pieces)


def late_kernel(
    order, student_mix, teacher_mix, student_part, teacher_part, residual_own, residual_other, picked_own, picked_other,
    scale, *refs
):
    pair, student_weight, teacher_weight, student_out, matched_out, sums_out, held = refs
    held[:, :128, :] = pair[...]
    held[0, 128:, :] = student_weight[...]
    held[1, 128:, :] = teacher_weight[...]
    factor = scale[...] * (KIN ** (-0.5))
    student_sum = student_part[...] + jnp.dot(student_mix[...], held[0], preferred_element_type=jnp.float32)
    teacher_sum = teacher_part[...] + jnp.dot(teacher_mix[...], held[1], preferred_element_type=jnp.float32)
    own = residual_own.shape[0]
    first = pl.program_id(0) == 0
    for side, (residual, picked) in enumerate(((residual_own, picked_own), (residual_other, picked_other))):
        tokens = slice(side * own, (side + 1) * own)
        student = residual[...].astype(jnp.float32) + factor * student_sum[tokens]
        matched = picked[...].astype(jnp.float32) + factor * teacher_sum[tokens]
        student_out[tokens, :] = student
        matched_out[tokens, :] = matched
        spot = lax.broadcasted_iota(jnp.int32, (own, 128), 1)
        sums = jnp.where(
            spot == 0,
            jnp.sum(student * student, axis=-1, keepdims=True),
            jnp.where(
                spot == 1,
                jnp.sum(matched * matched, axis=-1, keepdims=True),
                jnp.where(spot == 2, jnp.sum(student * matched, axis=-1, keepdims=True), 0.0),
            ),
        )
        sums_out[tokens, :] = sums + jnp.where(first, 0.0, sums_out[tokens, :])


def late_forward(
    order, pieces, student_mix, teacher_mix, student_part, teacher_part, residual, residual_other, picked, picked_other,
    scale
):
    (rows, columns), own, width = student_part.shape, residual.shape[0], 256
    steps = columns // width
    whole = pl.BlockSpec((rows, LATE * 128), lambda j, order: (0, 0))
    column = pl.BlockSpec((rows, width), lambda j, order: (0, j))
    tokens = pl.BlockSpec((own, width), lambda j, order: (0, order[HALF_AT] * steps + j))
    return pl.pallas_call(
        late_kernel,
        grid_spec=pltpu.PrefetchScalarGridSpec(
            num_scalar_prefetch=1,
            grid=(steps,),
            in_specs=[whole, whole, column, column]
            + [tokens] * 4
            + [pl.BlockSpec((1, width), lambda j, order: (0, order[HALF_AT] * steps + j))]
            + [pl.BlockSpec((2, 128, width), lambda j, order: (0, 0, j))]
            + [pl.BlockSpec((128, width), lambda j, order: (0, j))] * 2,
            out_specs=[column, column, pl.BlockSpec((rows, 128), lambda j, order: (0, 0))],
            scratch_shapes=[pltpu.VMEM((2, LATE * 128, width), jnp.bfloat16)],
        ),
        out_shape=[
            jax.ShapeDtypeStruct((rows, columns), jnp.float32),
            jax.ShapeDtypeStruct((rows, columns), jnp.float32),
            jax.ShapeDtypeStruct((rows, 128), jnp.float32),
        ],
        compiler_params=pltpu.CompilerParams(vmem_limit_bytes=VMEM_LIMIT),
        cost_estimate=pl.CostEstimate(
            flops=4 * rows * LATE * 128 * columns, bytes_accessed=13 * 1024 * 1024, transcendentals=0
        ),
    )(
        order, student_mix, teacher_mix, student_part, teacher_part, residual, residual_other, picked, picked_other,
        scale, *pieces
    )


def send_kernel(
    total_tokens, order, student, matched, sums, more_sums, scale, mix, next_out, previous_out, twin_out, held_out,
    tokens_own, tokens_other
):
    own = more_sums.shape[0] // 2
    swapped = jnp.concatenate([more_sums[own:, :], more_sums[:own, :]], axis=0)
    total = (sums[...] + swapped) * (1.0 / DOUT)
    inverse_rms = lax.rsqrt(total[:, 0:1] + EPS)
    inverse_matched = lax.rsqrt(total[:, 1:2] + EPS)
    overlap = inverse_rms * inverse_matched * total[:, 2:3]
    shared = inverse_rms * (1.0 / total_tokens)
    student_part = shared * inverse_rms * (EPS * inverse_rms * inverse_rms + overlap)
    matched_part = shared * inverse_matched
    values = student[...]
    tokens = (values * inverse_rms).astype(jnp.bfloat16)
    tokens_own[...] = tokens[:own]
    tokens_other[...] = tokens[own:]
    factor = scale[...] * (KIN ** (-0.5))
    held_out[...] = (factor * (values * student_part - matched[...] * matched_part)).astype(jnp.bfloat16)
    at = 0
    for out, count in zip((next_out, previous_out, twin_out), SENT):
        grad = jnp.dot(
            mix[at : at + count].reshape(count * 128, mix.shape[-1]),
            held_out[...],
            preferred_element_type=jnp.float32,
        )
        out[:count] = grad.astype(jnp.bfloat16).reshape((count,) + out.shape[1:])
        for spare in range(count, out.shape[0]):
            out[spare] = out[count - 1]
        at += count


def send_grads(total_tokens, part, order, student, matched, sums, more_sums, scale, turned):
    rows, columns = student.shape
    steps, count, first = columns // TILE, PARTS[part], sum(PARTS[:part])
    column = pl.BlockSpec((rows, TILE), lambda j, order: (0, first + j))
    narrow = pl.BlockSpec((rows, 128), lambda j, order: (0, 0))
    out = pl.BlockSpec((rows, TILE), lambda j, order: (0, j))
    half = pl.BlockSpec((rows // 2, TILE), lambda j, order: (0, j))
    return pl.pallas_call(
        functools.partial(send_kernel, total_tokens),
        grid_spec=pltpu.PrefetchScalarGridSpec(
            num_scalar_prefetch=1,
            grid=(count,),
            in_specs=[
                column,
                column,
                narrow,
                narrow,
                pl.BlockSpec((1, TILE), lambda j, order: (0, order[HALF_AT] * steps + first + j)),
                pl.BlockSpec((8, 128, rows), lambda j, order: (0, 0, 0)),
            ],
            out_specs=[pl.BlockSpec((size, 128, TILE), lambda j, order: (0, 0, j)) for size in PADDED[part]]
            + [out, half, half],
        ),
        out_shape=[jax.ShapeDtypeStruct((size, 128, count * TILE), jnp.bfloat16) for size in PADDED[part]]
        + [
            jax.ShapeDtypeStruct((rows, count * TILE), jnp.bfloat16),
            jax.ShapeDtypeStruct((rows // 2, count * TILE), jnp.bfloat16),
            jax.ShapeDtypeStruct((rows // 2, count * TILE), jnp.bfloat16),
        ],
        compiler_params=pltpu.CompilerParams(vmem_limit_bytes=VMEM_LIMIT),
        cost_estimate=pl.CostEstimate(
            flops=rows * KIN * count * TILE, bytes_accessed=3 * count * 1024 * 1024, transcendentals=0
        ),
    )(order, student, matched, sums, more_sums, scale, turned)


def keep_kernel(held, mix, out):
    grad = jnp.dot(
        mix[...].reshape(8 * 128, mix.shape[-1]), held[...], preferred_element_type=jnp.float32
    )
    out[...] = grad.reshape(out.shape)


def keep_grads(held, kept):
    (rows, columns), width = held.shape, 256
    return pl.pallas_call(
        keep_kernel,
        grid=(columns // width,),
        in_specs=[
            pl.BlockSpec((rows, width), lambda j: (0, j)),
            pl.BlockSpec((8, 128, rows), lambda j: (0, 0, 0)),
        ],
        out_specs=pl.BlockSpec((8, 128, width), lambda j: (0, 0, j)),
        out_shape=jax.ShapeDtypeStruct((8, 128, columns), jnp.float32),
        compiler_params=pltpu.CompilerParams(vmem_limit_bytes=VMEM_LIMIT),
        cost_estimate=pl.CostEstimate(
            flops=rows * KIN * columns, bytes_accessed=7 * 1024 * 1024, transcendentals=0
        ),
    )(held, kept)


def add_kernel(kept, *refs):
    passed, out = refs[:-1], refs[-1]
    at = 0
    for part, count in zip(passed, SENT):
        spot = slice(at, at + count)
        out[spot] = (kept[spot] + part[...].astype(jnp.float32)).astype(jnp.bfloat16)
        at += count


def add_passed(kept, passed):
    width = 256

    def blocks(count):
        return pl.BlockSpec((count, 128, width), lambda j: (0, 0, j))

    return pl.pallas_call(
        add_kernel,
        grid=(kept.shape[-1] // width,),
        in_specs=[blocks(8)] + [blocks(count) for count in SENT],
        out_specs=blocks(8),
        out_shape=jax.ShapeDtypeStruct(kept.shape, jnp.bfloat16),
        compiler_params=pltpu.CompilerParams(vmem_limit_bytes=VMEM_LIMIT),
    )(kept, *passed)


def join_kernel(order, first_own, last_own, first_other, last_other, out):
    step, width = pl.program_id(0), first_own.shape[1]
    for at, (first, last) in enumerate(((first_own, last_own), (first_other, last_other))):
        @pl.when(step == (at ^ order[HALF_AT]))
        def _():
            out[:, :width] = first[...]
            out[:, width:] = last[...]


def join_tokens(order, first_own, last_own, first_other, last_other):
    rows, half = first_own.shape[0], first_own.shape[1] + last_own.shape[1]
    first = pl.BlockSpec(first_own.shape, lambda j, order: (0, 0))
    last = pl.BlockSpec(last_own.shape, lambda j, order: (0, 0))
    return pl.pallas_call(
        join_kernel,
        grid_spec=pltpu.PrefetchScalarGridSpec(
            num_scalar_prefetch=1,
            grid=(2,),
            in_specs=[first, last, first, last],
            out_specs=pl.BlockSpec((rows, half), lambda j, order: (0, j)),
        ),
        out_shape=jax.ShapeDtypeStruct((rows, 2 * half), jnp.bfloat16),
        compiler_params=pltpu.CompilerParams(vmem_limit_bytes=SMALL_LIMIT),
        cost_estimate=pl.CostEstimate(flops=0, bytes_accessed=2400 * 1024, transcendentals=0),
    )(order, first_own, last_own, first_other, last_other)


def total_kernel(first, last, out):
    at = 0
    for chips in (first, last):
        total = chips[0].astype(jnp.float32)
        for chip in range(1, chips.shape[0]):
            total = total + chips[chip].astype(jnp.float32)
        out[:, at : at + total.shape[1]] = total.astype(jnp.bfloat16)
        at += total.shape[1]


def total_rows(first, last):
    chips, rows, _ = first.shape
    parts = [pl.BlockSpec((chips, rows // 2, part.shape[-1]), lambda i: (0, i, 0)) for part in (first, last)]
    columns = first.shape[-1] + last.shape[-1]
    return pl.pallas_call(
        total_kernel,
        grid=(2,),
        in_specs=parts,
        out_specs=pl.BlockSpec((rows // 2, columns), lambda i: (i, 0)),
        out_shape=jax.ShapeDtypeStruct((rows, columns), jnp.bfloat16),
        compiler_params=pltpu.CompilerParams(vmem_limit_bytes=SMALL_LIMIT),
        cost_estimate=pl.CostEstimate(flops=0, bytes_accessed=2400 * 1024, transcendentals=0),
    )(first, last)


def spread_kernel(copies, out):
    total = copies[0].astype(jnp.float32)
    for copy in range(1, copies.shape[0]):
        total = total + copies[copy].astype(jnp.float32)
    out[...] = jnp.broadcast_to(total.astype(jnp.bfloat16)[None], out.shape)


def spread_rows(copies, count):
    _, rows, columns = copies.shape
    return pl.pallas_call(
        spread_kernel,
        out_shape=jax.ShapeDtypeStruct((count, rows, columns), jnp.bfloat16),
        compiler_params=pltpu.CompilerParams(vmem_limit_bytes=SMALL_LIMIT),
        cost_estimate=pl.CostEstimate(flops=0, bytes_accessed=800 * 1024, transcendentals=0),
    )(copies)


def update_kernel(flip, grads, weight, teacher, first, squares, weight_out, teacher_out, first_out, squares_out):
    rows = []
    for index in range(grads.shape[0]):
        swap = ((flip[0] + index) & 1) == 1
        left = jnp.where(swap, grads[index, 1], grads[index, 0])
        right = jnp.where(swap, grads[index, 0], grads[index, 1])
        rows.append(jnp.concatenate([left, right], axis=1))
    grad = jnp.concatenate(rows, axis=0).astype(jnp.float32)
    first_next = 0.9 * first[...] + 0.1 * grad
    squares_next = 0.95 * squares[...] + 0.05 * grad * grad
    held = weight[...]
    weight_next = held - 0.1 * (first_next / (jnp.sqrt(squares_next) + 1e-08) + 0.04 * held)
    weight_out[...] = weight_next
    teacher_out[...] = 0.96 * teacher[...] + 0.04 * weight_next
    first_out[...] = first_next
    squares_out[...] = squares_next


def adamw_update(flip, grads, weight, teacher, first, squares):
    rows = pl.BlockSpec((32, DOUT), lambda i, flip: (i, 0))
    return pl.pallas_call(
        update_kernel,
        grid_spec=pltpu.PrefetchScalarGridSpec(
            num_scalar_prefetch=1,
            grid=(4,),
            in_specs=[pl.BlockSpec((2, 2, 16, DOUT // 2), lambda i, flip: (i, 0, 0, 0))] + [rows] * 4,
            out_specs=[rows] * 4,
        ),
        out_shape=[jax.ShapeDtypeStruct(weight.shape, jnp.float32)] * 4,
        compiler_params=pltpu.CompilerParams(vmem_limit_bytes=VMEM_LIMIT),
    )(flip, grads, weight, teacher, first, squares)


def shards(
    residual,
    student_mix,
    teacher_mix,
    positions,
    layer_scale,
    student_weight,
    teacher_weight,
    moment,
    second,
):
    half = DOUT // 2
    token_count = student_mix.shape[0]
    total_tokens = token_count * 256
    z, xlo, y, xhi, core = (lax.axis_index(name) for name in AXES)
    which = (core + z + xhi + xlo) & 1

    order = jnp.stack(
        [(((y + dy) & 3) * 2 + (xhi ^ dx)) * 2 + (core ^ side) for side, dy, dx in ORDER] + [which, core]
    ).astype(jnp.int32)
    scale = layer_scale.reshape(1, DOUT)
    own = jnp.stack(
        [
            lax.dynamic_slice_in_dim(weight, which * half, half, axis=-1)
            for weight in (student_weight, teacher_weight)
        ]
    ).astype(jnp.bfloat16)

    own, student_sent, teacher_sent, positions_sent, student_held, teacher_held, residual = lax.optimization_barrier(
        (own, student_mix, teacher_mix, positions, student_weight, teacher_weight, residual)
    )
    student_weight, teacher_weight = student_held, teacher_held
    student_other, positions_sent = lax.optimization_barrier((swap_cores(student_sent), positions_sent))
    teacher_other, places_other = swap_cores(teacher_sent), swap_cores(positions_sent)
    up, down, across, student_other, teacher_other, places, places_other, student_held, teacher_held = (
        lax.optimization_barrier(
            (
                from_y_next(own), from_y_previous(own), from_x_near(own), student_other, teacher_other, positions,
                places_other, student_held, teacher_held,
            )
        )
    )
    other_sent = split_weights(order, student_held, teacher_held)
    student_prepared = prepare_student(order, student_mix, student_other)
    (
        up_two, across_down, across_up, passed_up, passed_down, across, other_sent, places, places_other,
        student_prepared, teacher_other, residual,
    ) = lax.optimization_barrier(
        (
            from_y_next(up), from_y_previous(across), from_x_near(up), from_z_next(up), from_z_previous(down), across,
            other_sent, places, places_other, student_prepared,
            teacher_other, residual,
        )
    )
    prepared = prepare_teacher(order, teacher_mix, teacher_other, residual, places, places_other)
    across_two = from_y_next(across_up)
    (
        (student_two, teacher_two), passed_two, passed_across_up, passed_across_down, passed_across, prepared,
        other_sent, residual_sent,
    ) = lax.optimization_barrier(
        (
            both_halves(across_two), from_z_next(up_two), from_z_previous(across_up), from_x_near(passed_down),
            from_x_twin(across), prepared, other_sent, residual,
        )
    )
    student_early, student_late, sent_mix, kept_mix = student_prepared
    teacher_early, teacher_late, picked = prepared
    student_two, teacher_two = from_z_next(student_two), from_z_previous(teacher_two)
    residual_other, picked_other, other = swap_cores(residual_sent), swap_cores(picked), swap_cores(other_sent)
    student_part, teacher_part = early_forward(
        (
            own, up, down, across, up_two, across_down, across_up, passed_up, passed_down, across_two, passed_two,
            passed_across_up, passed_across_down, passed_across,
        ),
        student_early,
        teacher_early,
    )
    student_out, matched, sums = late_forward(
        order, (other, student_two, teacher_two), student_late, teacher_late, student_part, teacher_part, residual,
        residual_other, picked, picked_other, scale
    )
    more_sums = swap_cores(sums)

    def to_neighbours(part, after):
        part_sums, after = lax.optimization_barrier((sums, after))
        *sent, held, tokens_own, tokens_other = send_grads(
            total_tokens, part, order, student_out, matched, part_sums, more_sums, scale, sent_mix
        )
        passed = (from_z_previous(sent[0]), from_z_next(sent[1]), from_x_twin(sent[2]))
        return sent, held, tokens_own, tokens_other, passed

    def over_fsdp(rows):
        return lax.all_to_all(rows, ("xlo", "y", "xhi"), 0, 0, axis_index_groups=FSDP_GROUPS)

    sent, first_held, first_own, first_other, first_passed = to_neighbours(0, more_sums)
    _, last_held, last_own, last_other, last_passed = to_neighbours(1, sent)
    first_kept, last_kept = keep_grads(first_held, kept_mix), keep_grads(last_held, kept_mix)
    first_passed, last_kept, last_other = lax.optimization_barrier((first_passed, last_kept, last_other))
    first_rows, last_kept, last_other = lax.optimization_barrier(
        (add_passed(first_kept, first_passed), last_kept, last_other)
    )
    swapped = swap_cores(first_other), swap_cores(last_other)
    first_chip, last_rows = lax.optimization_barrier((over_fsdp(first_rows), add_passed(last_kept, last_passed)))
    last_chip = over_fsdp(last_rows)
    student_tokens = join_tokens(order, first_own, last_own, *swapped)
    first_chip, last_chip, student_tokens = lax.optimization_barrier((first_chip, last_chip, student_tokens))
    total = total_rows(first_chip, last_chip)
    by_copy = lax.all_to_all(
        total.reshape(8, 16, half), ("z", "xlo"), 0, 0, axis_index_groups=DP_GROUPS
    )
    full = lax.all_to_all(spread_rows(by_copy, 16), ("z", "xlo"), 0, 0)
    flip = ((core + xhi) & 1).astype(jnp.int32).reshape(1)
    weight_next, teacher_next, first_next, squares_next = adamw_update(
        flip, full.reshape(8, 2, 16, half), student_weight, teacher_weight, moment, second
    )
    return (weight_next, teacher_next, first_next, squares_next, student_tokens)


def solution(mesh):
    split = Mesh(mesh.devices.reshape(8, 2, 4, 2, 2), AXES)
    tokens = P(AXES, None)
    owned = P(("y", "xhi", "core"), None)
    return jax.shard_map(
        shards,
        mesh=split,
        in_specs=(tokens, tokens, tokens, tokens, P(), owned, owned, owned, owned),
        out_specs=(owned, owned, owned, owned, tokens),
        check_vma=False,
    )
```

```python
import functools

import jax
import jax.numpy as jnp
from jax import lax
from jax.experimental import pallas as pl
from jax.experimental.pallas import tpu as pltpu
from jax.sharding import Mesh, PartitionSpec as P

KIN = 2048
DOUT = 2048
PATCHES = 144
EPS = 1e-06
AXES = ("z", "xlo", "y", "xhi", "core")
VMEM_LIMIT = 32 * 1024 * 1024
SMALL_LIMIT = 16 * 1024 * 1024

X_INDEX = (0, 2, 1, 3)
CORE_SWAP = ((0, 1), (1, 0))
X_NEAR = tuple((X_INDEX[a], X_INDEX[b]) for a, b in ((1, 2), (2, 1), (0, 3), (3, 0)))


def from_next(size):
    return tuple(((i + 1) % size, i) for i in range(size))


def from_previous(size):
    return tuple((i, (i + 1) % size) for i in range(size))


def with_core_flip(pairs):
    return tuple((2 * a + 1 - core, 2 * b + core) for a, b in pairs for core in range(2))


FSDP_GROUPS = tuple(
    tuple((xhi ^ side) * 8 + y * 2 + xhi for y in range(4) for xhi in range(2)) for side in range(2)
)
DP_GROUPS = tuple(tuple(z * 2 + ((z + side) & 1) for z in range(8)) for side in range(2))


def swap_cores(value):
    return lax.ppermute(value, "core", CORE_SWAP)


def from_y_next(value):
    return lax.ppermute(value, "y", from_next(4))


def from_y_previous(value):
    return lax.ppermute(value, "y", from_previous(4))


def from_x_near(value):
    return lax.ppermute(value, ("xlo", "xhi"), X_NEAR)


def from_z_next(value):
    return lax.ppermute(value, ("z", "core"), with_core_flip(from_next(8)))


def from_z_previous(value):
    return lax.ppermute(value, ("z", "core"), with_core_flip(from_previous(8)))


def from_x_twin(value):
    return lax.ppermute(value, ("xlo", "core"), with_core_flip(CORE_SWAP))


ORDER = (
    (0, 0, 0), (0, 1, 0), (0, 3, 0), (0, 0, 1), (0, 2, 0), (0, 3, 1), (0, 1, 1), (1, 1, 0), (1, 3, 0), (0, 2, 1),
    (1, 2, 0), (1, 1, 1), (1, 3, 1), (1, 0, 1), (1, 0, 0), (1, 2, 1),
)
EARLY = 14
LATE = len(ORDER) - EARLY
HALF_AT = len(ORDER)
CORE_AT = HALF_AT + 1
SENT = (3, 3, 2)
PADDED = (SENT, (3, 3, 3))
TILE = 256
PARTS = (1, 3)


def split_kernel(order, student, teacher, out):
    out[0] = student[...].astype(jnp.bfloat16)
    out[1] = teacher[...].astype(jnp.bfloat16)


def split_weights(order, student, teacher):
    rows, width, steps = student.shape[0], 512, 2

    def half(j, order):
        return (0, (order[HALF_AT] ^ 1) * steps + j)

    return pl.pallas_call(
        split_kernel,
        grid_spec=pltpu.PrefetchScalarGridSpec(
            num_scalar_prefetch=1,
            grid=(steps,),
            in_specs=[pl.BlockSpec((rows, width), half)] * 2,
            out_specs=pl.BlockSpec((2, rows, width), lambda j, order: (0, 0, j)),
        ),
        out_shape=jax.ShapeDtypeStruct((2, rows, width * steps), jnp.bfloat16),
        compiler_params=pltpu.CompilerParams(vmem_limit_bytes=SMALL_LIMIT),
        cost_estimate=pl.CostEstimate(flops=0, bytes_accessed=1536 * 1024, transcendentals=0),
    )(order, student, teacher)


def halves_kernel(pair, first, second):
    first[...] = pair[0]
    second[...] = pair[1]


def both_halves(pair):
    _, rows, columns = pair.shape
    return pl.pallas_call(
        halves_kernel,
        out_shape=[jax.ShapeDtypeStruct((rows, columns), pair.dtype)] * 2,
        compiler_params=pltpu.CompilerParams(vmem_limit_bytes=SMALL_LIMIT),
        cost_estimate=pl.CostEstimate(flops=0, bytes_accessed=1024 * 1024, transcendentals=0),
    )(pair)


def place_blocks(order, step, packed, early, late):
    for part in range(2):
        columns = slice(part * 128, (part + 1) * 128)
        for block in range(len(ORDER)):
            @pl.when(order[block] == 2 * step + part)
            def _():
                if block < EARLY:
                    early[:, block * 128 : (block + 1) * 128] = packed[:, columns]
                else:
                    late[:, (block - EARLY) * 128 : (block - EARLY + 1) * 128] = packed[:, columns]


def student_kernel(order, mix_own, mix_other, early, late, sent_out, kept_out, turned, packed):
    own = mix_own.shape[0]
    packed[:own, :] = mix_own[...]
    packed[own:, :] = mix_other[...]
    turned[...] = packed[...].T
    core = order[CORE_AT]
    kept_out[0] = turned[pl.ds(pl.multiple_of(core * 128, 128), 128), :]
    sent_out[0] = turned[pl.ds(pl.multiple_of((1 - core) * 128, 128), 128), :]
    place_blocks(order, pl.program_id(0), packed, early, late)


def teacher_kernel(
    order, mix_own, mix_other, residual, places_own, places_other, early, late, picked_out, packed, picks
):
    own, step = mix_own.shape[0], pl.program_id(0)
    crops = own // PATCHES

    @pl.when(step == 0)
    def _():
        source = lax.broadcasted_iota(jnp.int32, (PATCHES, PATCHES), 0)
        for side, places in enumerate((places_own, places_other)):
            for crop in range(crops):
                chosen = jnp.where(places[crop : crop + 1, :] == source, 1.0, 0.0)
                picks[side * crops + crop] = chosen.T.astype(jnp.bfloat16)

    for side, mix in enumerate((mix_own, mix_other)):
        for crop in range(crops):
            rows = slice(crop * PATCHES, (crop + 1) * PATCHES)
            at = side * crops + crop
            packed[at * PATCHES : (at + 1) * PATCHES, :] = jnp.dot(
                picks[at], mix[rows, :], preferred_element_type=jnp.float32
            ).astype(jnp.bfloat16)
            if side == 0:
                picked_out[rows, :] = jnp.dot(
                    picks[at], residual[rows, :], preferred_element_type=jnp.float32
                ).astype(jnp.bfloat16)
    place_blocks(order, step, packed, early, late)


def prepare_student(order, mix_own, mix_other):
    own, steps = mix_own.shape[0], 8
    rows, width = 2 * own, KIN // steps
    mix = pl.BlockSpec((own, width), lambda i, order: (0, i))
    turned = pl.BlockSpec((1, 128, rows), lambda i, order: (i, 0, 0))
    return pl.pallas_call(
        student_kernel,
        grid_spec=pltpu.PrefetchScalarGridSpec(
            num_scalar_prefetch=1,
            grid=(steps,),
            in_specs=[mix] * 2,
            out_specs=[
                pl.BlockSpec((rows, EARLY * 128), lambda i, order: (0, 0)),
                pl.BlockSpec((rows, LATE * 128), lambda i, order: (0, 0)),
                turned,
                turned,
            ],
            scratch_shapes=[pltpu.VMEM((width, rows), jnp.bfloat16), pltpu.VMEM((rows, width), jnp.bfloat16)],
        ),
        out_shape=[
            jax.ShapeDtypeStruct((rows, EARLY * 128), jnp.bfloat16),
            jax.ShapeDtypeStruct((rows, LATE * 128), jnp.bfloat16),
            jax.ShapeDtypeStruct((8, 128, rows), jnp.bfloat16),
            jax.ShapeDtypeStruct((8, 128, rows), jnp.bfloat16),
        ],
        compiler_params=pltpu.CompilerParams(vmem_limit_bytes=VMEM_LIMIT),
        cost_estimate=pl.CostEstimate(flops=0, bytes_accessed=7 * 1024 * 1024, transcendentals=0),
    )(order, mix_own, mix_other)


def prepare_teacher(order, mix_own, mix_other, residual, places, places_other):
    own, steps = mix_own.shape[0], 8
    rows, width = 2 * own, KIN // steps
    mix = pl.BlockSpec((own, width), lambda i, order: (0, i))
    place = pl.BlockSpec(places.shape, lambda i, order: (0, 0))
    return pl.pallas_call(
        teacher_kernel,
        grid_spec=pltpu.PrefetchScalarGridSpec(
            num_scalar_prefetch=1,
            grid=(steps,),
            in_specs=[mix] * 3 + [place] * 2,
            out_specs=[
                pl.BlockSpec((rows, EARLY * 128), lambda i, order: (0, 0)),
                pl.BlockSpec((rows, LATE * 128), lambda i, order: (0, 0)),
                mix,
            ],
            scratch_shapes=[
                pltpu.VMEM((rows, width), jnp.bfloat16),
                pltpu.VMEM((rows // PATCHES, PATCHES, PATCHES), jnp.bfloat16),
            ],
        ),
        out_shape=[
            jax.ShapeDtypeStruct((rows, EARLY * 128), jnp.bfloat16),
            jax.ShapeDtypeStruct((rows, LATE * 128), jnp.bfloat16),
            jax.ShapeDtypeStruct((own, DOUT), jnp.bfloat16),
        ],
        compiler_params=pltpu.CompilerParams(vmem_limit_bytes=VMEM_LIMIT),
        cost_estimate=pl.CostEstimate(
            flops=3 * rows * PATCHES * KIN, bytes_accessed=9 * 1024 * 1024, transcendentals=0
        ),
    )(order, mix_own, mix_other, residual, places, places_other)


def early_kernel(student_mix, teacher_mix, *refs):
    weights, (student_out, teacher_out, held) = refs[:EARLY], refs[EARLY:]
    for block in range(EARLY):
        rows = slice(block * 128, (block + 1) * 128)
        held[0, rows, :] = weights[block][0]
        held[1, rows, :] = weights[block][1]
    student_out[...] = jnp.dot(student_mix[...], held[0], preferred_element_type=jnp.float32)
    teacher_out[...] = jnp.dot(teacher_mix[...], held[1], preferred_element_type=jnp.float32)


def early_forward(pieces, student_mix, teacher_mix):
    rows, depth = student_mix.shape
    columns, width = pieces[0].shape[-1], 256
    whole = pl.BlockSpec((rows, depth), lambda j: (0, 0))
    column = pl.BlockSpec((rows, width), lambda j: (0, j))
    return pl.pallas_call(
        early_kernel,
        grid=(columns // width,),
        in_specs=[whole, whole] + [pl.BlockSpec((2, 128, width), lambda j: (0, 0, j))] * EARLY,
        out_specs=[column, column],
        out_shape=[jax.ShapeDtypeStruct((rows, columns), jnp.float32)] * 2,
        scratch_shapes=[pltpu.VMEM((2, depth, width), jnp.bfloat16)],
        compiler_params=pltpu.CompilerParams(vmem_limit_bytes=VMEM_LIMIT),
        cost_estimate=pl.CostEstimate(
            flops=4 * rows * depth * columns, bytes_accessed=17 * 1024 * 1024, transcendentals=0
        ),
    )(student_mix, teacher_mix, *pieces)


def late_kernel(
    order, student_mix, teacher_mix, student_part, teacher_part, residual_own, residual_other, picked_own, picked_other,
    scale, *refs
):
    pair, student_weight, teacher_weight, student_out, matched_out, sums_out, held = refs
    held[:, :128, :] = pair[...]
    held[0, 128:, :] = student_weight[...]
    held[1, 128:, :] = teacher_weight[...]
    factor = scale[...] * (KIN ** (-0.5))
    student_sum = student_part[...] + jnp.dot(student_mix[...], held[0], preferred_element_type=jnp.float32)
    teacher_sum = teacher_part[...] + jnp.dot(teacher_mix[...], held[1], preferred_element_type=jnp.float32)
    own = residual_own.shape[0]
    first = pl.program_id(0) == 0
    for side, (residual, picked) in enumerate(((residual_own, picked_own), (residual_other, picked_other))):
        tokens = slice(side * own, (side + 1) * own)
        student = residual[...].astype(jnp.float32) + factor * student_sum[tokens]
        matched = picked[...].astype(jnp.float32) + factor * teacher_sum[tokens]
        student_out[tokens, :] = student
        matched_out[tokens, :] = matched
        spot = lax.broadcasted_iota(jnp.int32, (own, 128), 1)
        sums = jnp.where(
            spot == 0,
            jnp.sum(student * student, axis=-1, keepdims=True),
            jnp.where(
                spot == 1,
                jnp.sum(matched * matched, axis=-1, keepdims=True),
                jnp.where(spot == 2, jnp.sum(student * matched, axis=-1, keepdims=True), 0.0),
            ),
        )
        sums_out[tokens, :] = sums + jnp.where(first, 0.0, sums_out[tokens, :])


def late_forward(
    order, pieces, student_mix, teacher_mix, student_part, teacher_part, residual, residual_other, picked, picked_other,
    scale
):
    (rows, columns), own, width = student_part.shape, residual.shape[0], 256
    steps = columns // width
    whole = pl.BlockSpec((rows, LATE * 128), lambda j, order: (0, 0))
    column = pl.BlockSpec((rows, width), lambda j, order: (0, j))
    tokens = pl.BlockSpec((own, width), lambda j, order: (0, order[HALF_AT] * steps + j))
    return pl.pallas_call(
        late_kernel,
        grid_spec=pltpu.PrefetchScalarGridSpec(
            num_scalar_prefetch=1,
            grid=(steps,),
            in_specs=[whole, whole, column, column]
            + [tokens] * 4
            + [pl.BlockSpec((1, width), lambda j, order: (0, order[HALF_AT] * steps + j))]
            + [pl.BlockSpec((2, 128, width), lambda j, order: (0, 0, j))]
            + [pl.BlockSpec((128, width), lambda j, order: (0, j))] * 2,
            out_specs=[column, column, pl.BlockSpec((rows, 128), lambda j, order: (0, 0))],
            scratch_shapes=[pltpu.VMEM((2, LATE * 128, width), jnp.bfloat16)],
        ),
        out_shape=[
            jax.ShapeDtypeStruct((rows, columns), jnp.float32),
            jax.ShapeDtypeStruct((rows, columns), jnp.float32),
            jax.ShapeDtypeStruct((rows, 128), jnp.float32),
        ],
        compiler_params=pltpu.CompilerParams(vmem_limit_bytes=VMEM_LIMIT),
        cost_estimate=pl.CostEstimate(
            flops=4 * rows * LATE * 128 * columns, bytes_accessed=13 * 1024 * 1024, transcendentals=0
        ),
    )(
        order, student_mix, teacher_mix, student_part, teacher_part, residual, residual_other, picked, picked_other,
        scale, *pieces
    )


def send_kernel(
    total_tokens, order, student, matched, sums, more_sums, scale, mix, next_out, previous_out, twin_out, held_out,
    tokens_own, tokens_other
):
    own = more_sums.shape[0] // 2
    swapped = jnp.concatenate([more_sums[own:, :], more_sums[:own, :]], axis=0)
    total = (sums[...] + swapped) * (1.0 / DOUT)
    inverse_rms = lax.rsqrt(total[:, 0:1] + EPS)
    inverse_matched = lax.rsqrt(total[:, 1:2] + EPS)
    overlap = inverse_rms * inverse_matched * total[:, 2:3]
    shared = inverse_rms * (1.0 / total_tokens)
    student_part = shared * inverse_rms * (EPS * inverse_rms * inverse_rms + overlap)
    matched_part = shared * inverse_matched
    values = student[...]
    tokens = (values * inverse_rms).astype(jnp.bfloat16)
    tokens_own[...] = tokens[:own]
    tokens_other[...] = tokens[own:]
    factor = scale[...] * (KIN ** (-0.5))
    held_out[...] = (factor * (values * student_part - matched[...] * matched_part)).astype(jnp.bfloat16)
    at = 0
    for out, count in zip((next_out, previous_out, twin_out), SENT):
        grad = jnp.dot(
            mix[at : at + count].reshape(count * 128, mix.shape[-1]),
            held_out[...],
            preferred_element_type=jnp.float32,
        )
        out[:count] = grad.astype(jnp.bfloat16).reshape((count,) + out.shape[1:])
        for spare in range(count, out.shape[0]):
            out[spare] = out[count - 1]
        at += count


def send_grads(total_tokens, part, order, student, matched, sums, more_sums, scale, turned):
    rows, columns = student.shape
    steps, count, first = columns // TILE, PARTS[part], sum(PARTS[:part])
    column = pl.BlockSpec((rows, TILE), lambda j, order: (0, first + j))
    narrow = pl.BlockSpec((rows, 128), lambda j, order: (0, 0))
    out = pl.BlockSpec((rows, TILE), lambda j, order: (0, j))
    half = pl.BlockSpec((rows // 2, TILE), lambda j, order: (0, j))
    return pl.pallas_call(
        functools.partial(send_kernel, total_tokens),
        grid_spec=pltpu.PrefetchScalarGridSpec(
            num_scalar_prefetch=1,
            grid=(count,),
            in_specs=[
                column,
                column,
                narrow,
                narrow,
                pl.BlockSpec((1, TILE), lambda j, order: (0, order[HALF_AT] * steps + first + j)),
                pl.BlockSpec((8, 128, rows), lambda j, order: (0, 0, 0)),
            ],
            out_specs=[pl.BlockSpec((size, 128, TILE), lambda j, order: (0, 0, j)) for size in PADDED[part]]
            + [out, half, half],
        ),
        out_shape=[jax.ShapeDtypeStruct((size, 128, count * TILE), jnp.bfloat16) for size in PADDED[part]]
        + [
            jax.ShapeDtypeStruct((rows, count * TILE), jnp.bfloat16),
            jax.ShapeDtypeStruct((rows // 2, count * TILE), jnp.bfloat16),
            jax.ShapeDtypeStruct((rows // 2, count * TILE), jnp.bfloat16),
        ],
        compiler_params=pltpu.CompilerParams(vmem_limit_bytes=VMEM_LIMIT),
        cost_estimate=pl.CostEstimate(
            flops=rows * KIN * count * TILE, bytes_accessed=3 * count * 1024 * 1024, transcendentals=0
        ),
    )(order, student, matched, sums, more_sums, scale, turned)


def keep_kernel(held, mix, out):
    grad = jnp.dot(
        mix[...].reshape(8 * 128, mix.shape[-1]), held[...], preferred_element_type=jnp.float32
    )
    out[...] = grad.reshape(out.shape)


def keep_grads(held, kept):
    (rows, columns), width = held.shape, 256
    return pl.pallas_call(
        keep_kernel,
        grid=(columns // width,),
        in_specs=[
            pl.BlockSpec((rows, width), lambda j: (0, j)),
            pl.BlockSpec((8, 128, rows), lambda j: (0, 0, 0)),
        ],
        out_specs=pl.BlockSpec((8, 128, width), lambda j: (0, 0, j)),
        out_shape=jax.ShapeDtypeStruct((8, 128, columns), jnp.float32),
        compiler_params=pltpu.CompilerParams(vmem_limit_bytes=VMEM_LIMIT),
        cost_estimate=pl.CostEstimate(
            flops=rows * KIN * columns, bytes_accessed=7 * 1024 * 1024, transcendentals=0
        ),
    )(held, kept)


def add_kernel(kept, *refs):
    passed, out = refs[:-1], refs[-1]
    at = 0
    for part, count in zip(passed, SENT):
        spot = slice(at, at + count)
        out[spot] = (kept[spot] + part[...].astype(jnp.float32)).astype(jnp.bfloat16)
        at += count


def add_passed(kept, passed):
    width = 256

    def blocks(count):
        return pl.BlockSpec((count, 128, width), lambda j: (0, 0, j))

    return pl.pallas_call(
        add_kernel,
        grid=(kept.shape[-1] // width,),
        in_specs=[blocks(8)] + [blocks(count) for count in SENT],
        out_specs=blocks(8),
        out_shape=pltpu.HBM(kept.shape, jnp.bfloat16),
        compiler_params=pltpu.CompilerParams(vmem_limit_bytes=VMEM_LIMIT),
    )(kept, *passed)


def join_kernel(order, first_own, last_own, first_other, last_other, out):
    step, width = pl.program_id(0), first_own.shape[1]
    for at, (first, last) in enumerate(((first_own, last_own), (first_other, last_other))):
        @pl.when(step == (at ^ order[HALF_AT]))
        def _():
            out[:, :width] = first[...]
            out[:, width:] = last[...]


def join_tokens(order, first_own, last_own, first_other, last_other):
    rows, half = first_own.shape[0], first_own.shape[1] + last_own.shape[1]
    first = pl.BlockSpec(first_own.shape, lambda j, order: (0, 0))
    last = pl.BlockSpec(last_own.shape, lambda j, order: (0, 0))
    return pl.pallas_call(
        join_kernel,
        grid_spec=pltpu.PrefetchScalarGridSpec(
            num_scalar_prefetch=1,
            grid=(2,),
            in_specs=[first, last, first, last],
            out_specs=pl.BlockSpec((rows, half), lambda j, order: (0, j)),
        ),
        out_shape=jax.ShapeDtypeStruct((rows, 2 * half), jnp.bfloat16),
        compiler_params=pltpu.CompilerParams(vmem_limit_bytes=SMALL_LIMIT),
        cost_estimate=pl.CostEstimate(flops=0, bytes_accessed=2400 * 1024, transcendentals=0),
    )(order, first_own, last_own, first_other, last_other)


def total_kernel(first, last, out):
    at = 0
    for chips in (first, last):
        total = chips[0].astype(jnp.float32)
        for chip in range(1, chips.shape[0]):
            total = total + chips[chip].astype(jnp.float32)
        out[:, at : at + total.shape[1]] = total.astype(jnp.bfloat16)
        at += total.shape[1]


def total_rows(first, last):
    chips, rows, _ = first.shape
    parts = [pl.BlockSpec((chips, rows // 2, part.shape[-1]), lambda i: (0, i, 0)) for part in (first, last)]
    columns = first.shape[-1] + last.shape[-1]
    return pl.pallas_call(
        total_kernel,
        grid=(2,),
        in_specs=parts,
        out_specs=pl.BlockSpec((rows // 2, columns), lambda i: (i, 0)),
        out_shape=jax.ShapeDtypeStruct((rows, columns), jnp.bfloat16),
        compiler_params=pltpu.CompilerParams(vmem_limit_bytes=SMALL_LIMIT),
        cost_estimate=pl.CostEstimate(flops=0, bytes_accessed=2400 * 1024, transcendentals=0),
    )(first, last)


def spread_kernel(copies, out):
    total = copies[0].astype(jnp.float32)
    for copy in range(1, copies.shape[0]):
        total = total + copies[copy].astype(jnp.float32)
    out[...] = jnp.broadcast_to(total.astype(jnp.bfloat16)[None], out.shape)


def spread_rows(copies, count):
    _, rows, columns = copies.shape
    return pl.pallas_call(
        spread_kernel,
        out_shape=jax.ShapeDtypeStruct((count, rows, columns), jnp.bfloat16),
        compiler_params=pltpu.CompilerParams(vmem_limit_bytes=SMALL_LIMIT),
        cost_estimate=pl.CostEstimate(flops=0, bytes_accessed=800 * 1024, transcendentals=0),
    )(copies)


def update_kernel(flip, grads, weight, teacher, first, squares, weight_out, teacher_out, first_out, squares_out):
    rows = []
    for index in range(grads.shape[0]):
        swap = ((flip[0] + index) & 1) == 1
        left = jnp.where(swap, grads[index, 1], grads[index, 0])
        right = jnp.where(swap, grads[index, 0], grads[index, 1])
        rows.append(jnp.concatenate([left, right], axis=1))
    grad = jnp.concatenate(rows, axis=0).astype(jnp.float32)
    first_next = 0.9 * first[...] + 0.1 * grad
    squares_next = 0.95 * squares[...] + 0.05 * grad * grad
    held = weight[...]
    weight_next = held - 0.1 * (first_next / (jnp.sqrt(squares_next) + 1e-08) + 0.04 * held)
    weight_out[...] = weight_next
    teacher_out[...] = 0.96 * teacher[...] + 0.04 * weight_next
    first_out[...] = first_next
    squares_out[...] = squares_next


def adamw_update(flip, grads, weight, teacher, first, squares):
    rows = pl.BlockSpec((32, DOUT), lambda i, flip: (i, 0))
    return pl.pallas_call(
        update_kernel,
        grid_spec=pltpu.PrefetchScalarGridSpec(
            num_scalar_prefetch=1,
            grid=(4,),
            in_specs=[pl.BlockSpec((2, 2, 16, DOUT // 2), lambda i, flip: (i, 0, 0, 0))] + [rows] * 4,
            out_specs=[rows] * 4,
        ),
        out_shape=[jax.ShapeDtypeStruct(weight.shape, jnp.float32)] * 4,
        compiler_params=pltpu.CompilerParams(vmem_limit_bytes=VMEM_LIMIT),
    )(flip, grads, weight, teacher, first, squares)


def shards(
    residual,
    student_mix,
    teacher_mix,
    positions,
    layer_scale,
    student_weight,
    teacher_weight,
    moment,
    second,
):
    half = DOUT // 2
    token_count = student_mix.shape[0]
    total_tokens = token_count * 256
    z, xlo, y, xhi, core = (lax.axis_index(name) for name in AXES)
    which = (core + z + xhi + xlo) & 1

    order = jnp.stack(
        [(((y + dy) & 3) * 2 + (xhi ^ dx)) * 2 + (core ^ side) for side, dy, dx in ORDER] + [which, core]
    ).astype(jnp.int32)
    scale = layer_scale.reshape(1, DOUT)
    own = jnp.stack(
        [
            lax.dynamic_slice_in_dim(weight, which * half, half, axis=-1)
            for weight in (student_weight, teacher_weight)
        ]
    ).astype(jnp.bfloat16)

    own, student_sent, teacher_sent, positions_sent, student_held, teacher_held, residual = lax.optimization_barrier(
        (own, student_mix, teacher_mix, positions, student_weight, teacher_weight, residual)
    )
    student_weight, teacher_weight = student_held, teacher_held
    student_other, positions_sent = lax.optimization_barrier((swap_cores(student_sent), positions_sent))
    teacher_other, places_other = swap_cores(teacher_sent), swap_cores(positions_sent)
    up, down, across, student_other, teacher_other, places, places_other, student_held, teacher_held, order = (
        lax.optimization_barrier(
            (
                from_y_next(own), from_y_previous(own), from_x_near(own), student_other, teacher_other, positions,
                places_other, student_held, teacher_held, order,
            )
        )
    )
    other_sent = split_weights(order, student_held, teacher_held)
    student_prepared = prepare_student(order, student_mix, student_other)
    (
        up_two, across_down, across_up, passed_up, passed_down, across, other_sent, places, places_other,
        student_prepared, teacher_other, residual,
    ) = lax.optimization_barrier(
        (
            from_y_next(up), from_y_previous(across), from_x_near(up), from_z_next(up), from_z_previous(down), across,
            other_sent, places, places_other, student_prepared,
            teacher_other, residual,
        )
    )
    prepared = prepare_teacher(order, teacher_mix, teacher_other, residual, places, places_other)
    across_two = from_y_next(across_up)
    (
        (student_two, teacher_two), passed_two, passed_across_up, passed_across_down, passed_across, prepared,
        other_sent, residual_sent,
    ) = lax.optimization_barrier(
        (
            both_halves(across_two), from_z_next(up_two), from_z_previous(across_up), from_x_near(passed_down),
            from_x_twin(across), prepared, other_sent, residual,
        )
    )
    student_early, student_late, sent_mix, kept_mix = student_prepared
    teacher_early, teacher_late, picked = prepared
    student_two, teacher_two = from_z_next(student_two), from_z_previous(teacher_two)
    residual_other, picked_other, other = swap_cores(residual_sent), swap_cores(picked), swap_cores(other_sent)
    student_part, teacher_part = early_forward(
        (
            own, up, down, across, up_two, across_down, across_up, passed_up, passed_down, across_two, passed_two,
            passed_across_up, passed_across_down, passed_across,
        ),
        student_early,
        teacher_early,
    )
    student_out, matched, sums = late_forward(
        order, (other, student_two, teacher_two), student_late, teacher_late, student_part, teacher_part, residual,
        residual_other, picked, picked_other, scale
    )
    more_sums = swap_cores(sums)

    def to_neighbours(part, after):
        part_sums, after = lax.optimization_barrier((sums, after))
        *sent, held, tokens_own, tokens_other = send_grads(
            total_tokens, part, order, student_out, matched, part_sums, more_sums, scale, sent_mix
        )
        passed = (from_z_previous(sent[0]), from_z_next(sent[1]), from_x_twin(sent[2]))
        return sent, held, tokens_own, tokens_other, passed

    def over_fsdp(rows):
        return lax.all_to_all(rows, ("xlo", "y", "xhi"), 0, 0, axis_index_groups=FSDP_GROUPS)

    sent, first_held, first_own, first_other, first_passed = to_neighbours(0, more_sums)
    _, last_held, last_own, last_other, last_passed = to_neighbours(1, sent)
    first_kept, last_kept = keep_grads(first_held, kept_mix), keep_grads(last_held, kept_mix)
    first_passed, last_kept, last_other = lax.optimization_barrier((first_passed, last_kept, last_other))
    first_rows, last_kept, last_other = lax.optimization_barrier(
        (add_passed(first_kept, first_passed), last_kept, last_other)
    )
    swapped = swap_cores(first_other), swap_cores(last_other)
    first_chip, last_rows = lax.optimization_barrier((over_fsdp(first_rows), add_passed(last_kept, last_passed)))
    last_chip = over_fsdp(last_rows)
    student_tokens = join_tokens(order, first_own, last_own, *swapped)
    first_chip, last_chip, student_tokens = lax.optimization_barrier((first_chip, last_chip, student_tokens))
    total = total_rows(first_chip, last_chip)
    by_copy = lax.all_to_all(
        total.reshape(8, 16, half), ("z", "xlo"), 0, 0, axis_index_groups=DP_GROUPS
    )
    full = lax.all_to_all(spread_rows(by_copy, 16), ("z", "xlo"), 0, 0)
    flip = ((core + xhi) & 1).astype(jnp.int32).reshape(1)
    weight_next, teacher_next, first_next, squares_next = adamw_update(
        flip, full.reshape(8, 2, 16, half), student_weight, teacher_weight, moment, second
    )
    return (weight_next, teacher_next, first_next, squares_next, student_tokens)


def solution(mesh):
    split = Mesh(mesh.devices.reshape(8, 2, 4, 2, 2), AXES)
    tokens = P(AXES, None)
    owned = P(("y", "xhi", "core"), None)
    return jax.shard_map(
        shards,
        mesh=split,
        in_specs=(tokens, tokens, tokens, tokens, P(), owned, owned, owned, owned),
        out_specs=(owned, owned, owned, owned, tokens),
        check_vma=False,
    )
```

```python
import functools

import jax
import jax.numpy as jnp
from jax import lax
from jax.experimental import pallas as pl
from jax.experimental.pallas import tpu as pltpu
from jax.sharding import Mesh, PartitionSpec as P

KIN = 2048
DOUT = 2048
PATCHES = 144
EPS = 1e-06
AXES = ("z", "xlo", "y", "xhi", "core")
VMEM_LIMIT = 32 * 1024 * 1024
SMALL_LIMIT = 16 * 1024 * 1024

X_INDEX = (0, 2, 1, 3)
CORE_SWAP = ((0, 1), (1, 0))
X_NEAR = tuple((X_INDEX[a], X_INDEX[b]) for a, b in ((1, 2), (2, 1), (0, 3), (3, 0)))


def from_next(size):
    return tuple(((i + 1) % size, i) for i in range(size))


def from_previous(size):
    return tuple((i, (i + 1) % size) for i in range(size))


def with_core_flip(pairs):
    return tuple((2 * a + 1 - core, 2 * b + core) for a, b in pairs for core in range(2))


FSDP_GROUPS = tuple(
    tuple((xhi ^ side) * 8 + y * 2 + xhi for y in range(4) for xhi in range(2)) for side in range(2)
)
DP_GROUPS = tuple(tuple(z * 2 + ((z + side) & 1) for z in range(8)) for side in range(2))


def swap_cores(value):
    return lax.ppermute(value, "core", CORE_SWAP)


def from_y_next(value):
    return lax.ppermute(value, "y", from_next(4))


def from_y_previous(value):
    return lax.ppermute(value, "y", from_previous(4))


def from_x_near(value):
    return lax.ppermute(value, ("xlo", "xhi"), X_NEAR)


def from_z_next(value):
    return lax.ppermute(value, ("z", "core"), with_core_flip(from_next(8)))


def from_z_previous(value):
    return lax.ppermute(value, ("z", "core"), with_core_flip(from_previous(8)))


def from_x_twin(value):
    return lax.ppermute(value, ("xlo", "core"), with_core_flip(CORE_SWAP))


ORDER = (
    (0, 0, 0), (0, 1, 0), (0, 3, 0), (0, 0, 1), (0, 2, 0), (0, 3, 1), (0, 1, 1), (1, 1, 0), (1, 3, 0), (0, 2, 1),
    (1, 2, 0), (1, 1, 1), (1, 3, 1), (1, 0, 1), (1, 0, 0), (1, 2, 1),
)
EARLY = 14
LATE = len(ORDER) - EARLY
HALF_AT = len(ORDER)
CORE_AT = HALF_AT + 1
SENT = (3, 3, 2)
PADDED = (SENT, (3, 3, 3))
TILE = 256
PARTS = (1, 3)


def split_kernel(order, student, teacher, out):
    out[0] = student[...].astype(jnp.bfloat16)
    out[1] = teacher[...].astype(jnp.bfloat16)


def split_weights(order, student, teacher):
    rows, width, steps = student.shape[0], 512, 2

    def half(j, order):
        return (0, (order[HALF_AT] ^ 1) * steps + j)

    return pl.pallas_call(
        split_kernel,
        grid_spec=pltpu.PrefetchScalarGridSpec(
            num_scalar_prefetch=1,
            grid=(steps,),
            in_specs=[pl.BlockSpec((rows, width), half)] * 2,
            out_specs=pl.BlockSpec((2, rows, width), lambda j, order: (0, 0, j)),
        ),
        out_shape=jax.ShapeDtypeStruct((2, rows, width * steps), jnp.bfloat16),
        compiler_params=pltpu.CompilerParams(vmem_limit_bytes=SMALL_LIMIT),
        cost_estimate=pl.CostEstimate(flops=0, bytes_accessed=1536 * 1024, transcendentals=0),
    )(order, student, teacher)


def halves_kernel(pair, first, second):
    first[...] = pair[0]
    second[...] = pair[1]


def both_halves(pair):
    _, rows, columns = pair.shape
    return pl.pallas_call(
        halves_kernel,
        out_shape=[jax.ShapeDtypeStruct((rows, columns), pair.dtype)] * 2,
        compiler_params=pltpu.CompilerParams(vmem_limit_bytes=SMALL_LIMIT),
        cost_estimate=pl.CostEstimate(flops=0, bytes_accessed=1024 * 1024, transcendentals=0),
    )(pair)


def place_blocks(order, step, packed, early, late):
    for part in range(2):
        columns = slice(part * 128, (part + 1) * 128)
        for block in range(len(ORDER)):
            @pl.when(order[block] == 2 * step + part)
            def _():
                if block < EARLY:
                    early[:, block * 128 : (block + 1) * 128] = packed[:, columns]
                else:
                    late[:, (block - EARLY) * 128 : (block - EARLY + 1) * 128] = packed[:, columns]


def student_kernel(order, mix_own, mix_other, early, late, sent_out, kept_out, turned, packed):
    own = mix_own.shape[0]
    packed[:own, :] = mix_own[...]
    packed[own:, :] = mix_other[...]
    turned[...] = packed[...].T
    core = order[CORE_AT]
    kept_out[0] = turned[pl.ds(pl.multiple_of(core * 128, 128), 128), :]
    sent_out[0] = turned[pl.ds(pl.multiple_of((1 - core) * 128, 128), 128), :]
    place_blocks(order, pl.program_id(0), packed, early, late)


def teacher_kernel(
    order, mix_own, mix_other, residual, places_own, places_other, early, late, picked_out, packed, picks
):
    own, step = mix_own.shape[0], pl.program_id(0)
    crops = own // PATCHES

    @pl.when(step == 0)
    def _():
        source = lax.broadcasted_iota(jnp.int32, (PATCHES, PATCHES), 0)
        for side, places in enumerate((places_own, places_other)):
            for crop in range(crops):
                chosen = jnp.where(places[crop : crop + 1, :] == source, 1.0, 0.0)
                picks[side * crops + crop] = chosen.T.astype(jnp.bfloat16)

    for side, mix in enumerate((mix_own, mix_other)):
        for crop in range(crops):
            rows = slice(crop * PATCHES, (crop + 1) * PATCHES)
            at = side * crops + crop
            packed[at * PATCHES : (at + 1) * PATCHES, :] = jnp.dot(
                picks[at], mix[rows, :], preferred_element_type=jnp.float32
            ).astype(jnp.bfloat16)
            if side == 0:
                picked_out[rows, :] = jnp.dot(
                    picks[at], residual[rows, :], preferred_element_type=jnp.float32
                ).astype(jnp.bfloat16)
    place_blocks(order, step, packed, early, late)


def prepare_student(order, mix_own, mix_other):
    own, steps = mix_own.shape[0], 8
    rows, width = 2 * own, KIN // steps
    mix = pl.BlockSpec((own, width), lambda i, order: (0, i))
    turned = pl.BlockSpec((1, 128, rows), lambda i, order: (i, 0, 0))
    return pl.pallas_call(
        student_kernel,
        grid_spec=pltpu.PrefetchScalarGridSpec(
            num_scalar_prefetch=1,
            grid=(steps,),
            in_specs=[mix] * 2,
            out_specs=[
                pl.BlockSpec((rows, EARLY * 128), lambda i, order: (0, 0)),
                pl.BlockSpec((rows, LATE * 128), lambda i, order: (0, 0)),
                turned,
                turned,
            ],
            scratch_shapes=[pltpu.VMEM((width, rows), jnp.bfloat16), pltpu.VMEM((rows, width), jnp.bfloat16)],
        ),
        out_shape=[
            jax.ShapeDtypeStruct((rows, EARLY * 128), jnp.bfloat16),
            jax.ShapeDtypeStruct((rows, LATE * 128), jnp.bfloat16),
            jax.ShapeDtypeStruct((8, 128, rows), jnp.bfloat16),
            jax.ShapeDtypeStruct((8, 128, rows), jnp.bfloat16),
        ],
        compiler_params=pltpu.CompilerParams(vmem_limit_bytes=VMEM_LIMIT),
        cost_estimate=pl.CostEstimate(flops=0, bytes_accessed=7 * 1024 * 1024, transcendentals=0),
    )(order, mix_own, mix_other)


def prepare_teacher(order, mix_own, mix_other, residual, places, places_other):
    own, steps = mix_own.shape[0], 8
    rows, width = 2 * own, KIN // steps
    mix = pl.BlockSpec((own, width), lambda i, order: (0, i))
    place = pl.BlockSpec(places.shape, lambda i, order: (0, 0))
    return pl.pallas_call(
        teacher_kernel,
        grid_spec=pltpu.PrefetchScalarGridSpec(
            num_scalar_prefetch=1,
            grid=(steps,),
            in_specs=[mix] * 3 + [place] * 2,
            out_specs=[
                pl.BlockSpec((rows, EARLY * 128), lambda i, order: (0, 0)),
                pl.BlockSpec((rows, LATE * 128), lambda i, order: (0, 0)),
                mix,
            ],
            scratch_shapes=[
                pltpu.VMEM((rows, width), jnp.bfloat16),
                pltpu.VMEM((rows // PATCHES, PATCHES, PATCHES), jnp.bfloat16),
            ],
        ),
        out_shape=[
            jax.ShapeDtypeStruct((rows, EARLY * 128), jnp.bfloat16),
            jax.ShapeDtypeStruct((rows, LATE * 128), jnp.bfloat16),
            jax.ShapeDtypeStruct((own, DOUT), jnp.bfloat16),
        ],
        compiler_params=pltpu.CompilerParams(vmem_limit_bytes=VMEM_LIMIT),
        cost_estimate=pl.CostEstimate(
            flops=3 * rows * PATCHES * KIN, bytes_accessed=9 * 1024 * 1024, transcendentals=0
        ),
    )(order, mix_own, mix_other, residual, places, places_other)


def early_kernel(student_mix, teacher_mix, *refs):
    weights, (student_out, teacher_out, held) = refs[:EARLY], refs[EARLY:]
    for block in range(EARLY):
        rows = slice(block * 128, (block + 1) * 128)
        held[0, rows, :] = weights[block][0]
        held[1, rows, :] = weights[block][1]
    student_out[...] = jnp.dot(student_mix[...], held[0], preferred_element_type=jnp.float32)
    teacher_out[...] = jnp.dot(teacher_mix[...], held[1], preferred_element_type=jnp.float32)


def early_forward(pieces, student_mix, teacher_mix):
    rows, depth = student_mix.shape
    columns, width = pieces[0].shape[-1], 256
    whole = pl.BlockSpec((rows, depth), lambda j: (0, 0))
    column = pl.BlockSpec((rows, width), lambda j: (0, j))
    return pl.pallas_call(
        early_kernel,
        grid=(columns // width,),
        in_specs=[whole, whole] + [pl.BlockSpec((2, 128, width), lambda j: (0, 0, j))] * EARLY,
        out_specs=[column, column],
        out_shape=[jax.ShapeDtypeStruct((rows, columns), jnp.float32)] * 2,
        scratch_shapes=[pltpu.VMEM((2, depth, width), jnp.bfloat16)],
        compiler_params=pltpu.CompilerParams(vmem_limit_bytes=VMEM_LIMIT),
        cost_estimate=pl.CostEstimate(
            flops=4 * rows * depth * columns, bytes_accessed=17 * 1024 * 1024, transcendentals=0
        ),
    )(student_mix, teacher_mix, *pieces)


def late_kernel(
    order, student_mix, teacher_mix, student_part, teacher_part, residual_own, residual_other, picked_own, picked_other,
    scale, *refs
):
    pair, student_weight, teacher_weight, student_out, matched_out, sums_out, held = refs
    held[:, :128, :] = pair[...]
    held[0, 128:, :] = student_weight[...]
    held[1, 128:, :] = teacher_weight[...]
    factor = scale[...] * (KIN ** (-0.5))
    student_sum = student_part[...] + jnp.dot(student_mix[...], held[0], preferred_element_type=jnp.float32)
    teacher_sum = teacher_part[...] + jnp.dot(teacher_mix[...], held[1], preferred_element_type=jnp.float32)
    own = residual_own.shape[0]
    first = pl.program_id(0) == 0
    for side, (residual, picked) in enumerate(((residual_own, picked_own), (residual_other, picked_other))):
        tokens = slice(side * own, (side + 1) * own)
        student = residual[...].astype(jnp.float32) + factor * student_sum[tokens]
        matched = picked[...].astype(jnp.float32) + factor * teacher_sum[tokens]
        student_out[tokens, :] = student
        matched_out[tokens, :] = matched
        spot = lax.broadcasted_iota(jnp.int32, (own, 128), 1)
        sums = jnp.where(
            spot == 0,
            jnp.sum(student * student, axis=-1, keepdims=True),
            jnp.where(
                spot == 1,
                jnp.sum(matched * matched, axis=-1, keepdims=True),
                jnp.where(spot == 2, jnp.sum(student * matched, axis=-1, keepdims=True), 0.0),
            ),
        )
        sums_out[tokens, :] = sums + jnp.where(first, 0.0, sums_out[tokens, :])


def late_forward(
    order, pieces, student_mix, teacher_mix, student_part, teacher_part, residual, residual_other, picked, picked_other,
    scale
):
    (rows, columns), own, width = student_part.shape, residual.shape[0], 256
    steps = columns // width
    whole = pl.BlockSpec((rows, LATE * 128), lambda j, order: (0, 0))
    column = pl.BlockSpec((rows, width), lambda j, order: (0, j))
    tokens = pl.BlockSpec((own, width), lambda j, order: (0, order[HALF_AT] * steps + j))
    return pl.pallas_call(
        late_kernel,
        grid_spec=pltpu.PrefetchScalarGridSpec(
            num_scalar_prefetch=1,
            grid=(steps,),
            in_specs=[whole, whole, column, column]
            + [tokens] * 4
            + [pl.BlockSpec((1, width), lambda j, order: (0, order[HALF_AT] * steps + j))]
            + [pl.BlockSpec((2, 128, width), lambda j, order: (0, 0, j))]
            + [pl.BlockSpec((128, width), lambda j, order: (0, j))] * 2,
            out_specs=[column, column, pl.BlockSpec((rows, 128), lambda j, order: (0, 0))],
            scratch_shapes=[pltpu.VMEM((2, LATE * 128, width), jnp.bfloat16)],
        ),
        out_shape=[
            jax.ShapeDtypeStruct((rows, columns), jnp.float32),
            jax.ShapeDtypeStruct((rows, columns), jnp.float32),
            jax.ShapeDtypeStruct((rows, 128), jnp.float32),
        ],
        compiler_params=pltpu.CompilerParams(vmem_limit_bytes=VMEM_LIMIT),
        cost_estimate=pl.CostEstimate(
            flops=4 * rows * LATE * 128 * columns, bytes_accessed=13 * 1024 * 1024, transcendentals=0
        ),
    )(
        order, student_mix, teacher_mix, student_part, teacher_part, residual, residual_other, picked, picked_other,
        scale, *pieces
    )


def send_kernel(
    total_tokens, order, student, matched, sums, more_sums, scale, mix, next_out, previous_out, twin_out, held_out,
    tokens_own, tokens_other
):
    own = more_sums.shape[0] // 2
    swapped = jnp.concatenate([more_sums[own:, :], more_sums[:own, :]], axis=0)
    total = (sums[...] + swapped) * (1.0 / DOUT)
    inverse_rms = lax.rsqrt(total[:, 0:1] + EPS)
    inverse_matched = lax.rsqrt(total[:, 1:2] + EPS)
    overlap = inverse_rms * inverse_matched * total[:, 2:3]
    shared = inverse_rms * (1.0 / total_tokens)
    student_part = shared * inverse_rms * (EPS * inverse_rms * inverse_rms + overlap)
    matched_part = shared * inverse_matched
    values = student[...]
    tokens = (values * inverse_rms).astype(jnp.bfloat16)
    tokens_own[...] = tokens[:own]
    tokens_other[...] = tokens[own:]
    factor = scale[...] * (KIN ** (-0.5))
    held_out[...] = (factor * (values * student_part - matched[...] * matched_part)).astype(jnp.bfloat16)
    at = 0
    for out, count in zip((next_out, previous_out, twin_out), SENT):
        grad = jnp.dot(
            mix[at : at + count].reshape(count * 128, mix.shape[-1]),
            held_out[...],
            preferred_element_type=jnp.float32,
        )
        out[:count] = grad.astype(jnp.bfloat16).reshape((count,) + out.shape[1:])
        for spare in range(count, out.shape[0]):
            out[spare] = out[count - 1]
        at += count


def send_grads(total_tokens, part, order, student, matched, sums, more_sums, scale, turned):
    rows, columns = student.shape
    steps, count, first = columns // TILE, PARTS[part], sum(PARTS[:part])
    column = pl.BlockSpec((rows, TILE), lambda j, order: (0, first + j))
    narrow = pl.BlockSpec((rows, 128), lambda j, order: (0, 0))
    out = pl.BlockSpec((rows, TILE), lambda j, order: (0, j))
    half = pl.BlockSpec((rows // 2, TILE), lambda j, order: (0, j))
    return pl.pallas_call(
        functools.partial(send_kernel, total_tokens),
        grid_spec=pltpu.PrefetchScalarGridSpec(
            num_scalar_prefetch=1,
            grid=(count,),
            in_specs=[
                column,
                column,
                narrow,
                narrow,
                pl.BlockSpec((1, TILE), lambda j, order: (0, order[HALF_AT] * steps + first + j)),
                pl.BlockSpec((8, 128, rows), lambda j, order: (0, 0, 0)),
            ],
            out_specs=[pl.BlockSpec((size, 128, TILE), lambda j, order: (0, 0, j)) for size in PADDED[part]]
            + [out, half, half],
        ),
        out_shape=[jax.ShapeDtypeStruct((size, 128, count * TILE), jnp.bfloat16) for size in PADDED[part]]
        + [
            jax.ShapeDtypeStruct((rows, count * TILE), jnp.bfloat16),
            jax.ShapeDtypeStruct((rows // 2, count * TILE), jnp.bfloat16),
            jax.ShapeDtypeStruct((rows // 2, count * TILE), jnp.bfloat16),
        ],
        compiler_params=pltpu.CompilerParams(vmem_limit_bytes=VMEM_LIMIT),
        cost_estimate=pl.CostEstimate(
            flops=rows * KIN * count * TILE, bytes_accessed=3 * count * 1024 * 1024, transcendentals=0
        ),
    )(order, student, matched, sums, more_sums, scale, turned)


def keep_kernel(held, mix, out):
    grad = jnp.dot(
        mix[...].reshape(8 * 128, mix.shape[-1]), held[...], preferred_element_type=jnp.float32
    )
    out[...] = grad.reshape(out.shape)


def keep_grads(held, kept):
    (rows, columns), width = held.shape, 256
    return pl.pallas_call(
        keep_kernel,
        grid=(columns // width,),
        in_specs=[
            pl.BlockSpec((rows, width), lambda j: (0, j)),
            pl.BlockSpec((8, 128, rows), lambda j: (0, 0, 0)),
        ],
        out_specs=pl.BlockSpec((8, 128, width), lambda j: (0, 0, j)),
        out_shape=jax.ShapeDtypeStruct((8, 128, columns), jnp.float32),
        compiler_params=pltpu.CompilerParams(vmem_limit_bytes=VMEM_LIMIT),
        cost_estimate=pl.CostEstimate(
            flops=rows * KIN * columns, bytes_accessed=7 * 1024 * 1024, transcendentals=0
        ),
    )(held, kept)


def add_kernel(kept, *refs):
    passed, out = refs[:-1], refs[-1]
    at = 0
    for part, count in zip(passed, SENT):
        spot = slice(at, at + count)
        out[spot] = (kept[spot] + part[...].astype(jnp.float32)).astype(jnp.bfloat16)
        at += count


def add_passed(kept, passed):
    width = 256

    def blocks(count):
        return pl.BlockSpec((count, 128, width), lambda j: (0, 0, j))

    return pl.pallas_call(
        add_kernel,
        grid=(kept.shape[-1] // width,),
        in_specs=[blocks(8)] + [blocks(count) for count in SENT],
        out_specs=blocks(8),
        out_shape=pltpu.HBM(kept.shape, jnp.bfloat16),
        compiler_params=pltpu.CompilerParams(vmem_limit_bytes=VMEM_LIMIT),
    )(kept, *passed)


def join_kernel(order, first_own, last_own, first_other, last_other, out):
    step, width = pl.program_id(0), first_own.shape[1]
    for at, (first, last) in enumerate(((first_own, last_own), (first_other, last_other))):
        @pl.when(step == (at ^ order[HALF_AT]))
        def _():
            out[:, :width] = first[...]
            out[:, width:] = last[...]


def join_tokens(order, first_own, last_own, first_other, last_other):
    rows, half = first_own.shape[0], first_own.shape[1] + last_own.shape[1]
    first = pl.BlockSpec(first_own.shape, lambda j, order: (0, 0))
    last = pl.BlockSpec(last_own.shape, lambda j, order: (0, 0))
    return pl.pallas_call(
        join_kernel,
        grid_spec=pltpu.PrefetchScalarGridSpec(
            num_scalar_prefetch=1,
            grid=(2,),
            in_specs=[first, last, first, last],
            out_specs=pl.BlockSpec((rows, half), lambda j, order: (0, j)),
        ),
        out_shape=jax.ShapeDtypeStruct((rows, 2 * half), jnp.bfloat16),
        compiler_params=pltpu.CompilerParams(vmem_limit_bytes=SMALL_LIMIT),
        cost_estimate=pl.CostEstimate(flops=0, bytes_accessed=2400 * 1024, transcendentals=0),
    )(order, first_own, last_own, first_other, last_other)


def total_kernel(first, last, out):
    at = 0
    for chips in (first, last):
        total = chips[0].astype(jnp.float32)
        for chip in range(1, chips.shape[0]):
            total = total + chips[chip].astype(jnp.float32)
        out[:, at : at + total.shape[1]] = total.astype(jnp.bfloat16)
        at += total.shape[1]


def total_rows(first, last):
    chips, rows, _ = first.shape
    parts = [pl.BlockSpec((chips, rows // 2, part.shape[-1]), lambda i: (0, i, 0)) for part in (first, last)]
    columns = first.shape[-1] + last.shape[-1]
    return pl.pallas_call(
        total_kernel,
        grid=(2,),
        in_specs=parts,
        out_specs=pl.BlockSpec((rows // 2, columns), lambda i: (i, 0)),
        out_shape=jax.ShapeDtypeStruct((rows, columns), jnp.bfloat16),
        compiler_params=pltpu.CompilerParams(vmem_limit_bytes=SMALL_LIMIT),
        cost_estimate=pl.CostEstimate(flops=0, bytes_accessed=2400 * 1024, transcendentals=0),
    )(first, last)


def spread_kernel(copies, out):
    total = copies[0].astype(jnp.float32)
    for copy in range(1, copies.shape[0]):
        total = total + copies[copy].astype(jnp.float32)
    out[...] = jnp.broadcast_to(total.astype(jnp.bfloat16)[None], out.shape)


def spread_rows(copies, count):
    _, rows, columns = copies.shape
    return pl.pallas_call(
        spread_kernel,
        out_shape=jax.ShapeDtypeStruct((count, rows, columns), jnp.bfloat16),
        compiler_params=pltpu.CompilerParams(vmem_limit_bytes=SMALL_LIMIT),
        cost_estimate=pl.CostEstimate(flops=0, bytes_accessed=800 * 1024, transcendentals=0),
    )(copies)


def update_kernel(flip, grads, weight, teacher, first, squares, weight_out, teacher_out, first_out, squares_out):
    rows = []
    for index in range(grads.shape[0]):
        swap = ((flip[0] + index) & 1) == 1
        left = jnp.where(swap, grads[index, 1], grads[index, 0])
        right = jnp.where(swap, grads[index, 0], grads[index, 1])
        rows.append(jnp.concatenate([left, right], axis=1))
    grad = jnp.concatenate(rows, axis=0).astype(jnp.float32)
    first_next = 0.9 * first[...] + 0.1 * grad
    squares_next = 0.95 * squares[...] + 0.05 * grad * grad
    held = weight[...]
    weight_next = held - 0.1 * (first_next / (jnp.sqrt(squares_next) + 1e-08) + 0.04 * held)
    weight_out[...] = weight_next
    teacher_out[...] = 0.96 * teacher[...] + 0.04 * weight_next
    first_out[...] = first_next
    squares_out[...] = squares_next


def adamw_update(flip, grads, weight, teacher, first, squares):
    rows = pl.BlockSpec((32, DOUT), lambda i, flip: (i, 0))
    return pl.pallas_call(
        update_kernel,
        grid_spec=pltpu.PrefetchScalarGridSpec(
            num_scalar_prefetch=1,
            grid=(4,),
            in_specs=[pl.BlockSpec((2, 2, 16, DOUT // 2), lambda i, flip: (i, 0, 0, 0))] + [rows] * 4,
            out_specs=[rows] * 4,
        ),
        out_shape=[jax.ShapeDtypeStruct(weight.shape, jnp.float32)] * 4,
        compiler_params=pltpu.CompilerParams(vmem_limit_bytes=VMEM_LIMIT),
    )(flip, grads, weight, teacher, first, squares)


def shards(
    residual,
    student_mix,
    teacher_mix,
    positions,
    layer_scale,
    student_weight,
    teacher_weight,
    moment,
    second,
):
    half = DOUT // 2
    token_count = student_mix.shape[0]
    total_tokens = token_count * 256
    z, xlo, y, xhi, core = (lax.axis_index(name) for name in AXES)
    which = (core + z + xhi + xlo) & 1

    order = jnp.stack(
        [(((y + dy) & 3) * 2 + (xhi ^ dx)) * 2 + (core ^ side) for side, dy, dx in ORDER] + [which, core]
    ).astype(jnp.int32)
    scale = layer_scale.reshape(1, DOUT)
    own = jnp.stack(
        [
            lax.dynamic_slice_in_dim(weight, which * half, half, axis=-1)
            for weight in (student_weight, teacher_weight)
        ]
    ).astype(jnp.bfloat16)

    own, student_sent, teacher_sent, positions_sent, student_held, teacher_held, residual = lax.optimization_barrier(
        (own, student_mix, teacher_mix, positions, student_weight, teacher_weight, residual)
    )
    student_weight, teacher_weight = student_held, teacher_held
    student_other, positions_sent = lax.optimization_barrier((swap_cores(student_sent), positions_sent))
    teacher_other, places_other = swap_cores(teacher_sent), swap_cores(positions_sent)
    up, down, across, student_other, teacher_other, places, places_other, student_held, teacher_held, order = (
        lax.optimization_barrier(
            (
                from_y_next(own), from_y_previous(own), from_x_near(own), student_other, teacher_other, positions,
                places_other, student_held, teacher_held, order,
            )
        )
    )
    other_sent = split_weights(order, student_held, teacher_held)
    student_prepared = prepare_student(order, student_mix, student_other)
    (
        up_two, across_down, across_up, passed_up, passed_down, across, other_sent, places, places_other,
        student_prepared, teacher_other, residual,
    ) = lax.optimization_barrier(
        (
            from_y_next(up), from_y_previous(across), from_x_near(up), from_z_next(up), from_z_previous(down), across,
            other_sent, places, places_other, student_prepared,
            teacher_other, residual,
        )
    )
    prepared = prepare_teacher(order, teacher_mix, teacher_other, residual, places, places_other)
    across_two = from_y_next(across_up)
    (
        (student_two, teacher_two), passed_two, passed_across_up, passed_across_down, passed_across, prepared,
        other_sent, residual_sent,
    ) = lax.optimization_barrier(
        (
            both_halves(across_two), from_z_next(up_two), from_z_previous(across_up), from_x_near(passed_down),
            from_x_twin(across), prepared, other_sent, residual,
        )
    )
    student_early, student_late, sent_mix, kept_mix = student_prepared
    teacher_early, teacher_late, picked = prepared
    student_two, teacher_two = from_z_next(student_two), from_z_previous(teacher_two)
    residual_other, picked_other, other = swap_cores(residual_sent), swap_cores(picked), swap_cores(other_sent)
    student_part, teacher_part = early_forward(
        (
            own, up, down, across, up_two, across_down, across_up, passed_up, passed_down, across_two, passed_two,
            passed_across_up, passed_across_down, passed_across,
        ),
        student_early,
        teacher_early,
    )
    student_out, matched, sums = late_forward(
        order, (other, student_two, teacher_two), student_late, teacher_late, student_part, teacher_part, residual,
        residual_other, picked, picked_other, scale
    )
    more_sums = swap_cores(sums)

    def to_neighbours(part, after):
        part_sums, after = lax.optimization_barrier((sums, after))
        *sent, held, tokens_own, tokens_other = send_grads(
            total_tokens, part, order, student_out, matched, part_sums, more_sums, scale, sent_mix
        )
        passed = (from_z_previous(sent[0]), from_z_next(sent[1]), from_x_twin(sent[2]))
        return sent, held, tokens_own, tokens_other, passed

    def over_fsdp(rows):
        return lax.all_to_all(rows, ("xlo", "y", "xhi"), 0, 0, axis_index_groups=FSDP_GROUPS)

    sent, first_held, first_own, first_other, first_passed = to_neighbours(0, more_sums)
    _, last_held, last_own, last_other, last_passed = to_neighbours(1, sent)
    first_kept, last_kept = keep_grads(first_held, kept_mix), keep_grads(last_held, kept_mix)
    first_passed, last_kept, last_other = lax.optimization_barrier((first_passed, last_kept, last_other))
    first_rows, last_kept, last_other = lax.optimization_barrier(
        (add_passed(first_kept, first_passed), last_kept, last_other)
    )
    swapped = swap_cores(first_other), swap_cores(last_other)
    first_chip, last_rows = lax.optimization_barrier((over_fsdp(first_rows), add_passed(last_kept, last_passed)))
    last_chip = over_fsdp(last_rows)
    student_tokens = join_tokens(order, first_own, last_own, *swapped)
    first_chip, last_chip, student_tokens = lax.optimization_barrier((first_chip, last_chip, student_tokens))
    total = total_rows(first_chip, last_chip)
    by_copy = lax.all_to_all(
        total.reshape(8, 16, half), ("z", "xlo"), 0, 0, axis_index_groups=DP_GROUPS
    )
    full = lax.all_to_all(spread_rows(by_copy, 16), ("z", "xlo"), 0, 0)
    flip = ((core + xhi) & 1).astype(jnp.int32).reshape(1)
    weight_next, teacher_next, first_next, squares_next = adamw_update(
        flip, full.reshape(8, 2, 16, half), student_weight, teacher_weight,
        pltpu.with_memory_space_constraint(moment, pltpu.HBM), pltpu.with_memory_space_constraint(second, pltpu.HBM),
    )
    return (weight_next, teacher_next, first_next, squares_next, student_tokens)


def solution(mesh):
    split = Mesh(mesh.devices.reshape(8, 2, 4, 2, 2), AXES)
    tokens = P(AXES, None)
    owned = P(("y", "xhi", "core"), None)
    return jax.shard_map(
        shards,
        mesh=split,
        in_specs=(tokens, tokens, tokens, tokens, P(), owned, owned, owned, owned),
        out_specs=(owned, owned, owned, owned, tokens),
        check_vma=False,
    )
```
